32 devices in a mesh: prow: 4 (over z), pcol: 8 (over y, x, core).
Axes of the slice: x: 2, y: 2, z: 4, core: 2. Of those that a mesh axis runs over, the one named last changes fastest.
Arguments:
- inverse_tiles: float32 [8192, 8192], P('pcol', 'prow'), may hold values from -6 to 6
- factor: float32 [2, 8192, 512], P(None, ('pcol', 'prow')), may hold values from -0.09375 to 0.09375
- link_factor: float32 [1, 512, 512], replicated, may hold values from -0.25 to 0.25
- diag_inverse: float32 [2, 512, 512], replicated, may hold values from -3 to 3
- ancestors: int32 [2, 8], replicated, may hold values from 0 to 15, as said below
Outputs:
- offdiag: float32 [2, 8192, 512], P(None, ('pcol', 'prow'))
- diag: float32 [2, 512, 512], P(None, 'pcol')
- link_blocks: float32 [1, 512, 512], P(None, 'pcol')
The draws below stay inside these ranges and needn't reach their ends.
Inputs may be any that keep to these rules, and one draw needn't show every extreme that they name: `ancestors`: row k lists 8 distinct stored block rows; every row lists block 15, and row 0 lists block 0.
All inputs are finite; a program needn't handle non-finite values.
Results may differ from the reference program's by a relative error of at most 0.0001.
Values sent between devices are 32-bit elements; how exact they have to be, the bound alone decides.
No kernel may reach another device: no remote copies, remote signals or barrier semaphores. Data moves between devices by JAX's collectives and lax.ppermute only.
A program may use at most 64 MiB of HBM per device.

```python
import jax
import jax.numpy as jnp
from jax import lax

B = 512
NB = 16
NSUP = 2
MB = 8
ROWS = 8192


def draw_ancestors(key, part):
    listed = []
    for number in range(NSUP):
        scores = jax.random.permutation(jax.random.fold_in(key, 17 + number), NB - 1).astype(jnp.int32)
        if number == 0:
            scores = scores.at[0].set(-1)
        chosen = jnp.argsort(scores, stable=True)[:MB - 1].astype(jnp.int32)
        listed.append(jnp.concatenate([jnp.full((1,), NB - 1, jnp.int32), chosen]))
    return jnp.stack(listed)


def spiked(drawn, key, source, target, shards_of, factor):
    def block_of(dim):
        return (jnp.arange(drawn.shape[dim]) // (drawn.shape[dim] // shards_of)).reshape((-1,) + (1,) * (drawn.ndim - 1 - dim))

    near = jax.random.permutation(key, shards_of)[block_of(target)]
    other_side = (block_of(target) + shards_of // 2) % shards_of
    return jnp.where((block_of(source) == near) | (block_of(source) == other_side), factor * drawn, drawn)


def steps_of(rng, shape, cuts, least, top_value):
    loudness = 1.0
    for dim, parts in cuts:
        steps = jax.random.uniform(jax.random.fold_in(jax.random.fold_in(rng, 6), dim), (parts,), jnp.float32, least / len(cuts), top_value / len(cuts))
        loudness = loudness * jnp.repeat(jnp.exp(steps), shape[dim] // parts).reshape((-1,) + (1,) * (len(shape) - 1 - dim))
    return loudness


def noise(stream_key, shape, width, bound, pieces=(), kind=jnp.bfloat16):
    values = width * jax.random.normal(stream_key, shape, jnp.float32)
    if pieces:
        values = values * steps_of(stream_key, shape, pieces, -0.22, 0.18)
    return jnp.clip(values, -bound, bound).astype(kind)


def gaussian_with(stream_key, dims, spread, reach, cuts, heavy, kind=jnp.bfloat16):
    entries = spread * jax.random.normal(stream_key, dims, jnp.float32)
    if cuts:
        entries = entries * steps_of(stream_key, dims, cuts, -0.22, 0.18)
    return jnp.clip(spiked(entries, jax.random.fold_in(stream_key, 3), *heavy), -reach, reach).astype(kind)


def setup_inputs(seed: int = 0) -> dict:
    splits = jax.random.split(jax.random.key(seed), 6)
    inverse_tiles = gaussian_with(splits[0], (ROWS, ROWS), 1.0, 6.0, ((0, 8), (1, 4)), (1, 0, 8, 2.0), jnp.float32)
    factor = noise(splits[1], (NSUP, ROWS, B), (MB * B) ** -0.5, 0.09375, ((1, 32),), jnp.float32)
    link_factor = noise(splits[2], (NSUP - 1, B, B), B ** -0.5, 0.25, (), jnp.float32)
    diag_inverse = noise(splits[3], (NSUP, B, B), 0.5, 3.0, (), jnp.float32)
    ancestors = draw_ancestors(jax.random.fold_in(splits[5], 71), 0)
    return dict(inverse_tiles=inverse_tiles, factor=factor, link_factor=link_factor, diag_inverse=diag_inverse, ancestors=ancestors)


def select_rows(listed):
    block_ids = jnp.arange(NB * B, dtype=jnp.int32) // B
    return jnp.any(block_ids[:, None] == listed[None, :].astype(jnp.int32), axis=1).astype(jnp.float32)[:, None]


def product(left_part, right_part):
    return jnp.dot(left_part, right_part, precision=lax.Precision.HIGHEST, preferred_element_type=jnp.float32)


def reference(inverse_tiles, factor, link_factor, diag_inverse, ancestors):
    offdiag_list = []
    diag_list = []
    link_list = []
    prior_offdiag = None
    prior_diag = None
    for number in range(NSUP):
        keep_rows = select_rows(ancestors[number])
        masked = factor[number] * keep_rows
        applied = product(inverse_tiles, masked)
        gram_sum = product(masked.T, applied)
        if number == 0:
            result = -(keep_rows * applied)
            diag_block = diag_inverse[0] + gram_sum
        else:
            link_block = link_factor[number - 1]
            cross_sum = product(prior_offdiag.T, masked)
            result = -(keep_rows * (applied + product(prior_offdiag, link_block)))
            link_out = -(cross_sum + product(prior_diag, link_block))
            diag_block = diag_inverse[number] + gram_sum + product(cross_sum.T, link_block) - product(link_block.T, link_out)
            link_list.append(link_out)
        offdiag_list.append(result)
        diag_list.append(diag_block)
        prior_offdiag = result
        prior_diag = diag_block
    return (jnp.stack(offdiag_list), jnp.stack(diag_list), jnp.stack(link_list))
```

```python
import functools

import jax
import jax.numpy as jnp
import numpy as np
from jax import lax
from jax.experimental import pallas as pl
from jax.experimental.pallas import tpu as pltpu
from jax.sharding import PartitionSpec as P

BOTH = ("prow", "pcol")
VMEM_LIMIT = 48 * 1024 * 1024
LANES = 128


def product(left_part, right_part):
    return jnp.dot(
        left_part, right_part, precision=lax.Precision.HIGH, preferred_element_type=jnp.float32
    )


def halves(value):
    high = value.astype(jnp.bfloat16)
    low = (value - high.astype(jnp.float32)).astype(jnp.bfloat16)
    return high, low


def flip(value, axis, bit):
    return lax.ppermute(value, axis, [(i, i ^ bit) for i in range(lax.axis_size(axis))])


def spread_kernel(meta, factor_ref, *out_refs):
    nsuper = factor_ref.shape[0]
    count = len(out_refs) // nsuper
    width = out_refs[0].shape[1]
    for number in range(nsuper):
        for r in range(count):
            start = pl.multiple_of((meta[1] ^ r) * width, width)
            out_refs[number * count + r][...] = factor_ref[number, :, pl.ds(start, width)]


def spread(meta, factor, count):
    nsuper, unit_rows, columns = factor.shape
    width = columns // count
    if width % LANES:
        pieces = []
        for number in range(nsuper):
            for r in range(count):
                start = (meta[1] ^ r) * width
                pieces.append(lax.dynamic_slice_in_dim(factor[number], start, width, 1))
        return pieces
    return pl.pallas_call(
        spread_kernel,
        grid_spec=pltpu.PrefetchScalarGridSpec(
            num_scalar_prefetch=1,
            grid=(1,),
            in_specs=[pl.BlockSpec(factor.shape, lambda i, m: (0, 0, 0))],
            out_specs=[pl.BlockSpec((unit_rows, width), lambda i, m: (0, 0))] * (nsuper * count),
        ),
        out_shape=[jax.ShapeDtypeStruct((unit_rows, width), factor.dtype)] * (nsuper * count),
        compiler_params=pltpu.CompilerParams(vmem_limit_bytes=VMEM_LIMIT),
        cost_estimate=pl.CostEstimate(
            flops=0, bytes_accessed=2 * factor.size * 4, transcendentals=0
        ),
        name="spread",
    )(meta, factor)


def split_kernel(tile_ref, high_ref, low_ref):
    high_ref[...], low_ref[...] = halves(tile_ref[...])


def split(tiles, steps):
    rows, cols = tiles.shape
    block = pl.BlockSpec((rows // steps, cols), lambda i: (i, 0))
    shape = jax.ShapeDtypeStruct((rows, cols), jnp.bfloat16)
    return pl.pallas_call(
        split_kernel,
        grid=(steps,),
        in_specs=[block],
        out_specs=[block, block],
        out_shape=[shape, shape],
        compiler_params=pltpu.CompilerParams(vmem_limit_bytes=VMEM_LIMIT),
        cost_estimate=pl.CostEstimate(flops=0, bytes_accessed=8 * rows * cols, transcendentals=0),
        name="split",
    )(tiles)


def partial_kernel(places, ratio, count, meta, high_ref, low_ref, *refs):
    piece_refs = refs[: len(places)]
    out_ref, right_high, right_low = refs[len(places) :]
    columns = out_ref.shape[1]
    blocks = high_ref.shape[1] // columns
    step = pl.program_id(0)

    @pl.when(step == 0)
    def _assemble():
        for ref, place in zip(piece_refs, places):
            if place is None:
                right_high[...], right_low[...] = halves(ref[...])
                continue
            offset, first = place
            unit_rows, width = ref.shape[1:]
            owner = meta[0] ^ offset
            column = owner // ratio
            lane = pl.multiple_of(column * width, width)
            for r in range(ref.shape[0]):
                unit = (owner % ratio) * count + (column ^ (first + r))
                rows = pl.ds(pl.multiple_of(unit * unit_rows, unit_rows), unit_rows)
                high, low = halves(ref[r])
                right_high[rows, pl.ds(lane, width)] = high
                right_low[rows, pl.ds(lane, width)] = low

    out_ref[...] = jnp.zeros_like(out_ref)

    @pl.when(meta[3 + blocks + step] != 0)
    def _multiply():
        def add(number, carry):
            span = pl.ds(pl.multiple_of(meta[3 + number] * columns, columns), columns)
            high, low = high_ref[:, span], low_ref[:, span]
            right = right_high[span, :]
            dot = functools.partial(jnp.dot, preferred_element_type=jnp.float32)
            out_ref[...] += dot(high, right) + (dot(high, right_low[span, :]) + dot(low, right))
            return carry

        lax.fori_loop(0, meta[2], add, 0)


def partial_product(meta, high, low, pieces, places, ratio, count, columns):
    rows, cols = high.shape
    chunk = rows // count
    tile = pl.BlockSpec((chunk, cols), lambda i, m: (i, 0))
    whole = [
        pl.BlockSpec(piece.shape, functools.partial(lambda n, i, m: (0,) * n, piece.ndim))
        for piece in pieces
    ]
    return pl.pallas_call(
        functools.partial(partial_kernel, places, ratio, count),
        grid_spec=pltpu.PrefetchScalarGridSpec(
            num_scalar_prefetch=1,
            grid=(count,),
            in_specs=[tile, tile] + whole,
            out_specs=pl.BlockSpec((chunk, columns), lambda i, m: (i, 0)),
            scratch_shapes=[pltpu.VMEM((cols, columns), jnp.bfloat16)] * 2,
        ),
        out_shape=jax.ShapeDtypeStruct((rows, columns), jnp.float32),
        compiler_params=pltpu.CompilerParams(vmem_limit_bytes=VMEM_LIMIT),
        cost_estimate=pl.CostEstimate(
            flops=6 * rows * cols * columns,
            bytes_accessed=4 * (rows * cols + cols * columns + rows * columns),
            transcendentals=0,
        ),
        name="partial_product",
    )(meta, high, low, *pieces)


def to_plane(sends, count, ratio):
    pcol_count = count * ratio
    received = []
    for r, piece in enumerate(sends):
        perm = []
        for z in range(count):
            for c in range(count):
                for k in range(ratio):
                    source = z * pcol_count + c * ratio + k
                    perm.append((source, c * pcol_count + (z ^ r) * ratio + k))
        received.append(lax.ppermute(piece, BOTH, perm))
    return jnp.stack(received)


def gather_plane(own, pcol_count):
    parts = own.shape[0]
    found = {0: [(own, 0)]}
    even = [o for o in range(2, pcol_count, 2)]
    for offset in sorted(even, key=lambda o: bin(o).count("1")):
        bits = [1 << b for b in range(1, pcol_count.bit_length()) if offset >> b & 1]
        if len(bits) == 2 and parts % 2 == 0:
            half = parts // 2
            found[offset] = [
                (flip(found[offset ^ bit][0][0][i * half : (i + 1) * half], "pcol", bit), i * half)
                for i, bit in enumerate(bits)
            ]
        else:
            found[offset] = [
                (flip(piece, "pcol", bits[0]), first) for piece, first in found[offset ^ bits[0]]
            ]
    for offset in [0] + even:
        if pcol_count > 1:
            found[offset ^ 1] = [(flip(piece, "pcol", 1), first) for piece, first in found[offset]]
    return [(piece, o, first) for o in sorted(found) for piece, first in found[o]]


def gather_whole(own, count, ratio):
    _, unit_rows, width = own.shape
    gathered = lax.all_gather(own, "pcol", axis=0)
    column = np.arange(count)[None, None, :]
    owner = column * ratio + np.arange(ratio)[:, None, None]
    part = np.broadcast_to(column ^ np.arange(count)[None, :, None], (ratio, count, count))
    rows = jnp.transpose(gathered[np.broadcast_to(owner, part.shape), part], (0, 1, 3, 2, 4))
    return rows.reshape(ratio * count * unit_rows, count * width)


def sum_over_line(partial, count, z):
    rows = partial.shape[0] // count

    def chunk(index):
        start = jnp.clip(index, 0, count - 1) * rows
        return lax.dynamic_slice_in_dim(partial, start, rows, 0)

    up = down = None
    for t in range(1, count):
        up_send, down_send = chunk(z + count - t), chunk(z + t - count)
        if up is not None:
            up_send, down_send = up_send + up, down_send + down
        up = lax.ppermute(up_send, "prow", [(i, i + 1) for i in range(min(t, count - 1))])
        down = lax.ppermute(
            down_send, "prow", [(i, i - 1) for i in range(max(count - t, 1), count)]
        )
    mine = chunk(z)
    return mine if up is None else mine + up + down


def sum_rows(matrix, pcol_count, count, pcol_index):
    rows, columns = matrix.shape
    if pcol_count > 1:
        paired = matrix.reshape(pcol_count // 2, 2, rows // pcol_count, columns)
        core = pcol_index % 2
        send = lax.dynamic_index_in_dim(paired, 1 - core, 1, keepdims=False)
        mine = lax.dynamic_index_in_dim(paired, core, 1, keepdims=False) + flip(send, "pcol", 1)
        chip = pcol_index // 2
        matrix = lax.dynamic_index_in_dim(mine, chip, 0, keepdims=False)
        for o in range(1, pcol_count // 2):
            send = lax.dynamic_index_in_dim(mine, chip ^ o, 0, keepdims=False)
            matrix = matrix + flip(send, "pcol", 2 * o)
    bit = 1
    while bit < count:
        matrix = matrix + flip(matrix, "prow", bit)
        bit *= 2
    return matrix


def body(inverse_tiles, factor, link_factor, diag_inverse, ancestors):
    row_count, col_count = inverse_tiles.shape
    nsuper, unit_rows, columns = factor.shape
    count = lax.axis_size("prow")
    pcol_count = lax.axis_size("pcol")
    ratio = col_count // row_count
    z = lax.axis_index("prow")
    pcol_index = lax.axis_index("pcol")
    slice_rows = columns // pcol_count
    slice_start = pcol_index * slice_rows
    width = columns // count

    listed = jnp.any(
        lax.iota(jnp.int32, count * col_count // columns)[None, :, None] == ancestors[:, None, :],
        axis=2,
    )
    unit_ids = (pcol_index * count + lax.iota(jnp.int32, count)) * unit_rows // columns
    chunk_kept = listed[:, unit_ids]
    keep = chunk_kept[:, z][:, None, None]
    blocks = col_count // columns
    block_kept = lax.dynamic_slice_in_dim(listed, z * blocks, blocks, 1)
    ids = lax.iota(jnp.int32, blocks)
    rank = jnp.cumsum(block_kept.astype(jnp.int32), axis=1) - 1
    taken = (rank[:, None, :] == ids[None, :, None]) & block_kept[:, None, :]
    order = jnp.sum(jnp.where(taken, ids[None, None, :], 0), axis=2)
    place = jnp.stack([pcol_index, z]).astype(jnp.int32)
    metas = [
        jnp.concatenate(
            [
                place,
                jnp.sum(block_kept[number], dtype=jnp.int32)[None],
                order[number].astype(jnp.int32),
                chunk_kept[number].astype(jnp.int32),
            ]
        )
        for number in range(nsuper)
    ]

    sends = spread(place, factor, count)
    high, low = split(inverse_tiles, count)
    local = jnp.where(keep, factor, 0.0)

    partials = []
    for number in range(nsuper):
        own = to_plane(sends[number * count : (number + 1) * count], count, ratio)
        if width % LANES:
            pieces, places = [gather_whole(own, count, ratio)], [None]
        else:
            found = gather_plane(own, pcol_count)
            pieces = [piece for piece, _, _ in found]
            places = [(offset, first) for _, offset, first in found]
        partials.append(
            partial_product(metas[number], high, low, pieces, places, ratio, count, columns)
        )

    offdiag_list, diag_list, link_list = [], [], []
    prior_offdiag = prior_part = prior_base = None
    for number in range(nsuper):
        summed = sum_over_line(partials[number], count, z)
        gram_part = product(local[number].T, summed)
        if number == 0:
            result = -jnp.where(keep[number], summed, 0.0)
            part = gram_part
            base = diag_inverse[0]
        else:
            link_block = link_factor[number - 1]
            result = -jnp.where(keep[number], summed + product(prior_offdiag, link_block), 0.0)
            cross_part = product(prior_offdiag.T, local[number])
            link_part = cross_part + product(prior_part, link_block)
            rest = product(cross_part.T, link_block) + product(link_block.T, link_part)
            part = gram_part + rest
            base_link = product(prior_base, link_block)
            base = diag_inverse[number] + product(link_block.T, base_link)
            link_sum = sum_rows(link_part, pcol_count, count, pcol_index)
            link_list.append(
                -(link_sum + lax.dynamic_slice_in_dim(base_link, slice_start, slice_rows, 0))
            )
        diag_sum = sum_rows(part, pcol_count, count, pcol_index)
        diag_list.append(diag_sum + lax.dynamic_slice_in_dim(base, slice_start, slice_rows, 0))
        offdiag_list.append(result)
        prior_offdiag, prior_part, prior_base = result, part, base
    return (jnp.stack(offdiag_list), jnp.stack(diag_list), jnp.stack(link_list))


def solution(mesh):
    in_specs = (P("pcol", "prow"), P(None, ("pcol", "prow"), None), P(), P(), P())
    out_specs = (P(None, ("pcol", "prow"), None), P(None, "pcol", None), P(None, "pcol", None))
    return jax.shard_map(body, mesh=mesh, in_specs=in_specs, out_specs=out_specs, check_vma=False)
```

```python
import functools

import jax
import jax.numpy as jnp
import numpy as np
from jax import lax
from jax.experimental import pallas as pl
from jax.experimental.pallas import tpu as pltpu
from jax.sharding import PartitionSpec as P

BOTH = ("prow", "pcol")
VMEM_LIMIT = 48 * 1024 * 1024
LANES = 128


def product(left_part, right_part):
    return jnp.dot(
        left_part, right_part, precision=lax.Precision.HIGH, preferred_element_type=jnp.float32
    )


def halves(value):
    high = value.astype(jnp.bfloat16)
    low = (value - high.astype(jnp.float32)).astype(jnp.bfloat16)
    return high, low


def flip(value, axis, bit):
    return lax.ppermute(value, axis, [(i, i ^ bit) for i in range(lax.axis_size(axis))])


def spread_kernel(meta, factor_ref, *out_refs):
    nsuper = factor_ref.shape[0]
    count = len(out_refs) // nsuper
    width = out_refs[0].shape[1]
    for number in range(nsuper):
        for r in range(count):
            start = pl.multiple_of((meta[0] ^ r) * width, width)
            out_refs[number * count + r][...] = factor_ref[number, :, pl.ds(start, width)]


def spread(meta, factor, count):
    nsuper, unit_rows, columns = factor.shape
    width = columns // count
    if width % LANES:
        pieces = []
        for number in range(nsuper):
            for r in range(count):
                start = (meta[0] ^ r) * width
                pieces.append(lax.dynamic_slice_in_dim(factor[number], start, width, 1))
        return pieces
    return pl.pallas_call(
        spread_kernel,
        grid_spec=pltpu.PrefetchScalarGridSpec(
            num_scalar_prefetch=1,
            grid=(1,),
            in_specs=[pl.BlockSpec(factor.shape, lambda i, m: (0, 0, 0))],
            out_specs=[pl.BlockSpec((unit_rows, width), lambda i, m: (0, 0))] * (nsuper * count),
        ),
        out_shape=[jax.ShapeDtypeStruct((unit_rows, width), factor.dtype)] * (nsuper * count),
        compiler_params=pltpu.CompilerParams(vmem_limit_bytes=VMEM_LIMIT),
        cost_estimate=pl.CostEstimate(
            flops=0, bytes_accessed=2 * factor.size * 4, transcendentals=0
        ),
        name="spread",
    )(meta, factor)


def partial_kernel(places, ratio, count, meta, tile_ref, *refs):
    piece_refs = refs[: len(places)]
    out_refs = refs[len(places) : -2]
    right_high, right_low = refs[-2:]
    columns = out_refs[0].shape[1]
    blocks = tile_ref.shape[1] // columns
    step = pl.program_id(0)

    @pl.when(step == 0)
    def _assemble():
        for ref, offset in zip(piece_refs, places):
            if offset is None:
                right_high[...], right_low[...] = halves(ref[...])
                continue
            unit_rows, width = ref.shape[1:]
            owner = meta[0] ^ offset
            column = owner // ratio
            lane = pl.multiple_of(column * width, width)
            for r in range(ref.shape[0]):
                unit = (owner % ratio) * count + (column ^ meta[1] ^ r)
                rows = pl.ds(pl.multiple_of(unit * unit_rows, unit_rows), unit_rows)
                high, low = halves(ref[r])
                right_high[rows, pl.ds(lane, width)] = high
                right_low[rows, pl.ds(lane, width)] = low

    def multiply(out_ref):
        out_ref[...] = jnp.zeros_like(out_ref)

        def add(number, carry):
            span = pl.ds(pl.multiple_of(meta[3 + number] * columns, columns), columns)
            high, low = halves(tile_ref[:, span])
            right = right_high[span, :]
            dot = functools.partial(jnp.dot, preferred_element_type=jnp.float32)
            out_ref[...] += dot(high, right) + (dot(high, right_low[span, :]) + dot(low, right))
            return carry

        lax.fori_loop(0, jnp.where(meta[3 + blocks + count + step] != 0, meta[2], 0), add, 0)

    for number, out_ref in enumerate(out_refs):
        pl.when(step == number)(functools.partial(multiply, out_ref))


def partial_product(meta, tiles, pieces, places, ratio, count, columns):
    rows, cols = tiles.shape
    chunk = rows // count
    first = 3 + cols // columns
    whole = [
        pl.BlockSpec(piece.shape, functools.partial(lambda n, i, m: (0,) * n, piece.ndim))
        for piece in pieces
    ]
    return pl.pallas_call(
        functools.partial(partial_kernel, places, ratio, count),
        grid_spec=pltpu.PrefetchScalarGridSpec(
            num_scalar_prefetch=1,
            grid=(count,),
            in_specs=[pl.BlockSpec((chunk, cols), lambda i, m: (m[first + i], 0))] + whole,
            out_specs=[pl.BlockSpec((chunk, columns), lambda i, m: (0, 0))] * count,
            scratch_shapes=[pltpu.VMEM((cols, columns), jnp.bfloat16)] * 2,
        ),
        out_shape=[jax.ShapeDtypeStruct((chunk, columns), jnp.float32)] * count,
        compiler_params=pltpu.CompilerParams(vmem_limit_bytes=VMEM_LIMIT),
        cost_estimate=pl.CostEstimate(
            flops=6 * rows * cols * columns,
            bytes_accessed=4 * (rows * cols + cols * columns + rows * columns),
            transcendentals=0,
        ),
        name="partial_product",
    )(meta, tiles, *pieces)


def to_plane(sends, count, ratio):
    pcol_count = count * ratio
    received = []
    for r, piece in enumerate(sends):
        perm = []
        for z in range(count):
            for c in range(count):
                for k in range(ratio):
                    source = z * pcol_count + c * ratio + k
                    perm.append((source, c * pcol_count + (c ^ z ^ r) * ratio + k))
        received.append(lax.ppermute(piece, BOTH, perm))
    return jnp.stack(received)


def gather_plane(own, pcol_count):
    found = {0: own}
    for offset in range(2, pcol_count, 2):
        found[offset] = flip(own, "pcol", offset)
    for offset in range(0, pcol_count, 2):
        found[offset + 1] = flip(found[offset], "pcol", 1)
    return found


def gather_whole(own, count, ratio):
    _, unit_rows, width = own.shape
    gathered = lax.all_gather(own, "pcol", axis=0)
    column = np.arange(count)[None, None, :]
    owner = np.broadcast_to(
        column * ratio + np.arange(ratio)[:, None, None], (ratio, count, count)
    )
    part = jnp.asarray(column ^ np.arange(count)[None, :, None]) ^ lax.axis_index("prow")
    part = jnp.broadcast_to(part, owner.shape)
    rows = jnp.transpose(gathered[owner, part], (0, 1, 3, 2, 4))
    return rows.reshape(ratio * count * unit_rows, count * width)


FOUR_SLOTS = ((3, 2, 1, 0), (2, 0, 3, 1), (1, 3, 0, 2), (0, 1, 2, 3))


def slots_of(count):
    return FOUR_SLOTS if count == len(FOUR_SLOTS) else (tuple(range(count)),) * count


def sum_over_four(slots):
    near = lax.ppermute(slots[0], "prow", [(0, 1), (3, 2)])
    total = lax.ppermute(slots[1], "prow", [(0, 2), (2, 3), (3, 1), (1, 0)])
    middle = lax.ppermute(slots[0], "prow", [(1, 2), (2, 1)])
    last = lax.ppermute(slots[2] + near, "prow", [(1, 3), (2, 0), (0, 1), (3, 2)])
    return ((slots[3] + total) + middle) + last


def sum_over_line(slots, z):
    count = len(slots)
    if count == len(FOUR_SLOTS):
        return sum_over_four(slots)
    chunks = jnp.stack(slots)

    def chunk(index):
        return lax.dynamic_index_in_dim(chunks, jnp.clip(index, 0, count - 1), 0, keepdims=False)

    up = down = None
    for t in range(1, count):
        up_send, down_send = chunk(z + count - t), chunk(z + t - count)
        if up is not None:
            up_send, down_send = up_send + up, down_send + down
        up = lax.ppermute(up_send, "prow", [(i, i + 1) for i in range(min(t, count - 1))])
        down = lax.ppermute(
            down_send, "prow", [(i, i - 1) for i in range(max(count - t, 1), count)]
        )
    mine = chunk(z)
    return mine if up is None else mine + up + down


def sum_rows(matrices, pcol_count, count, pcol_index):
    number, rows, columns = matrices.shape
    if pcol_count > 1:
        paired = matrices.reshape(number, pcol_count // 2, 2, rows // pcol_count, columns)
        core = pcol_index % 2
        send = lax.dynamic_index_in_dim(paired, 1 - core, 2, keepdims=False)
        mine = lax.dynamic_index_in_dim(paired, core, 2, keepdims=False) + flip(send, "pcol", 1)
        chip = pcol_index // 2
        matrices = lax.dynamic_index_in_dim(mine, chip, 1, keepdims=False)
        for o in range(1, pcol_count // 2):
            send = lax.dynamic_index_in_dim(mine, chip ^ o, 1, keepdims=False)
            matrices = matrices + flip(send, "pcol", 2 * o)
    bit = 1
    while bit < count:
        matrices = matrices + flip(matrices, "prow", bit)
        bit *= 2
    return matrices


def body(inverse_tiles, factor, link_factor, diag_inverse, ancestors):
    row_count, col_count = inverse_tiles.shape
    nsuper, unit_rows, columns = factor.shape
    count = lax.axis_size("prow")
    pcol_count = lax.axis_size("pcol")
    ratio = col_count // row_count
    z = lax.axis_index("prow")
    pcol_index = lax.axis_index("pcol")
    slice_rows = columns // pcol_count
    slice_start = pcol_index * slice_rows
    width = columns // count

    listed = jnp.any(
        lax.iota(jnp.int32, count * col_count // columns)[None, :, None] == ancestors[:, None, :],
        axis=2,
    )
    unit_ids = (pcol_index * count + lax.iota(jnp.int32, count)) * unit_rows // columns
    chunk_kept = listed[:, unit_ids]
    keep = chunk_kept[:, z][:, None, None]
    blocks = col_count // columns
    block_kept = lax.dynamic_slice_in_dim(listed, z * blocks, blocks, 1)
    ids = lax.iota(jnp.int32, blocks)
    rank = jnp.cumsum(block_kept.astype(jnp.int32), axis=1) - 1
    taken = (rank[:, None, :] == ids[None, :, None]) & block_kept[:, None, :]
    order = jnp.sum(jnp.where(taken, ids[None, None, :], 0), axis=2)
    slots = jnp.asarray(slots_of(count), jnp.int32)[z]
    place = jnp.stack([pcol_index, z]).astype(jnp.int32)
    metas = [
        jnp.concatenate(
            [
                place,
                jnp.sum(block_kept[number], dtype=jnp.int32)[None],
                order[number].astype(jnp.int32),
                slots,
                chunk_kept[number][slots].astype(jnp.int32),
            ]
        )
        for number in range(nsuper)
    ]

    target = ((pcol_index // ratio) ^ z).astype(jnp.int32)
    sends = spread(target[None], factor, count)
    local = jnp.where(keep, factor, 0.0)

    partials = []
    for number in range(nsuper):
        own = to_plane(sends[number * count : (number + 1) * count], count, ratio)
        if width % LANES:
            pieces, places = [gather_whole(own, count, ratio)], [None]
        else:
            found = gather_plane(own, pcol_count)
            places, pieces = list(found.keys()), list(found.values())
        partials.append(
            partial_product(metas[number], inverse_tiles, pieces, places, ratio, count, columns)
        )

    def own_rows(matrices):
        return lax.dynamic_slice_in_dim(matrices, slice_start, slice_rows, -2)

    offdiag_list, sums, bases = [], [], []
    for number in range(nsuper):
        summed = sum_over_line(partials[number], z)
        part = product(local[number].T, summed)
        if number == 0:
            result = -jnp.where(keep[number], summed, 0.0)
            base = diag_inverse[0]
            ready = [part]
        else:
            link_block = link_factor[number - 1]
            result = -jnp.where(keep[number], summed + product(prior_offdiag, link_block), 0.0)
            cross_part = product(prior_offdiag.T, local[number])
            link_part = cross_part + product(prior_part, link_block)
            rest = product(cross_part.T, link_block) + product(link_block.T, link_part)
            base_link = product(prior_base, link_block)
            base = diag_inverse[number] + product(link_block.T, base_link)
            sums.append(sum_rows(jnp.stack(ready + [link_part]), pcol_count, count, pcol_index))
            bases += [own_rows(prior_base), own_rows(base_link)]
            part = part + rest
            ready = [part]
        offdiag_list.append(result)
        prior_offdiag, prior_part, prior_base = result, part, base
    sums.append(sum_rows(jnp.stack(ready), pcol_count, count, pcol_index))
    bases.append(own_rows(prior_base))
    totals = jnp.concatenate(sums) + jnp.stack(bases)
    return (jnp.stack(offdiag_list), totals[0::2], -totals[1::2])


def solution(mesh):
    in_specs = (P("pcol", "prow"), P(None, ("pcol", "prow"), None), P(), P(), P())
    out_specs = (P(None, ("pcol", "prow"), None), P(None, "pcol", None), P(None, "pcol", None))
    return jax.shard_map(body, mesh=mesh, in_specs=in_specs, out_specs=out_specs, check_vma=False)
```

```python
import functools

import jax
import jax.numpy as jnp
from jax import lax
from jax.experimental import pallas as pl
from jax.experimental.pallas import tpu as pltpu
from jax.sharding import PartitionSpec as P

BOTH = ("prow", "pcol")
VMEM_LIMIT = 48 * 1024 * 1024
LANES = 128


def product(left_part, right_part):
    return jnp.dot(
        left_part, right_part, precision=lax.Precision.HIGH, preferred_element_type=jnp.float32
    )


def halves(value):
    high = value.astype(jnp.bfloat16)
    low = (value - high.astype(jnp.float32)).astype(jnp.bfloat16)
    return high, low


def flip(value, axis, bit):
    return lax.ppermute(value, axis, [(i, i ^ bit) for i in range(lax.axis_size(axis))])


def partial_kernel(places, ratio, count, meta, tile_ref, *refs):
    piece_refs = refs[: len(places)]
    out_refs = refs[len(places) : -2]
    right_high, right_low = refs[-2:]
    columns = out_refs[0].shape[1]
    blocks = tile_ref.shape[1] // columns
    step = pl.program_id(0)

    @pl.when(step == 0)
    def _assemble():
        for ref, offset in zip(piece_refs, places):
            if offset is None:
                right_high[...], right_low[...] = halves(ref[...])
                continue
            unit_rows, width = ref.shape[1:]
            owner = meta[0] ^ offset
            column = owner // ratio
            lane = pl.multiple_of(column * width, width)
            for r in range(ref.shape[0]):
                unit = (owner % ratio) * count + r
                rows = pl.ds(pl.multiple_of(unit * unit_rows, unit_rows), unit_rows)
                high, low = halves(ref[r])
                right_high[rows, pl.ds(lane, width)] = high
                right_low[rows, pl.ds(lane, width)] = low

    def multiply(out_ref):
        out_ref[...] = jnp.zeros_like(out_ref)

        def add(number, carry):
            span = pl.ds(pl.multiple_of(meta[3 + number] * columns, columns), columns)
            high, low = halves(tile_ref[:, span])
            right = right_high[span, :]
            dot = functools.partial(jnp.dot, preferred_element_type=jnp.float32)
            out_ref[...] += dot(high, right) + (dot(high, right_low[span, :]) + dot(low, right))
            return carry

        lax.fori_loop(0, jnp.where(meta[3 + blocks + count + step] != 0, meta[2], 0), add, 0)

    for number, out_ref in enumerate(out_refs):
        pl.when(step == number)(functools.partial(multiply, out_ref))


def partial_product(meta, tiles, pieces, places, ratio, count, columns):
    rows, cols = tiles.shape
    chunk = rows // count
    first = 3 + cols // columns
    whole = [
        pl.BlockSpec(piece.shape, functools.partial(lambda n, i, m: (0,) * n, piece.ndim))
        for piece in pieces
    ]
    return pl.pallas_call(
        functools.partial(partial_kernel, places, ratio, count),
        grid_spec=pltpu.PrefetchScalarGridSpec(
            num_scalar_prefetch=1,
            grid=(count,),
            in_specs=[pl.BlockSpec((chunk, cols), lambda i, m: (m[first + i], 0))] + whole,
            out_specs=[pl.BlockSpec((chunk, columns), lambda i, m: (0, 0))] * count,
            scratch_shapes=[pltpu.VMEM((cols, columns), jnp.bfloat16)] * 2,
        ),
        out_shape=[jax.ShapeDtypeStruct((chunk, columns), jnp.float32)] * count,
        compiler_params=pltpu.CompilerParams(vmem_limit_bytes=VMEM_LIMIT),
        cost_estimate=pl.CostEstimate(
            flops=6 * rows * cols * columns,
            bytes_accessed=4 * (rows * cols + cols * columns + rows * columns),
            transcendentals=0,
        ),
        name="partial_product",
    )(meta, tiles, *pieces)


def to_plane(pieces, count, ratio):
    groups = [[c * ratio + k for c in range(count)] for k in range(ratio)]
    spread = lax.all_to_all(pieces, "pcol", 0, 0, axis_index_groups=groups)
    return lax.all_to_all(spread, "prow", 0, 0)


def gather_plane(own, pcol_count):
    found = {0: own}
    for offset in range(2, pcol_count, 2):
        found[offset] = flip(own, "pcol", offset)
    for offset in range(0, pcol_count, 2):
        found[offset + 1] = flip(found[offset], "pcol", 1)
    return found


def gather_whole(own, count, ratio):
    _, unit_rows, width = own.shape
    gathered = lax.all_gather(own, "pcol", axis=0)
    split = gathered.reshape(count, ratio, count, unit_rows, width)
    rows = jnp.transpose(split, (1, 2, 3, 0, 4))
    return rows.reshape(ratio * count * unit_rows, count * width)


FOUR_SLOTS = ((3, 2, 1, 0), (2, 0, 3, 1), (1, 3, 0, 2), (0, 1, 2, 3))


def slots_of(count):
    return FOUR_SLOTS if count == len(FOUR_SLOTS) else (tuple(range(count)),) * count


def sum_over_four(slots):
    near = lax.ppermute(slots[0], "prow", [(0, 1), (3, 2)])
    total = lax.ppermute(slots[1], "prow", [(0, 2), (2, 3), (3, 1), (1, 0)])
    middle = lax.ppermute(slots[0], "prow", [(1, 2), (2, 1)])
    last = lax.ppermute(slots[2] + near, "prow", [(1, 3), (2, 0), (0, 1), (3, 2)])
    return ((slots[3] + total) + middle) + last


def sum_over_line(slots, z):
    count = len(slots)
    if count == len(FOUR_SLOTS):
        return sum_over_four(slots)
    chunks = jnp.stack(slots)

    def chunk(index):
        return lax.dynamic_index_in_dim(chunks, jnp.clip(index, 0, count - 1), 0, keepdims=False)

    up = down = None
    for t in range(1, count):
        up_send, down_send = chunk(z + count - t), chunk(z + t - count)
        if up is not None:
            up_send, down_send = up_send + up, down_send + down
        up = lax.ppermute(up_send, "prow", [(i, i + 1) for i in range(min(t, count - 1))])
        down = lax.ppermute(
            down_send, "prow", [(i, i - 1) for i in range(max(count - t, 1), count)]
        )
    mine = chunk(z)
    return mine if up is None else mine + up + down


def sum_rows(matrices, pcol_count, count, pcol_index):
    number, rows, columns = matrices.shape
    if pcol_count > 1:
        paired = matrices.reshape(number, pcol_count // 2, 2, rows // pcol_count, columns)
        core = pcol_index % 2
        send = lax.dynamic_index_in_dim(paired, 1 - core, 2, keepdims=False)
        mine = lax.dynamic_index_in_dim(paired, core, 2, keepdims=False) + flip(send, "pcol", 1)
        chip = pcol_index // 2
        matrices = lax.dynamic_index_in_dim(mine, chip, 1, keepdims=False)
        for o in range(1, pcol_count // 2):
            send = lax.dynamic_index_in_dim(mine, chip ^ o, 1, keepdims=False)
            matrices = matrices + flip(send, "pcol", 2 * o)
    bit = 1
    while bit < count:
        matrices = matrices + flip(matrices, "prow", bit)
        bit *= 2
    return matrices


def body(inverse_tiles, factor, link_factor, diag_inverse, ancestors):
    row_count, col_count = inverse_tiles.shape
    nsuper, unit_rows, columns = factor.shape
    count = lax.axis_size("prow")
    pcol_count = lax.axis_size("pcol")
    ratio = col_count // row_count
    z = lax.axis_index("prow")
    pcol_index = lax.axis_index("pcol")
    slice_rows = columns // pcol_count
    slice_start = pcol_index * slice_rows
    width = columns // count

    listed = jnp.any(
        lax.iota(jnp.int32, count * col_count // columns)[None, :, None] == ancestors[:, None, :],
        axis=2,
    )
    unit_ids = (pcol_index * count + lax.iota(jnp.int32, count)) * unit_rows // columns
    chunk_kept = listed[:, unit_ids]
    keep = chunk_kept[:, z][:, None, None]
    blocks = col_count // columns
    block_kept = lax.dynamic_slice_in_dim(listed, z * blocks, blocks, 1)
    ids = lax.iota(jnp.int32, blocks)
    rank = jnp.cumsum(block_kept.astype(jnp.int32), axis=1) - 1
    taken = (rank[:, None, :] == ids[None, :, None]) & block_kept[:, None, :]
    order = jnp.sum(jnp.where(taken, ids[None, None, :], 0), axis=2)
    slots = jnp.asarray(slots_of(count), jnp.int32)[z]
    place = jnp.stack([pcol_index, z]).astype(jnp.int32)
    metas = [
        jnp.concatenate(
            [
                place,
                jnp.sum(block_kept[number], dtype=jnp.int32)[None],
                order[number].astype(jnp.int32),
                slots,
                chunk_kept[number][slots].astype(jnp.int32),
            ]
        )
        for number in range(nsuper)
    ]

    local = jnp.where(keep, factor, 0.0)
    cut = jnp.swapaxes(factor.reshape(nsuper, unit_rows, count, width), 1, 2)

    partials = []
    for number in range(nsuper):
        own = to_plane(cut[number], count, ratio)
        if width % LANES:
            pieces, places = [gather_whole(own, count, ratio)], [None]
        else:
            found = gather_plane(own, pcol_count)
            places, pieces = list(found.keys()), list(found.values())
        partials.append(
            partial_product(metas[number], inverse_tiles, pieces, places, ratio, count, columns)
        )

    def own_rows(matrices):
        return lax.dynamic_slice_in_dim(matrices, slice_start, slice_rows, -2)

    offdiag_list, sums, bases = [], [], []
    for number in range(nsuper):
        summed = sum_over_line(partials[number], z)
        part = product(local[number].T, summed)
        if number == 0:
            result = -jnp.where(keep[number], summed, 0.0)
            base = diag_inverse[0]
            ready = [part]
        else:
            link_block = link_factor[number - 1]
            result = -jnp.where(keep[number], summed + product(prior_offdiag, link_block), 0.0)
            cross_part = product(prior_offdiag.T, local[number])
            link_part = cross_part + product(prior_part, link_block)
            rest = product(cross_part.T, link_block) + product(link_block.T, link_part)
            base_link = product(prior_base, link_block)
            base = diag_inverse[number] + product(link_block.T, base_link)
            sums.append(sum_rows(jnp.stack(ready + [link_part]), pcol_count, count, pcol_index))
            bases += [own_rows(prior_base), own_rows(base_link)]
            part = part + rest
            ready = [part]
        offdiag_list.append(result)
        prior_offdiag, prior_part, prior_base = result, part, base
    sums.append(sum_rows(jnp.stack(ready), pcol_count, count, pcol_index))
    bases.append(own_rows(prior_base))
    totals = jnp.concatenate(sums) + jnp.stack(bases)
    return (jnp.stack(offdiag_list), totals[0::2], -totals[1::2])


def solution(mesh):
    in_specs = (P("pcol", "prow"), P(None, ("pcol", "prow"), None), P(), P(), P())
    out_specs = (P(None, ("pcol", "prow"), None), P(None, "pcol", None), P(None, "pcol", None))
    return jax.shard_map(body, mesh=mesh, in_specs=in_specs, out_specs=out_specs, check_vma=False)
```

```python
import functools

import jax
import jax.numpy as jnp
from jax import lax
from jax.experimental import pallas as pl
from jax.experimental.pallas import tpu as pltpu
from jax.sharding import PartitionSpec as P

BOTH = ("prow", "pcol")
VMEM_LIMIT = 48 * 1024 * 1024
LANES = 128


def product(left_part, right_part):
    return jnp.dot(
        left_part, right_part, precision=lax.Precision.HIGH, preferred_element_type=jnp.float32
    )


def halves(value):
    high = value.astype(jnp.bfloat16)
    low = (value - high.astype(jnp.float32)).astype(jnp.bfloat16)
    return high, low


def flip(value, axis, bit):
    return lax.ppermute(value, axis, [(i, i ^ bit) for i in range(lax.axis_size(axis))])


def nothing_kernel(*refs):
    del refs


def after(value, *others):
    anywhere = pl.BlockSpec(memory_space=pl.ANY)
    return pl.pallas_call(
        nothing_kernel,
        in_specs=[anywhere] * (1 + len(others)),
        out_specs=anywhere,
        out_shape=jax.ShapeDtypeStruct(value.shape, value.dtype),
        input_output_aliases={0: 0},
        cost_estimate=pl.CostEstimate(flops=0, bytes_accessed=0, transcendentals=0),
        name="after",
    )(value, *others)


def cut_kernel(place, factor_ref, *out_refs):
    width = out_refs[0].shape[1]
    for o, out_ref in enumerate(out_refs):
        start = pl.multiple_of((place[2] ^ o) * width, width)
        out_ref[...] = factor_ref[0, :, pl.ds(start, width)]


def cut(place, factor, number, count):
    _, unit_rows, columns = factor.shape
    width = columns // count
    return pl.pallas_call(
        cut_kernel,
        grid_spec=pltpu.PrefetchScalarGridSpec(
            num_scalar_prefetch=1,
            grid=(1,),
            in_specs=[pl.BlockSpec((1, unit_rows, columns), lambda i, m: (number, 0, 0))],
            out_specs=[pl.BlockSpec((unit_rows, width), lambda i, m: (0, 0))] * count,
        ),
        out_shape=[jax.ShapeDtypeStruct((unit_rows, width), factor.dtype)] * count,
        compiler_params=pltpu.CompilerParams(vmem_limit_bytes=VMEM_LIMIT),
        cost_estimate=pl.CostEstimate(
            flops=0, bytes_accessed=8 * unit_rows * columns, transcendentals=0
        ),
        name="cut",
    )(place, factor)


def arrange_kernel(place, *refs):
    out_ref = refs[-1]
    for o, piece_ref in enumerate(refs[:-1]):
        out_ref[place[2] ^ o] = piece_ref[...]


def arrange(place, pieces):
    shape = pieces[0].shape
    count = len(pieces)
    return pl.pallas_call(
        arrange_kernel,
        grid_spec=pltpu.PrefetchScalarGridSpec(
            num_scalar_prefetch=1,
            grid=(1,),
            in_specs=[pl.BlockSpec(shape, lambda i, m: (0, 0))] * count,
            out_specs=pl.BlockSpec((count,) + shape, lambda i, m: (0, 0, 0)),
        ),
        out_shape=jax.ShapeDtypeStruct((count,) + shape, pieces[0].dtype),
        compiler_params=pltpu.CompilerParams(vmem_limit_bytes=VMEM_LIMIT),
        cost_estimate=pl.CostEstimate(
            flops=0, bytes_accessed=8 * count * shape[0] * shape[1], transcendentals=0
        ),
        name="arrange",
    )(place, *pieces)


def partial_kernel(offsets, ratio, count, number, place, slots, ancestors, tile_ref, *refs):
    piece_refs = refs[: len(offsets)]
    out_refs = refs[len(offsets) : -2]
    right_high, right_low = refs[-2:]
    chunk_rows, columns = out_refs[0].shape
    blocks = tile_ref.shape[1] // columns
    step = pl.program_id(0)

    def listed(block):
        found = ancestors[number, 0] == block
        for i in range(1, ancestors.shape[1]):
            found = found | (ancestors[number, i] == block)
        return found

    @pl.when(step == 0)
    def _assemble():
        for ref, offset in zip(piece_refs, offsets):
            if offset is None:
                right_high[...], right_low[...] = halves(ref[...])
                continue
            unit_rows, width = ref.shape[1:]
            owner = place[0] ^ offset
            lane = pl.multiple_of(owner // ratio * width, width)
            for r in range(ref.shape[0]):
                unit = owner % ratio * count + r
                rows = pl.ds(pl.multiple_of(unit * unit_rows, unit_rows), unit_rows)
                high, low = halves(ref[r])
                right_high[rows, pl.ds(lane, width)] = high
                right_low[rows, pl.ds(lane, width)] = low

    def multiply(out_ref):
        out_ref[...] = jnp.zeros_like(out_ref)
        chunk = place[0] * count + slots[place[1], step]

        @pl.when(listed(chunk * chunk_rows // columns))
        def _chunk():
            def add(block, carry):
                @pl.when(listed(place[1] * blocks + block))
                def _block():
                    span = pl.ds(pl.multiple_of(block * columns, columns), columns)
                    high, low = halves(tile_ref[:, span])
                    right = right_high[span, :]
                    dot = functools.partial(jnp.dot, preferred_element_type=jnp.float32)
                    out_ref[...] += dot(high, right) + (
                        dot(high, right_low[span, :]) + dot(low, right)
                    )

                return carry

            lax.fori_loop(0, blocks, add, 0)

    for index, out_ref in enumerate(out_refs):
        pl.when(step == index)(functools.partial(multiply, out_ref))


def partial_product(place, slots, ancestors, tiles, pieces, offsets, ratio, columns, number):
    rows, cols = tiles.shape
    count = slots.shape[0]
    chunk = rows // count
    whole = [
        pl.BlockSpec(piece.shape, functools.partial(lambda n, i, *m: (0,) * n, piece.ndim))
        for piece in pieces
    ]
    return pl.pallas_call(
        functools.partial(partial_kernel, offsets, ratio, count, number),
        grid_spec=pltpu.PrefetchScalarGridSpec(
            num_scalar_prefetch=3,
            grid=(count,),
            in_specs=[pl.BlockSpec((chunk, cols), lambda i, p, s, a: (s[p[1], i], 0))] + whole,
            out_specs=[pl.BlockSpec((chunk, columns), lambda i, *m: (0, 0))] * count,
            scratch_shapes=[pltpu.VMEM((cols, columns), jnp.bfloat16)] * 2,
        ),
        out_shape=[jax.ShapeDtypeStruct((chunk, columns), jnp.float32)] * count,
        compiler_params=pltpu.CompilerParams(vmem_limit_bytes=VMEM_LIMIT),
        cost_estimate=pl.CostEstimate(
            flops=6 * rows * cols * columns,
            bytes_accessed=4 * (rows * cols + cols * columns + rows * columns),
            transcendentals=0,
        ),
        name="partial_product",
    )(place, slots, ancestors, tiles, *pieces)


def to_plane(place, pieces, ratio):
    received = [pieces[0]]
    for o in range(1, len(pieces)):
        received.append(flip(pieces[o], "pcol", o * ratio))
    return arrange(place, received)


def to_plane_whole(pieces, count, ratio):
    groups = [[c * ratio + k for c in range(count)] for k in range(ratio)]
    return lax.all_to_all(pieces, "pcol", 0, 0, axis_index_groups=groups)


def gather_plane(own, pcol_count):
    found = {0: own}
    for offset in range(2, pcol_count, 2):
        found[offset] = flip(own, "pcol", offset)
    for offset in range(0, pcol_count, 2):
        found[offset + 1] = flip(found[offset], "pcol", 1)
    return found


def gather_whole(own, count, ratio):
    _, unit_rows, width = own.shape
    gathered = lax.all_gather(own, "pcol", axis=0)
    split = gathered.reshape(count, ratio, count, unit_rows, width)
    rows = jnp.transpose(split, (1, 2, 3, 0, 4))
    return rows.reshape(ratio * count * unit_rows, count * width)


FOUR_SLOTS = ((3, 2, 1, 0), (2, 0, 3, 1), (1, 3, 0, 2), (0, 1, 2, 3))


def slots_of(count):
    return FOUR_SLOTS if count == len(FOUR_SLOTS) else (tuple(range(count)),) * count


def sum_over_four(slots, first):
    near = lax.ppermute(slots[0], "prow", [(0, 1), (3, 2)])
    total = lax.ppermute(slots[1], "prow", [(0, 2), (2, 3), (3, 1), (1, 0)])
    middle = lax.ppermute(slots[0], "prow", [(1, 2), (2, 1)])
    last = lax.ppermute(slots[2] + near, "prow", [(1, 3), (2, 0), (0, 1), (3, 2)])
    mine = after(slots[3], *first) if first else slots[3]
    return ((mine + total) + middle) + last


def sum_over_line(slots, z, first):
    count = len(slots)
    if count == len(FOUR_SLOTS):
        return sum_over_four(slots, first)
    chunks = jnp.stack(slots)

    def chunk(index):
        return lax.dynamic_index_in_dim(chunks, jnp.clip(index, 0, count - 1), 0, keepdims=False)

    up = down = None
    for t in range(1, count):
        up_send, down_send = chunk(z + count - t), chunk(z + t - count)
        if up is not None:
            up_send, down_send = up_send + up, down_send + down
        up = lax.ppermute(up_send, "prow", [(i, i + 1) for i in range(min(t, count - 1))])
        down = lax.ppermute(
            down_send, "prow", [(i, i - 1) for i in range(max(count - t, 1), count)]
        )
    mine = chunk(z)
    return mine if up is None else mine + up + down


def sum_plane(matrices, pcol_count, pcol_index):
    number, rows, columns = matrices.shape
    if pcol_count == 1:
        return matrices
    paired = matrices.reshape(number, pcol_count // 2, 2, rows // pcol_count, columns)
    core, chip = pcol_index % 2, pcol_index // 2
    send = lax.dynamic_index_in_dim(paired, 1 - core, 2, keepdims=False)
    mine = lax.dynamic_index_in_dim(paired, core, 2, keepdims=False) + flip(send, "pcol", 1)
    total = lax.dynamic_index_in_dim(mine, chip, 1, keepdims=False)
    for o in range(1, pcol_count // 2):
        send = lax.dynamic_index_in_dim(mine, chip ^ o, 1, keepdims=False)
        total = total + flip(send, "pcol", 2 * o)
    return total


def sum_planes(matrices, count):
    bit = 1
    while bit < count:
        matrices = matrices + flip(matrices, "prow", bit)
        bit *= 2
    return matrices


def body(inverse_tiles, factor, link_factor, diag_inverse, ancestors):
    row_count, col_count = inverse_tiles.shape
    nsuper, unit_rows, columns = factor.shape
    count = lax.axis_size("prow")
    pcol_count = lax.axis_size("pcol")
    ratio = col_count // row_count
    z = lax.axis_index("prow")
    pcol_index = lax.axis_index("pcol")
    slice_rows = columns // pcol_count
    slice_start = pcol_index * slice_rows
    width = columns // count

    place = jnp.stack([pcol_index, z, pcol_index // ratio]).astype(jnp.int32)
    slots = jnp.asarray(slots_of(count), jnp.int32)
    own_block = (pcol_index * count + z) * unit_rows // columns
    keep = jnp.any(ancestors == own_block, axis=1)[:, None, None]
    local = jnp.where(keep, factor, 0.0)

    partials = []
    received, gathered = None, None
    for number in range(nsuper):
        if width % LANES:
            pieces = jnp.swapaxes(factor[number].reshape(unit_rows, count, width), 0, 1)
            received = to_plane_whole(pieces, count, ratio)
            own = lax.all_to_all(received, "prow", 0, 0)
            pieces, offsets = [gather_whole(own, count, ratio)], [None]
        else:
            start = place if received is None else after(place, received)
            received = to_plane(place, cut(start, factor, number, count), ratio)
            own = lax.all_to_all(received, "prow", 0, 0)
            if gathered is not None:
                own = after(own, *gathered)
            found = gather_plane(own, pcol_count)
            gathered = [found[o] for o in range(2, pcol_count, 2)]
            offsets, pieces = list(found.keys()), list(found.values())
        partials.append(
            partial_product(
                place, slots, ancestors, inverse_tiles, pieces, offsets, ratio, columns, number
            )
        )

    def own_rows(matrices):
        return lax.dynamic_slice_in_dim(matrices, slice_start, slice_rows, -2)

    offdiag_list, sums, bases, ready, before = [], [], [], [], []
    for number in range(nsuper):
        summed = sum_over_line(partials[number], z, before)
        part = product(local[number].T, summed)
        if number == 0:
            result = -jnp.where(keep[number], summed, 0.0)
            base = diag_inverse[0]
        else:
            result = -jnp.where(keep[number], summed + link_rows, 0.0)
            part = part + rest
            base = diag_inverse[number] + product(link_block.T, base_link)
        offdiag_list.append(result)
        ready.append(part)
        bases.append(own_rows(base))
        if number + 1 < nsuper:
            link_block = link_factor[number]
            cross_part = product(result.T, local[number + 1])
            link_part = cross_part + product(part, link_block)
            rest = product(cross_part.T, link_block) + product(link_block.T, link_part)
            base_link = product(base, link_block)
            link_rows = product(result, link_block)
            bases.append(own_rows(base_link))
            ready.append(link_part)
            group = sum_plane(jnp.stack(ready), pcol_count, pcol_index)
            before = [group, rest, link_rows]
            sums.append(sum_planes(group, count))
            ready = []
    sums.append(sum_planes(sum_plane(jnp.stack(ready), pcol_count, pcol_index), count))
    totals = jnp.concatenate(sums) + jnp.stack(bases)
    return (jnp.stack(offdiag_list), totals[0::2], -totals[1::2])


def solution(mesh):
    in_specs = (P("pcol", "prow"), P(None, ("pcol", "prow"), None), P(), P(), P())
    out_specs = (P(None, ("pcol", "prow"), None), P(None, "pcol", None), P(None, "pcol", None))
    return jax.shard_map(body, mesh=mesh, in_specs=in_specs, out_specs=out_specs, check_vma=False)
```

```python
import functools

import jax
import jax.numpy as jnp
from jax import lax
from jax.experimental import pallas as pl
from jax.experimental.pallas import tpu as pltpu
from jax.sharding import PartitionSpec as P

BOTH = ("prow", "pcol")
VMEM_LIMIT = 28 * 1024 * 1024
LANES = 128


def product(left_part, right_part):
    return jnp.dot(
        left_part, right_part, precision=lax.Precision.HIGH, preferred_element_type=jnp.float32
    )


def halves(value):
    high = value.astype(jnp.bfloat16)
    low = (value - high.astype(jnp.float32)).astype(jnp.bfloat16)
    return high, low


def flip(value, axis, bit):
    return lax.ppermute(value, axis, [(i, i ^ bit) for i in range(lax.axis_size(axis))])


def run(kernel, scalars, arrays, specs, waits, outs, out_specs, grid=(1,), scratch=(), name=None):
    def corner(array):
        block = (1,) * (array.ndim - 2) + (8, LANES)
        return pl.BlockSpec(block, lambda *_: (0,) * array.ndim)

    def body(*refs):
        first = len(scalars) + len(arrays)
        kernel(*refs[:first], *refs[first + len(waits) :])

    return pl.pallas_call(
        body,
        grid_spec=pltpu.PrefetchScalarGridSpec(
            num_scalar_prefetch=len(scalars),
            grid=grid,
            in_specs=list(specs) + [corner(array) for array in waits],
            out_specs=out_specs,
            scratch_shapes=list(scratch),
        ),
        out_shape=outs,
        compiler_params=pltpu.CompilerParams(vmem_limit_bytes=VMEM_LIMIT),
        cost_estimate=pl.CostEstimate(flops=0, bytes_accessed=0, transcendentals=0),
        name=name,
    )(*scalars, *arrays, *waits)


def whole(array):
    return pl.BlockSpec(array.shape, lambda *_: (0,) * array.ndim)


def cut_kernel(place, factor_ref, *out_refs):
    width = out_refs[0].shape[1]
    for o, out_ref in enumerate(out_refs):
        start = pl.multiple_of((place[2] ^ o) * width, width)
        out_ref[...] = factor_ref[0, :, pl.ds(start, width)]


def cut(place, factor, number, count, waits):
    _, unit_rows, columns = factor.shape
    piece = jax.ShapeDtypeStruct((unit_rows, columns // count), factor.dtype)
    spec = pl.BlockSpec((1, unit_rows, columns), lambda *_: (number, 0, 0))
    return run(
        cut_kernel, [place], [factor], [spec], waits, [piece] * count, [whole(piece)] * count,
        name="cut",
    )


def turn_kernel(place, *refs):
    count = len(refs) // 2
    for shift in range(count):

        @pl.when((place[1] ^ place[2]) == shift)
        def _copy(shift=shift):
            for o in range(count):
                refs[count + o][...] = refs[o ^ shift][...]


def turn(place, pieces):
    count = len(pieces)
    piece = jax.ShapeDtypeStruct(pieces[0].shape, pieces[0].dtype)
    specs = [whole(piece)] * count
    return run(turn_kernel, [place], pieces, specs, [], [piece] * count, specs, name="turn")


def arrange_kernel(place, *refs):
    out_ref = refs[-1]
    for o, piece_ref in enumerate(refs[:-1]):
        out_ref[place[1] ^ o] = piece_ref[...]


def arrange(place, pieces, waits):
    out = jax.ShapeDtypeStruct((len(pieces),) + pieces[0].shape, pieces[0].dtype)
    specs = [whole(piece) for piece in pieces]
    return run(arrange_kernel, [place], pieces, specs, waits, out, whole(out), name="arrange")


def add_kernel(*refs):
    total = refs[0][...]
    for ref in refs[1:-1]:
        total = total + ref[...]
    refs[-1][...] = total


def add_up(arrays, waits):
    out = jax.ShapeDtypeStruct(arrays[0].shape, arrays[0].dtype)
    specs = [whole(array) for array in arrays]
    return run(add_kernel, [], arrays, specs, waits, out, whole(out), name="add_up")


def partial_kernel(ratio, count, number, place, slots, ancestors, tile_ref, right_ref, *refs):
    out_refs, (right_high, right_low) = refs[:-2], refs[-2:]
    chunk_rows, columns = out_refs[0].shape
    blocks = tile_ref.shape[1] // columns
    step = pl.program_id(0)

    def listed(block):
        found = ancestors[number, 0] == block
        for i in range(1, ancestors.shape[1]):
            found = found | (ancestors[number, i] == block)
        return found

    @pl.when(step == 0)
    def _assemble():
        if len(right_ref.shape) == 2:
            right_high[...], right_low[...] = halves(right_ref[...])
            return
        _, _, unit_rows, width = right_ref.shape
        for owner in range(right_ref.shape[0]):
            lanes = pl.ds(owner // ratio * width, width)
            rows = pl.ds(owner % ratio * count * unit_rows, count * unit_rows)
            high, low = halves(right_ref[owner].reshape(count * unit_rows, width))
            right_high[rows, lanes] = high
            right_low[rows, lanes] = low

    def multiply(out_ref):
        out_ref[...] = jnp.zeros_like(out_ref)
        chunk = place[0] * count + slots[place[1], step]

        @pl.when(listed(chunk * chunk_rows // columns))
        def _chunk():
            def add(block, carry):
                @pl.when(listed(place[1] * blocks + block))
                def _block():
                    span = pl.ds(pl.multiple_of(block * columns, columns), columns)
                    high, low = halves(tile_ref[:, span])
                    right = right_high[span, :]
                    dot = functools.partial(jnp.dot, preferred_element_type=jnp.float32)
                    out_ref[...] += dot(high, right) + (
                        dot(high, right_low[span, :]) + dot(low, right)
                    )

                return carry

            lax.fori_loop(0, blocks, add, 0)

    for index, out_ref in enumerate(out_refs):
        pl.when(step == index)(functools.partial(multiply, out_ref))


def partial_product(place, slots, ancestors, tiles, right, ratio, columns, number):
    rows, cols = tiles.shape
    count = slots.shape[0]
    out = jax.ShapeDtypeStruct((rows // count, columns), jnp.float32)
    tile = pl.BlockSpec((rows // count, cols), lambda i, p, s, a: (s[p[1], i], 0))
    return run(
        functools.partial(partial_kernel, ratio, count, number),
        [place, slots, ancestors],
        [tiles, right],
        [tile, whole(right)],
        [],
        [out] * count,
        [whole(out)] * count,
        grid=(count,),
        scratch=[pltpu.VMEM((cols, columns), jnp.bfloat16)] * 2,
        name="partial_product",
    )


def to_column(pieces, ratio):
    return [pieces[0]] + [flip(pieces[o], "pcol", o * ratio) for o in range(1, len(pieces))]


def to_plane(pieces):
    return [pieces[0]] + [flip(pieces[o], "prow", o) for o in range(1, len(pieces))]


def to_plane_whole(factor, count, ratio):
    pieces = jnp.swapaxes(factor.reshape(factor.shape[0], count, -1), 0, 1)
    groups = [[c * ratio + k for c in range(count)] for k in range(ratio)]
    spread = lax.all_to_all(pieces, "pcol", 0, 0, axis_index_groups=groups)
    return lax.all_to_all(spread, "prow", 0, 0)


def in_rows(gathered, count, ratio):
    _, _, unit_rows, width = gathered.shape
    split = gathered.reshape(count, ratio, count, unit_rows, width)
    rows = jnp.transpose(split, (1, 2, 3, 0, 4))
    return rows.reshape(ratio * count * unit_rows, count * width)


FOUR_SLOTS = ((3, 2, 1, 0), (2, 0, 3, 1), (1, 3, 0, 2), (0, 1, 2, 3))


def slots_of(count):
    return FOUR_SLOTS if count == len(FOUR_SLOTS) else (tuple(range(count)),) * count


def sum_over_four(slots, first):
    near = lax.ppermute(slots[0], "prow", [(0, 1), (3, 2)])
    total = lax.ppermute(slots[1], "prow", [(0, 2), (2, 3), (3, 1), (1, 0)])
    middle = lax.ppermute(slots[0], "prow", [(1, 2), (2, 1)])
    last = lax.ppermute(slots[2] + near, "prow", [(1, 3), (2, 0), (0, 1), (3, 2)])
    return add_up([slots[3], total, middle, last], first)


def sum_over_line(slots, z, first):
    count = len(slots)
    if count == len(FOUR_SLOTS):
        return sum_over_four(slots, first)
    chunks = jnp.stack(slots)

    def chunk(index):
        return lax.dynamic_index_in_dim(chunks, jnp.clip(index, 0, count - 1), 0, keepdims=False)

    up = down = None
    for t in range(1, count):
        up_send, down_send = chunk(z + count - t), chunk(z + t - count)
        if up is not None:
            up_send, down_send = up_send + up, down_send + down
        up = lax.ppermute(up_send, "prow", [(i, i + 1) for i in range(min(t, count - 1))])
        down = lax.ppermute(
            down_send, "prow", [(i, i - 1) for i in range(max(count - t, 1), count)]
        )
    mine = chunk(z)
    return mine if up is None else mine + up + down


def sum_plane(matrices, pcol_count, pcol_index):
    number, rows, columns = matrices.shape
    if pcol_count == 1:
        return matrices
    paired = matrices.reshape(number, pcol_count // 2, 2, rows // pcol_count, columns)
    core, chip = pcol_index % 2, pcol_index // 2
    send = lax.dynamic_index_in_dim(paired, 1 - core, 2, keepdims=False)
    mine = lax.dynamic_index_in_dim(paired, core, 2, keepdims=False) + flip(send, "pcol", 1)
    total = lax.dynamic_index_in_dim(mine, chip, 1, keepdims=False)
    for o in range(1, pcol_count // 2):
        send = lax.dynamic_index_in_dim(mine, chip ^ o, 1, keepdims=False)
        total = total + flip(send, "pcol", 2 * o)
    return total


def sum_planes(matrices, count):
    bit = 1
    while bit < count:
        matrices = matrices + flip(matrices, "prow", bit)
        bit *= 2
    return matrices


def body(inverse_tiles, factor, link_factor, diag_inverse, ancestors):
    row_count, col_count = inverse_tiles.shape
    nsuper, unit_rows, columns = factor.shape
    count = lax.axis_size("prow")
    pcol_count = lax.axis_size("pcol")
    ratio = col_count // row_count
    z = lax.axis_index("prow")
    pcol_index = lax.axis_index("pcol")
    slice_rows = columns // pcol_count
    slice_start = pcol_index * slice_rows
    width = columns // count

    place = jnp.stack([pcol_index, z, pcol_index // ratio]).astype(jnp.int32)
    slots = jnp.asarray(slots_of(count), jnp.int32)
    own_block = (pcol_index * count + z) * unit_rows // columns
    keep = jnp.any(ancestors == own_block, axis=1)[:, None, None]
    local = jnp.where(keep, factor, 0.0)

    partials = []
    moved, gathered = [], []
    for number in range(nsuper):
        if width % LANES:
            own = to_plane_whole(factor[number], count, ratio)
            right = in_rows(lax.all_gather(own, "pcol", axis=0), count, ratio)
        else:
            sent = to_column(cut(place, factor, number, count, moved), ratio)
            moved = sent[1:]
            own = arrange(place, to_plane(turn(place, sent)), gathered)
            right = lax.all_gather(own, "pcol", axis=0)
            gathered = [right]
        partials.append(
            partial_product(
                place, slots, ancestors, inverse_tiles, right, ratio, columns, number
            )
        )

    def own_rows(matrices):
        return lax.dynamic_slice_in_dim(matrices, slice_start, slice_rows, -2)

    offdiag_list, sums, bases, ready, before = [], [], [], [], []
    for number in range(nsuper):
        before = before + [later[0] for later in partials[number + 1 : number + 2]]
        summed = sum_over_line(partials[number], z, before)
        part = product(local[number].T, summed)
        if number == 0:
            result = -jnp.where(keep[number], summed, 0.0)
            base = diag_inverse[0]
        else:
            result = -jnp.where(keep[number], summed + link_rows, 0.0)
            part = part + rest
            base = diag_inverse[number] + product(link_block.T, base_link)
        offdiag_list.append(result)
        ready.append(part)
        bases.append(own_rows(base))
        if number + 1 < nsuper:
            link_block = link_factor[number]
            cross_part = product(result.T, local[number + 1])
            link_part = cross_part + product(part, link_block)
            rest = product(cross_part.T, link_block) + product(link_block.T, link_part)
            base_link = product(base, link_block)
            link_rows = product(result, link_block)
            bases.append(own_rows(base_link))
            ready.append(link_part)
            group = sum_plane(jnp.stack(ready), pcol_count, pcol_index)
            before = [group, rest, link_rows]
            sums.append(sum_planes(group, count))
            ready = []
    sums.append(sum_planes(sum_plane(jnp.stack(ready), pcol_count, pcol_index), count))
    totals = jnp.concatenate(sums) + jnp.stack(bases)
    return (jnp.stack(offdiag_list), totals[0::2], -totals[1::2])


def solution(mesh):
    in_specs = (P("pcol", "prow"), P(None, ("pcol", "prow"), None), P(), P(), P())
    out_specs = (P(None, ("pcol", "prow"), None), P(None, "pcol", None), P(None, "pcol", None))
    return jax.shard_map(body, mesh=mesh, in_specs=in_specs, out_specs=out_specs, check_vma=False)
```

```python
import functools

import jax
import jax.numpy as jnp
from jax import lax
from jax.experimental import pallas as pl
from jax.experimental.pallas import tpu as pltpu
from jax.sharding import PartitionSpec as P

BOTH = ("prow", "pcol")
VMEM_LIMIT = 28 * 1024 * 1024
LANES = 128


def halves(value):
    high = value.astype(jnp.bfloat16)
    low = (value - high.astype(jnp.float32)).astype(jnp.bfloat16)
    return high, low


def flip(value, axis, bit):
    return lax.ppermute(value, axis, [(i, i ^ bit) for i in range(lax.axis_size(axis))])


def run(
    kernel, scalars, arrays, specs, waits, outs, out_specs, grid=(1,), scratch=(), alias=None, name=None
):
    def corner(array):
        block = (1,) * (array.ndim - 2) + (8, LANES)
        return pl.BlockSpec(block, lambda *_: (0,) * array.ndim)

    def body(*refs):
        first = len(scalars) + len(arrays)
        kernel(*refs[:first], *refs[first + len(waits) :])

    return pl.pallas_call(
        body,
        grid_spec=pltpu.PrefetchScalarGridSpec(
            num_scalar_prefetch=len(scalars),
            grid=grid,
            in_specs=list(specs) + [corner(array) for array in waits],
            out_specs=out_specs,
            scratch_shapes=list(scratch),
        ),
        out_shape=outs,
        input_output_aliases=alias or {},
        compiler_params=pltpu.CompilerParams(vmem_limit_bytes=VMEM_LIMIT),
        cost_estimate=pl.CostEstimate(flops=0, bytes_accessed=0, transcendentals=0),
        name=name,
    )(*scalars, *arrays, *waits)


def whole(array):
    return pl.BlockSpec(array.shape, lambda *_: (0,) * array.ndim)


def cut_kernel(place, factor_ref, *out_refs):
    width = out_refs[0].shape[1]
    for o, out_ref in enumerate(out_refs):
        start = pl.multiple_of((place[2] ^ o) * width, width)
        out_ref[...] = factor_ref[0, :, pl.ds(start, width)]


def cut(place, factor, number, count, waits):
    _, unit_rows, columns = factor.shape
    piece = jax.ShapeDtypeStruct((unit_rows, columns // count), factor.dtype)
    spec = pl.BlockSpec((1, unit_rows, columns), lambda *_: (number, 0, 0))
    return run(
        cut_kernel, [place], [factor], [spec], waits, [piece] * count, [whole(piece)] * count,
        name="cut",
    )


def turn_kernel(place, *refs):
    count = len(refs) // 2
    for shift in range(count):

        @pl.when((place[1] ^ place[2]) == shift)
        def _copy(shift=shift):
            for o in range(count):
                refs[count + o][...] = refs[o ^ shift][...]


def turn(place, pieces):
    count = len(pieces)
    piece = jax.ShapeDtypeStruct(pieces[0].shape, pieces[0].dtype)
    specs = [whole(piece)] * count
    return run(turn_kernel, [place], pieces, specs, [], [piece] * count, specs, name="turn")


def arrange_kernel(place, *refs):
    out_ref = refs[-1]
    for o, piece_ref in enumerate(refs[:-1]):
        out_ref[place[1] ^ o] = piece_ref[...]


def arrange(place, pieces, waits):
    out = jax.ShapeDtypeStruct((len(pieces),) + pieces[0].shape, pieces[0].dtype)
    specs = [whole(piece) for piece in pieces]
    return run(arrange_kernel, [place], pieces, specs, waits, out, whole(out), name="arrange")


def add_kernel(*refs):
    total = refs[0][...]
    for ref in refs[1:-1]:
        total = total + ref[...]
    refs[-1][...] = total


def add_up(arrays, waits):
    out = jax.ShapeDtypeStruct(arrays[0].shape, arrays[0].dtype)
    specs = [whole(array) for array in arrays]
    return run(add_kernel, [], arrays, specs, waits, out, whole(out), name="add_up")


def is_listed(ancestors, number, block):
    found = ancestors[number, 0] == block
    for i in range(1, ancestors.shape[1]):
        found = found | (ancestors[number, i] == block)
    return found


def partial_kernel(offsets, ratio, count, number, place, slots, ancestors, tile_ref, *refs):
    piece_refs = refs[: len(offsets)]
    out_refs = refs[len(offsets) : -2]
    right_high, right_low = refs[-2:]
    chunk_rows, columns = out_refs[0].shape
    blocks = tile_ref.shape[1] // columns
    step = pl.program_id(0)

    def listed(block):
        return is_listed(ancestors, number, block)

    @pl.when(step == 0)
    def _assemble():
        for ref, offset in zip(piece_refs, offsets):
            if offset is None:
                right_high[...], right_low[...] = halves(ref[...])
                continue
            parts, unit_rows, width = ref.shape
            owner = place[0] ^ offset
            lanes = pl.ds(pl.multiple_of(owner // ratio * width, width), width)
            first = owner % ratio * (parts * unit_rows)
            rows = pl.ds(pl.multiple_of(first, parts * unit_rows), parts * unit_rows)
            high, low = halves(ref[...].reshape(parts * unit_rows, width))
            right_high[rows, lanes] = high
            right_low[rows, lanes] = low

    def multiply(out_ref):
        out_ref[...] = jnp.zeros_like(out_ref)
        chunk = place[0] * count + slots[place[1], step]

        @pl.when(listed(chunk * chunk_rows // columns))
        def _chunk():
            def add(block, carry):
                @pl.when(listed(place[1] * blocks + block))
                def _block():
                    span = pl.ds(pl.multiple_of(block * columns, columns), columns)
                    high, low = halves(tile_ref[:, span])
                    right = right_high[span, :]
                    dot = functools.partial(jnp.dot, preferred_element_type=jnp.float32)
                    out_ref[...] += dot(high, right) + (
                        dot(high, right_low[span, :]) + dot(low, right)
                    )

                return carry

            lax.fori_loop(0, blocks, add, 0)

    for index, out_ref in enumerate(out_refs):
        pl.when(step == index)(functools.partial(multiply, out_ref))


def partial_product(place, slots, ancestors, tiles, pieces, offsets, ratio, columns, number, waits):
    rows, cols = tiles.shape
    count = slots.shape[0]
    out = jax.ShapeDtypeStruct((rows // count, columns), jnp.float32)
    tile = pl.BlockSpec((rows // count, cols), lambda i, p, s, a: (s[p[1], i], 0))
    return run(
        functools.partial(partial_kernel, offsets, ratio, count, number),
        [place, slots, ancestors],
        [tiles] + pieces,
        [tile] + [whole(piece) for piece in pieces],
        waits,
        [out] * count,
        [whole(out)] * count,
        grid=(count,),
        scratch=[pltpu.VMEM((cols, columns), jnp.bfloat16)] * 2,
        name="partial_product",
    )


def dot(left, right, side=1):
    def one(a, b):
        return lax.dot_general(
            a, b, (((side,), (0,)), ((), ())), preferred_element_type=jnp.float32
        )

    left_high, left_low = halves(left)
    right_high, right_low = halves(right)
    return one(left_high, right_high) + (one(left_high, right_low) + one(left_low, right_high))


def part_by_core(place, matrix_ref, index, keep_ref, send_ref):
    _, chips, rows, _ = keep_ref.shape
    core = place[0] % 2
    for chip in range(chips):
        for ref, side in ((keep_ref, core), (send_ref, 1 - core)):
            first = pl.multiple_of((chip * 2 + side) * rows, rows)
            ref[index, chip] = matrix_ref[pl.ds(first, rows), :]


def finish_kernel(number, last, first, block, place, ancestors, *refs):
    refs = list(refs)
    sums, factor_ref = [refs.pop(0) for _ in range(4)], refs.pop(0)
    if not first:
        old_rest, old_rows, _ = (refs.pop(0) for _ in range(3))
    if not last:
        link_ref, next_ref = refs.pop(0), refs.pop(0)
    offdiag_ref, keep_ref, send_ref = (refs.pop(0) for _ in range(3))
    if not last:
        rest_ref, rows_ref = refs.pop(0), refs.pop(0)
    part_ref = refs.pop(0)
    offdiag_ref[...] = jnp.zeros_like(offdiag_ref)
    part_ref[...] = jnp.zeros_like(part_ref) if first else old_rest[...]

    own = block(place)

    @pl.when(is_listed(ancestors, number, own))
    def _own():
        summed = ((sums[0][...] + sums[1][...]) + sums[2][...]) + sums[3][...]
        part_ref[...] += dot(factor_ref[0], summed, 0)
        offdiag_ref[0] = -(summed if first else summed + old_rows[...])

    part_by_core(place, part_ref, 0, keep_ref, send_ref)
    if last:
        return
    link = link_ref[0]
    rest_ref[...] = jnp.zeros_like(rest_ref)
    rows_ref[...] = dot(offdiag_ref[0], link)

    @pl.when(is_listed(ancestors, number + 1, own))
    def _cross():
        rest_ref[...] = dot(offdiag_ref[0], next_ref[0], 0)

    cross = rest_ref[...]
    part_ref[...] = cross + dot(part_ref[...], link)
    part_by_core(place, part_ref, 1, keep_ref, send_ref)
    rest_ref[...] = dot(cross, link, 0) + dot(link, part_ref[...], 0)


def finish(number, block, place, ancestors, sums, factor, before, link_factor, chips, waits):
    nsuper, unit_rows, columns = factor.shape
    first, last = number == 0, number + 1 == nsuper
    slab = (1, unit_rows, columns)
    arrays, specs = list(sums), [whole(array) for array in sums]
    arrays.append(factor)
    specs.append(pl.BlockSpec(slab, lambda *_: (number, 0, 0)))
    alias = {}
    if not first:
        alias = {2 + len(arrays) + 2: 0}
        arrays += before
        specs += [whole(before[0]), whole(before[1])]
        specs.append(pl.BlockSpec((1, 8, LANES), lambda *_: (0, 0, 0)))
    if not last:
        arrays += [link_factor, factor]
        specs.append(pl.BlockSpec((1, columns, columns), lambda *_: (number, 0, 0)))
        specs.append(pl.BlockSpec(slab, lambda *_: (number + 1, 0, 0)))
    shape = jax.ShapeDtypeStruct
    groups = shape((1 if last else 2, chips, columns // (2 * chips), columns), jnp.float32)
    outs = [shape(factor.shape, jnp.float32), groups, groups]
    out_specs = [pl.BlockSpec(slab, lambda *_: (number, 0, 0)), whole(groups), whole(groups)]
    if not last:
        more = [shape((columns, columns), jnp.float32), shape((unit_rows, columns), jnp.float32)]
        outs += more
        out_specs += [whole(array) for array in more]
    return run(
        functools.partial(finish_kernel, number, last, first, block),
        [place, ancestors],
        arrays,
        specs,
        waits,
        outs,
        out_specs,
        scratch=[pltpu.VMEM((columns, columns), jnp.float32)],
        alias=alias,
        name="finish",
    )


def fold_kernel(place, keep_ref, received_ref, *out_refs):
    chip = place[0] // 2
    for o, out_ref in enumerate(out_refs):
        out_ref[...] = keep_ref[:, chip ^ o] + received_ref[:, chip ^ o]


def fold(place, keep, received):
    number, chips, rows, columns = keep.shape
    out = jax.ShapeDtypeStruct((number, rows, columns), jnp.float32)
    specs = [whole(keep)] * 2
    outs = [out] * chips
    return run(
        fold_kernel, [place], [keep, received], specs, [], outs, [whole(out)] * chips, name="fold"
    )


def bases_kernel(nsuper, place, diag_ref, link_ref, *refs):
    diag_out, link_out, base_ref, next_ref = refs
    rows = diag_out.shape[1]
    mine = pl.ds(pl.multiple_of(place[0] * rows, rows), rows)
    base_ref[...] = diag_ref[0]
    diag_out[0] = base_ref[mine, :]
    for number in range(1, nsuper):
        link = link_ref[number - 1]
        next_ref[...] = dot(base_ref[...], link)
        link_out[number - 1] = next_ref[mine, :]
        base_ref[...] = diag_ref[number] + dot(link, next_ref[...], 0)
        diag_out[number] = base_ref[mine, :]


def bases_of(place, diag_inverse, link_factor, rows, waits):
    nsuper, columns, _ = diag_inverse.shape
    outs = [
        jax.ShapeDtypeStruct((nsuper, rows, columns), jnp.float32),
        jax.ShapeDtypeStruct((nsuper - 1, rows, columns), jnp.float32),
    ]
    return run(
        functools.partial(bases_kernel, nsuper),
        [place],
        [diag_inverse, link_factor],
        [whole(diag_inverse), whole(link_factor)],
        waits,
        outs,
        [whole(out) for out in outs],
        scratch=[pltpu.VMEM((columns, columns), jnp.float32)] * 2,
        name="bases",
    )


def outputs_kernel(*refs):
    diag_base, link_base, *sums, diag_out, link_out = refs
    at = 0
    for left, right in zip(sums[::2], sums[1::2]):
        for index in range(left.shape[0]):
            total = left[index] + right[index]
            if at % 2 == 0:
                diag_out[at // 2] = total + diag_base[at // 2]
            else:
                link_out[at // 2] = -(total + link_base[at // 2])
            at += 1


def outputs(bases, sums):
    arrays = list(bases) + sums
    specs = [whole(array) for array in arrays]
    outs = [jax.ShapeDtypeStruct(base.shape, jnp.float32) for base in bases]
    return run(outputs_kernel, [], arrays, specs, [], outs, specs[:2], name="outputs")


def to_column(pieces, ratio):
    return [pieces[0]] + [flip(pieces[o], "pcol", o * ratio) for o in range(1, len(pieces))]


def to_plane(pieces):
    return [pieces[0]] + [flip(pieces[o], "prow", o) for o in range(1, len(pieces))]


def to_plane_whole(factor, count, ratio):
    pieces = jnp.swapaxes(factor.reshape(factor.shape[0], count, -1), 0, 1)
    groups = [[c * ratio + k for c in range(count)] for k in range(ratio)]
    spread = lax.all_to_all(pieces, "pcol", 0, 0, axis_index_groups=groups)
    return lax.all_to_all(spread, "prow", 0, 0)


def gather_plane(own, pcol_count):
    found = {0: own}
    for offset in range(2, pcol_count, 2):
        found[offset] = flip(own, "pcol", offset)
    for offset in range(0, pcol_count, 2):
        found[offset + 1] = flip(found[offset], "pcol", 1)
    return found


def in_rows(gathered, count, ratio):
    _, _, unit_rows, width = gathered.shape
    split = gathered.reshape(count, ratio, count, unit_rows, width)
    rows = jnp.transpose(split, (1, 2, 3, 0, 4))
    return rows.reshape(ratio * count * unit_rows, count * width)


FOUR_SLOTS = ((3, 2, 1, 0), (2, 0, 3, 1), (1, 3, 0, 2), (0, 1, 2, 3))


def slots_of(count):
    return FOUR_SLOTS if count == len(FOUR_SLOTS) else (tuple(range(count)),) * count


def sum_over_four(slots):
    near = lax.ppermute(slots[0], "prow", [(0, 1), (3, 2)])
    total = lax.ppermute(slots[1], "prow", [(0, 2), (2, 3), (3, 1), (1, 0)])
    middle = lax.ppermute(slots[0], "prow", [(1, 2), (2, 1)])
    both = add_up([slots[2], near], [])
    last = lax.ppermute(both, "prow", [(1, 3), (2, 0), (0, 1), (3, 2)])
    return [slots[3], total, middle, last]


def sum_over_line(slots, z):
    count = len(slots)
    if count == len(FOUR_SLOTS):
        return sum_over_four(slots)
    chunks = jnp.stack(slots)

    def chunk(index):
        return lax.dynamic_index_in_dim(chunks, jnp.clip(index, 0, count - 1), 0, keepdims=False)

    up = down = None
    for t in range(1, count):
        up_send, down_send = chunk(z + count - t), chunk(z + t - count)
        if up is not None:
            up_send, down_send = up_send + up, down_send + down
        up = lax.ppermute(up_send, "prow", [(i, i + 1) for i in range(min(t, count - 1))])
        down = lax.ppermute(
            down_send, "prow", [(i, i - 1) for i in range(max(count - t, 1), count)]
        )
    mine = chunk(z)
    none = jnp.zeros_like(mine)
    return [mine, none if up is None else up, none if down is None else down, none]


def sum_plane(place, keep, send):
    pieces = fold(place, keep, flip(send, "pcol", 1))
    return [pieces[0]] + [flip(pieces[o], "pcol", 2 * o) for o in range(1, len(pieces))]


def sum_planes(pieces, count, waits):
    bit = 1
    while True:
        total = add_up(pieces, waits)
        if bit >= count:
            return [total, jnp.zeros_like(total)]
        pieces, waits = [total, flip(total, "prow", bit)], []
        bit *= 2
        if bit >= count:
            return pieces


def body(inverse_tiles, factor, link_factor, diag_inverse, ancestors):
    row_count, col_count = inverse_tiles.shape
    nsuper, unit_rows, columns = factor.shape
    count = lax.axis_size("prow")
    pcol_count = lax.axis_size("pcol")
    ratio = col_count // row_count
    z = lax.axis_index("prow")
    pcol_index = lax.axis_index("pcol")
    width = columns // count
    place = jnp.stack([pcol_index, z, pcol_index // ratio]).astype(jnp.int32)
    slots = jnp.asarray(slots_of(count), jnp.int32)

    def own_block(place):
        return (place[0] * count + place[1]) * unit_rows // columns

    firsts = []
    moved, gathered = [], []
    for number in range(nsuper):
        if width % LANES:
            own = to_plane_whole(factor[number], count, ratio)
            right = in_rows(lax.all_gather(own, "pcol", axis=0), count, ratio)
            firsts.append((own, [None], [right]))
        else:
            sent = to_column(cut(place, factor, number, count, moved), ratio)
            moved = sent[1:]
            own = arrange(place, to_plane(turn(place, sent)), gathered)
            found = gather_plane(own, pcol_count)
            gathered = [found[o] for o in range(2, pcol_count, 2)]
            firsts.append((own, list(found.keys()), list(found.values())))
    bases = bases_of(place, diag_inverse, link_factor, columns // pcol_count, [firsts[0][0]])
    partials = []
    for number, (_, offsets, pieces) in enumerate(firsts):
        waits = [later[0] for later in firsts[number + 1 : number + 2]] + [bases[0]]
        partials.append(
            partial_product(
                place, slots, ancestors, inverse_tiles, pieces, offsets, ratio, columns, number,
                waits,
            )
        )

    sums, before, pending = [], [], None
    for number in range(nsuper):
        waits = [later[0] for later in partials[number + 1 : number + 2]]
        rows = sum_over_line(partials[number], z)
        offdiag, keep, send, *link = finish(
            number, own_block, place, ancestors, rows, factor, before, link_factor,
            pcol_count // 2, waits + (pending[1:] if pending else []),
        )
        if pending:
            sums += sum_planes(pending, count, [keep])
        before = link + [offdiag]
        pending = sum_plane(place, keep, send)
    sums += sum_planes(pending, count, [])
    return (offdiag, *outputs(bases, sums))


def solution(mesh):
    in_specs = (P("pcol", "prow"), P(None, ("pcol", "prow"), None), P(), P(), P())
    out_specs = (P(None, ("pcol", "prow"), None), P(None, "pcol", None), P(None, "pcol", None))
    return jax.shard_map(body, mesh=mesh, in_specs=in_specs, out_specs=out_specs, check_vma=False)
```

```python
import functools

import jax
import jax.numpy as jnp
from jax import lax
from jax.experimental import pallas as pl
from jax.experimental.pallas import tpu as pltpu
from jax.sharding import PartitionSpec as P

BOTH = ("prow", "pcol")
VMEM_LIMIT = 28 * 1024 * 1024
LANES = 128


def halves(value):
    high = value.astype(jnp.bfloat16)
    low = (value - high.astype(jnp.float32)).astype(jnp.bfloat16)
    return high, low


def flip(value, axis, bit):
    return lax.ppermute(value, axis, [(i, i ^ bit) for i in range(lax.axis_size(axis))])


def run(
    kernel, scalars, arrays, specs, waits, outs, out_specs, grid=(1,), scratch=(), alias=None, name=None
):
    def corner(array):
        block = (1,) * (array.ndim - 2) + (8, LANES)
        return pl.BlockSpec(block, lambda *_: (0,) * array.ndim)

    def body(*refs):
        first = len(scalars) + len(arrays)
        kernel(*refs[:first], *refs[first + len(waits) :])

    return pl.pallas_call(
        body,
        grid_spec=pltpu.PrefetchScalarGridSpec(
            num_scalar_prefetch=len(scalars),
            grid=grid,
            in_specs=list(specs) + [corner(array) for array in waits],
            out_specs=out_specs,
            scratch_shapes=list(scratch),
        ),
        out_shape=outs,
        input_output_aliases=alias or {},
        compiler_params=pltpu.CompilerParams(vmem_limit_bytes=VMEM_LIMIT),
        cost_estimate=pl.CostEstimate(flops=0, bytes_accessed=0, transcendentals=0),
        name=name,
    )(*scalars, *arrays, *waits)


def whole(array):
    return pl.BlockSpec(array.shape, lambda *_: (0,) * array.ndim)


def cut_kernel(place, factor_ref, *out_refs):
    width = out_refs[0].shape[2]
    for o, out_ref in enumerate(out_refs):
        start = pl.multiple_of((place[2] ^ o) * width, width)
        out_ref[...] = factor_ref[:, :, pl.ds(start, width)]


def cut(place, factor, count):
    nsuper, unit_rows, columns = factor.shape
    piece = jax.ShapeDtypeStruct((nsuper, unit_rows, columns // count), factor.dtype)
    outs = [piece] * count
    specs = [whole(piece)] * count
    return run(cut_kernel, [place], [factor], [whole(factor)], [], outs, specs, name="cut")


def turn_kernel(place, *refs):
    count = len(refs) // 2
    for shift in range(count):

        @pl.when((place[1] ^ place[2]) == shift)
        def _copy(shift=shift):
            for o in range(count):
                refs[count + o][...] = refs[o ^ shift][0]


def turn(place, pieces, number, waits):
    count = len(pieces)
    _, unit_rows, width = pieces[0].shape
    piece = jax.ShapeDtypeStruct((unit_rows, width), pieces[0].dtype)
    spec = pl.BlockSpec((1, unit_rows, width), lambda *_: (number, 0, 0))
    return run(
        turn_kernel, [place], pieces, [spec] * count, waits, [piece] * count,
        [whole(piece)] * count, name="turn",
    )


def arrange_kernel(place, *refs):
    out_ref = refs[-1]
    for o, piece_ref in enumerate(refs[:-1]):
        out_ref[place[1] ^ o] = piece_ref[...]


def arrange(place, pieces, waits):
    out = jax.ShapeDtypeStruct((len(pieces),) + pieces[0].shape, pieces[0].dtype)
    specs = [whole(piece) for piece in pieces]
    return run(arrange_kernel, [place], pieces, specs, waits, out, whole(out), name="arrange")


def pack_kernel(*refs):
    for index, ref in enumerate(refs[:-1]):
        refs[-1][index] = ref[...]


def pack(pieces, waits):
    out = jax.ShapeDtypeStruct((len(pieces),) + pieces[0].shape, pieces[0].dtype)
    specs = [whole(piece) for piece in pieces]
    return run(pack_kernel, [], pieces, specs, waits, out, whole(out), name="pack")


def add_kernel(*refs):
    total = refs[0][...]
    for ref in refs[1:-1]:
        total = total + ref[...]
    refs[-1][...] = total


def add_up(arrays, waits):
    out = jax.ShapeDtypeStruct(arrays[0].shape, arrays[0].dtype)
    specs = [whole(array) for array in arrays]
    return run(add_kernel, [], arrays, specs, waits, out, whole(out), name="add_up")


def is_listed(ancestors, number, block):
    found = ancestors[number, 0] == block
    for i in range(1, ancestors.shape[1]):
        found = found | (ancestors[number, i] == block)
    return found


def partial_kernel(sides, ratio, count, number, place, slots, ancestors, tile_ref, *refs):
    piece_refs, out_refs = refs[:sides], refs[sides:-2]
    right_high, right_low = refs[-2:]
    chunk_rows, columns = out_refs[0].shape
    blocks = tile_ref.shape[1] // columns
    step = pl.program_id(0)

    def listed(block):
        return is_listed(ancestors, number, block)

    @pl.when(step == 0)
    def _assemble():
        if len(piece_refs) == 1:
            right_high[...], right_low[...] = halves(piece_refs[0][...])
            return
        for side, ref in enumerate(piece_refs):
            chips, parts, unit_rows, width = ref.shape
            for o in range(chips):
                owner = place[0] ^ (2 * o + side)
                lanes = pl.ds(pl.multiple_of(owner // ratio * width, width), width)
                first = owner % ratio * (parts * unit_rows)
                rows = pl.ds(pl.multiple_of(first, parts * unit_rows), parts * unit_rows)
                high, low = halves(ref[o].reshape(parts * unit_rows, width))
                right_high[rows, lanes] = high
                right_low[rows, lanes] = low

    def multiply(out_ref):
        out_ref[...] = jnp.zeros_like(out_ref)
        chunk = place[0] * count + slots[place[1], step]

        @pl.when(listed(chunk * chunk_rows // columns))
        def _chunk():
            def add(block, carry):
                @pl.when(listed(place[1] * blocks + block))
                def _block():
                    span = pl.ds(pl.multiple_of(block * columns, columns), columns)
                    high, low = halves(tile_ref[:, span])
                    right = right_high[span, :]
                    dot = functools.partial(jnp.dot, preferred_element_type=jnp.float32)
                    out_ref[...] += dot(high, right) + (
                        dot(high, right_low[span, :]) + dot(low, right)
                    )

                return carry

            lax.fori_loop(0, blocks, add, 0)

    for index, out_ref in enumerate(out_refs):
        pl.when(step == index)(functools.partial(multiply, out_ref))


def partial_product(place, slots, ancestors, tiles, pieces, ratio, columns, number, waits):
    rows, cols = tiles.shape
    count = slots.shape[0]
    out = jax.ShapeDtypeStruct((rows // count, columns), jnp.float32)
    tile = pl.BlockSpec((rows // count, cols), lambda i, p, s, a: (s[p[1], i], 0))
    return run(
        functools.partial(partial_kernel, len(pieces), ratio, count, number),
        [place, slots, ancestors],
        [tiles] + pieces,
        [tile] + [whole(piece) for piece in pieces],
        waits,
        [out] * count,
        [whole(out)] * count,
        grid=(count,),
        scratch=[pltpu.VMEM((cols, columns), jnp.bfloat16)] * 2,
        name="partial_product",
    )


def dot(left, right, side=1):
    def one(a, b):
        return lax.dot_general(
            a, b, (((side,), (0,)), ((), ())), preferred_element_type=jnp.float32
        )

    left_high, left_low = halves(left)
    right_high, right_low = halves(right)
    return one(left_high, right_high) + (one(left_high, right_low) + one(left_low, right_high))


def part_by_core(place, matrix_ref, index, keep_ref, send_ref):
    _, chips, rows, _ = keep_ref.shape
    core = place[0] % 2
    for chip in range(chips):
        for ref, side in ((keep_ref, core), (send_ref, 1 - core)):
            first = pl.multiple_of((chip * 2 + side) * rows, rows)
            ref[index, chip] = matrix_ref[pl.ds(first, rows), :]


def finish_kernel(number, last, first, block, place, ancestors, *refs):
    refs = list(refs)
    sums, factor_ref = [refs.pop(0) for _ in range(4)], refs.pop(0)
    if not first:
        old_rest, old_rows, _ = (refs.pop(0) for _ in range(3))
    if not last:
        link_ref, next_ref = refs.pop(0), refs.pop(0)
    offdiag_ref, keep_ref, send_ref = (refs.pop(0) for _ in range(3))
    if not last:
        cross_ref, kept_ref = refs.pop(0), refs.pop(0)
    part_ref = refs.pop(0)
    offdiag_ref[...] = jnp.zeros_like(offdiag_ref)
    part_ref[...] = jnp.zeros_like(part_ref) if first else old_rest[...]

    own = block(place)

    @pl.when(is_listed(ancestors, number, own))
    def _own():
        summed = ((sums[0][...] + sums[1][...]) + sums[2][...]) + sums[3][...]
        part_ref[...] += dot(factor_ref[0], summed, 0)
        offdiag_ref[0] = -(summed if first else summed + old_rows[...])

    part_by_core(place, part_ref, 0, keep_ref, send_ref)
    if last:
        return
    cross_ref[...] = jnp.zeros_like(cross_ref)

    @pl.when(is_listed(ancestors, number + 1, own))
    def _cross():
        cross_ref[...] = dot(offdiag_ref[0], next_ref[0], 0)

    kept_ref[...] = cross_ref[...] + dot(part_ref[...], link_ref[0])
    part_by_core(place, kept_ref, 1, keep_ref, send_ref)


def rest_kernel(link_ref, cross_ref, part_ref, offdiag_ref, rest_ref, rows_ref):
    link = link_ref[0]
    rest_ref[...] = dot(cross_ref[...], link, 0) + dot(link, part_ref[...], 0)
    rows_ref[...] = dot(offdiag_ref[0], link)


def rest_of(link_factor, cross, link_part, offdiag, number):
    _, unit_rows, columns = offdiag.shape
    link = pl.BlockSpec((1, columns, columns), lambda *_: (number, 0, 0))
    rows = pl.BlockSpec((1, unit_rows, columns), lambda *_: (number, 0, 0))
    outs = [cross, jax.ShapeDtypeStruct((unit_rows, columns), jnp.float32)]
    outs = [jax.ShapeDtypeStruct(out.shape, jnp.float32) for out in outs]
    return run(
        rest_kernel, [], [link_factor, cross, link_part, offdiag],
        [link, whole(cross), whole(link_part), rows], [], outs, [whole(out) for out in outs],
        name="rest",
    )


def finish(number, block, place, ancestors, sums, factor, before, link_factor, chips, waits):
    nsuper, unit_rows, columns = factor.shape
    first, last = number == 0, number + 1 == nsuper
    slab = (1, unit_rows, columns)
    arrays, specs = list(sums), [whole(array) for array in sums]
    arrays.append(factor)
    specs.append(pl.BlockSpec(slab, lambda *_: (number, 0, 0)))
    alias = {}
    if not first:
        alias = {2 + len(arrays) + 2: 0}
        arrays += before
        specs += [whole(before[0]), whole(before[1])]
        specs.append(pl.BlockSpec((1, 8, LANES), lambda *_: (0, 0, 0)))
    if not last:
        arrays += [link_factor, factor]
        specs.append(pl.BlockSpec((1, columns, columns), lambda *_: (number, 0, 0)))
        specs.append(pl.BlockSpec(slab, lambda *_: (number + 1, 0, 0)))
    shape = jax.ShapeDtypeStruct
    groups = shape((1 if last else 2, chips, columns // (2 * chips), columns), jnp.float32)
    outs = [shape(factor.shape, jnp.float32), groups, groups]
    out_specs = [pl.BlockSpec(slab, lambda *_: (number, 0, 0)), whole(groups), whole(groups)]
    if not last:
        more = [shape((columns, columns), jnp.float32)] * 2
        outs += more
        out_specs += [whole(array) for array in more]
    return run(
        functools.partial(finish_kernel, number, last, first, block),
        [place, ancestors],
        arrays,
        specs,
        waits,
        outs,
        out_specs,
        scratch=[pltpu.VMEM((columns, columns), jnp.float32)],
        alias=alias,
        name="finish",
    )


def fold_kernel(place, keep_ref, received_ref, *out_refs):
    chip = place[0] // 2
    for o, out_ref in enumerate(out_refs):
        out_ref[...] = keep_ref[:, chip ^ o] + received_ref[:, chip ^ o]


def fold(place, keep, received, waits):
    number, chips, rows, columns = keep.shape
    out = jax.ShapeDtypeStruct((number, rows, columns), jnp.float32)
    specs = [whole(keep)] * 2
    outs = [out] * chips
    return run(
        fold_kernel, [place], [keep, received], specs, waits, outs, [whole(out)] * chips,
        name="fold",
    )


def fold_pair_kernel(place, *refs):
    *piece_refs, kept_ref, other_ref = refs
    mine = place[1] % 2
    for out_ref, index in ((kept_ref, mine), (other_ref, 1 - mine)):
        total = piece_refs[0][index]
        for ref in piece_refs[1:]:
            total = total + ref[index]
        out_ref[...] = total


def fold_pair(place, pieces):
    out = jax.ShapeDtypeStruct(pieces[0].shape[1:], jnp.float32)
    specs = [whole(piece) for piece in pieces]
    return run(
        fold_pair_kernel, [place], pieces, specs, [], [out] * 2, [whole(out)] * 2, name="fold_pair"
    )


def bases_kernel(nsuper, place, diag_ref, link_ref, *refs):
    diag_out, link_out, base_ref, next_ref = refs
    rows = diag_out.shape[1]
    mine = pl.ds(pl.multiple_of(place[0] * rows, rows), rows)
    base_ref[...] = diag_ref[0]
    diag_out[0] = base_ref[mine, :]
    for number in range(1, nsuper):
        link = link_ref[number - 1]
        next_ref[...] = dot(base_ref[...], link)
        link_out[number - 1] = next_ref[mine, :]
        base_ref[...] = diag_ref[number] + dot(link, next_ref[...], 0)
        diag_out[number] = base_ref[mine, :]


def bases_of(place, diag_inverse, link_factor, rows, waits):
    nsuper, columns, _ = diag_inverse.shape
    outs = [
        jax.ShapeDtypeStruct((nsuper, rows, columns), jnp.float32),
        jax.ShapeDtypeStruct((nsuper - 1, rows, columns), jnp.float32),
    ]
    return run(
        functools.partial(bases_kernel, nsuper),
        [place],
        [diag_inverse, link_factor],
        [whole(diag_inverse), whole(link_factor)],
        waits,
        outs,
        [whole(out) for out in outs],
        scratch=[pltpu.VMEM((columns, columns), jnp.float32)] * 2,
        name="bases",
    )


def outputs_kernel(place, *refs):
    diag_base, link_base, *sums, diag_out, link_out = refs
    steps = link_out.shape[0]
    for number in range(steps):
        pair = sums[2 * number : 2 * number + 2]

        def put(diag, link, number=number):
            diag_out[number] = diag[...] + diag_base[number]
            link_out[number] = -(link[...] + link_base[number])

        pl.when(place[1] % 2 == 0)(functools.partial(put, *pair))
        pl.when(place[1] % 2 == 1)(functools.partial(put, *pair[::-1]))
    diag_out[steps] = sums[-2][0] + sums[-1][0] + diag_base[steps]


def outputs(place, bases, sums):
    arrays = list(bases) + sums
    specs = [whole(array) for array in arrays]
    outs = [jax.ShapeDtypeStruct(base.shape, jnp.float32) for base in bases]
    return run(outputs_kernel, [place], arrays, specs, [], outs, specs[:2], name="outputs")


def to_column(pieces, ratio):
    return [pieces[0]] + [flip(pieces[o], "pcol", o * ratio) for o in range(1, len(pieces))]


def to_plane(pieces):
    return [pieces[0]] + [flip(pieces[o], "prow", o) for o in range(1, len(pieces))]


def to_plane_whole(factor, count, ratio):
    pieces = jnp.swapaxes(factor.reshape(factor.shape[0], count, -1), 0, 1)
    groups = [[c * ratio + k for c in range(count)] for k in range(ratio)]
    spread = lax.all_to_all(pieces, "pcol", 0, 0, axis_index_groups=groups)
    return lax.all_to_all(spread, "prow", 0, 0)


def gather_plane(own, pcol_count):
    return [own] + [flip(own, "pcol", offset) for offset in range(2, pcol_count, 2)]


def in_rows(gathered, count, ratio):
    _, _, unit_rows, width = gathered.shape
    split = gathered.reshape(count, ratio, count, unit_rows, width)
    rows = jnp.transpose(split, (1, 2, 3, 0, 4))
    return rows.reshape(ratio * count * unit_rows, count * width)


FOUR_SLOTS = ((3, 2, 1, 0), (2, 0, 3, 1), (1, 3, 0, 2), (0, 1, 2, 3))


def slots_of(count):
    return FOUR_SLOTS if count == len(FOUR_SLOTS) else (tuple(range(count)),) * count


def sum_over_four(slots):
    near = lax.ppermute(slots[0], "prow", [(0, 1), (3, 2)])
    total = lax.ppermute(slots[1], "prow", [(0, 2), (2, 3), (3, 1), (1, 0)])
    middle = lax.ppermute(slots[0], "prow", [(1, 2), (2, 1)])
    both = add_up([slots[2], near], [])
    last = lax.ppermute(both, "prow", [(1, 3), (2, 0), (0, 1), (3, 2)])
    return [slots[3], total, middle, last, near]


def sum_over_line(slots, z):
    count = len(slots)
    if count == len(FOUR_SLOTS):
        return sum_over_four(slots)
    chunks = jnp.stack(slots)

    def chunk(index):
        return lax.dynamic_index_in_dim(chunks, jnp.clip(index, 0, count - 1), 0, keepdims=False)

    up = down = None
    for t in range(1, count):
        up_send, down_send = chunk(z + count - t), chunk(z + t - count)
        if up is not None:
            up_send, down_send = up_send + up, down_send + down
        up = lax.ppermute(up_send, "prow", [(i, i + 1) for i in range(min(t, count - 1))])
        down = lax.ppermute(
            down_send, "prow", [(i, i - 1) for i in range(max(count - t, 1), count)]
        )
    mine = chunk(z)
    none = jnp.zeros_like(mine)
    return [mine, none if up is None else up, none if down is None else down, none, mine]


def sum_plane(place, keep, send, waits):
    pieces = fold(place, keep, flip(send, "pcol", 1), waits)
    return [pieces[0]] + [flip(pieces[o], "pcol", 2 * o) for o in range(1, len(pieces))]


def sum_planes(pieces, count):
    bit = 1
    while True:
        total = add_up(pieces, [])
        if bit >= count:
            return [total, jnp.zeros_like(total)]
        pieces = [total, flip(total, "prow", bit)]
        bit *= 2
        if bit >= count:
            return pieces


def sum_pair_near(place, pieces):
    kept, other = fold_pair(place, pieces)
    return [kept, flip(other, "prow", 1)]


def sum_pair_far(pieces, count, waits):
    bit = 2
    while True:
        total = add_up(pieces, waits)
        if bit >= count:
            return [total, flip(total, "prow", 1)]
        pieces, waits = [total, flip(total, "prow", bit)], []
        bit *= 2


def body(inverse_tiles, factor, link_factor, diag_inverse, ancestors):
    row_count, col_count = inverse_tiles.shape
    nsuper, unit_rows, columns = factor.shape
    count = lax.axis_size("prow")
    pcol_count = lax.axis_size("pcol")
    ratio = col_count // row_count
    z = lax.axis_index("prow")
    pcol_index = lax.axis_index("pcol")
    width = columns // count
    place = jnp.stack([pcol_index, z, pcol_index // ratio]).astype(jnp.int32)
    slots = jnp.asarray(slots_of(count), jnp.int32)

    def own_block(place):
        return (place[0] * count + place[1]) * unit_rows // columns

    received = []
    if width % LANES == 0:
        sent = to_column(cut(place, factor, count), ratio)
        for number in range(nsuper):
            waits = received[-1][1:] if received else []
            received.append(to_plane(turn(place, sent, number, waits)))
    rows, firsts, gathered = [], [], []
    for number in range(nsuper):
        if received:
            own = arrange(place, received[number], gathered)
            found = gather_plane(own, pcol_count)
            gathered = found[1:]
            waits = [piece for later in received[number + 1 : number + 2] for piece in later[1:]]
            packed = pack(found, waits + (rows[-1][1:4] if rows else []))
            pieces = [packed, flip(packed, "pcol", 1)]
        else:
            own = to_plane_whole(factor[number], count, ratio)
            pieces = [in_rows(lax.all_gather(own, "pcol", axis=0), count, ratio)]
        if number == 0:
            bases = bases_of(place, diag_inverse, link_factor, columns // pcol_count, [own])
        partial = partial_product(
            place, slots, ancestors, inverse_tiles, pieces, ratio, columns, number, [bases[0]]
        )
        firsts.append(partial[0])
        *early, last_row, near = sum_over_line(partial, z)
        rows.append([*early, near, last_row])

    sums, before, pending = [], [], None
    for number in range(nsuper):
        last = number + 1 == nsuper
        waits = [] if last else [firsts[number + 1], rows[number + 1][3]]
        offdiag, keep, send, *link = finish(
            number, own_block, place, ancestors, rows[number][:3] + rows[number][4:], factor, before,
            link_factor, pcol_count // 2, waits + (pending if pending else []),
        )
        if pending:
            sums += sum_pair_far(pending, count, [keep])
        waits = []
        if not last:
            rest = rest_of(link_factor, *link, offdiag, number)
            before = [*rest, offdiag]
            waits = [rest[0], rows[number + 1][1]]
        group = sum_plane(place, keep, send, waits)
        pending = None if last else sum_pair_near(place, group)
    sums += sum_planes(group, count)
    return (offdiag, *outputs(place, bases, sums))


def solution(mesh):
    in_specs = (P("pcol", "prow"), P(None, ("pcol", "prow"), None), P(), P(), P())
    out_specs = (P(None, ("pcol", "prow"), None), P(None, "pcol", None), P(None, "pcol", None))
    return jax.shard_map(body, mesh=mesh, in_specs=in_specs, out_specs=out_specs, check_vma=False)
```

```python
import functools

import jax
import jax.numpy as jnp
from jax import lax
from jax.experimental import pallas as pl
from jax.experimental.pallas import tpu as pltpu
from jax.sharding import PartitionSpec as P

BOTH = ("prow", "pcol")
VMEM_LIMIT = 28 * 1024 * 1024
LANES = 128


def halves(value):
    high = value.astype(jnp.bfloat16)
    low = (value - high.astype(jnp.float32)).astype(jnp.bfloat16)
    return high, low


def flip(value, axis, bit):
    return lax.ppermute(value, axis, [(i, i ^ bit) for i in range(lax.axis_size(axis))])


def run(
    kernel, scalars, arrays, specs, waits, outs, out_specs, grid=(1,), scratch=(), alias=None, name=None
):
    def corner(array):
        block = (1,) * (array.ndim - 2) + (8, LANES)
        return pl.BlockSpec(block, lambda *_: (0,) * array.ndim)

    def body(*refs):
        first = len(scalars) + len(arrays)
        kernel(*refs[:first], *refs[first + len(waits) :])

    return pl.pallas_call(
        body,
        grid_spec=pltpu.PrefetchScalarGridSpec(
            num_scalar_prefetch=len(scalars),
            grid=grid,
            in_specs=list(specs) + [corner(array) for array in waits],
            out_specs=out_specs,
            scratch_shapes=list(scratch),
        ),
        out_shape=outs,
        input_output_aliases=alias or {},
        compiler_params=pltpu.CompilerParams(vmem_limit_bytes=VMEM_LIMIT),
        cost_estimate=pl.CostEstimate(flops=0, bytes_accessed=0, transcendentals=0),
        name=name,
    )(*scalars, *arrays, *waits)


def whole(array):
    return pl.BlockSpec(array.shape, lambda *_: (0,) * array.ndim)


def cut_kernel(place, factor_ref, *out_refs):
    width = out_refs[0].shape[2]
    for o, out_ref in enumerate(out_refs):
        start = pl.multiple_of((place[2] ^ o) * width, width)
        out_ref[...] = factor_ref[:, :, pl.ds(start, width)]


def cut(place, factor, count):
    nsuper, unit_rows, columns = factor.shape
    piece = jax.ShapeDtypeStruct((nsuper, unit_rows, columns // count), factor.dtype)
    outs = [piece] * count
    specs = [whole(piece)] * count
    return run(cut_kernel, [place], [factor], [whole(factor)], [], outs, specs, name="cut")


def turn_kernel(place, *refs):
    count = len(refs) // 2
    for shift in range(count):

        @pl.when((place[1] ^ place[2]) == shift)
        def _copy(shift=shift):
            for o in range(count):
                refs[count + o][...] = refs[o ^ shift][0]


def turn(place, pieces, number, waits):
    count = len(pieces)
    _, unit_rows, width = pieces[0].shape
    piece = jax.ShapeDtypeStruct((unit_rows, width), pieces[0].dtype)
    spec = pl.BlockSpec((1, unit_rows, width), lambda *_: (number, 0, 0))
    return run(
        turn_kernel, [place], pieces, [spec] * count, waits, [piece] * count,
        [whole(piece)] * count, name="turn",
    )


def arrange_kernel(place, *refs):
    out_ref = refs[-1]
    for o, piece_ref in enumerate(refs[:-1]):
        out_ref[place[1] ^ o] = piece_ref[...]


def arrange(place, pieces, waits):
    out = jax.ShapeDtypeStruct((len(pieces),) + pieces[0].shape, pieces[0].dtype)
    specs = [whole(piece) for piece in pieces]
    return run(arrange_kernel, [place], pieces, specs, waits, out, whole(out), name="arrange")


def pack_kernel(*refs):
    for index, ref in enumerate(refs[:-1]):
        refs[-1][index] = ref[...]


def pack(pieces, waits):
    out = jax.ShapeDtypeStruct((len(pieces),) + pieces[0].shape, pieces[0].dtype)
    specs = [whole(piece) for piece in pieces]
    return run(pack_kernel, [], pieces, specs, waits, out, whole(out), name="pack")


def add_kernel(*refs):
    total = refs[0][...]
    for ref in refs[1:-1]:
        total = total + ref[...]
    refs[-1][...] = total


def add_up(arrays, waits):
    out = jax.ShapeDtypeStruct(arrays[0].shape, arrays[0].dtype)
    specs = [whole(array) for array in arrays]
    return run(add_kernel, [], arrays, specs, waits, out, whole(out), name="add_up")


def is_listed(ancestors, number, block):
    found = ancestors[number, 0] == block
    for i in range(1, ancestors.shape[1]):
        found = found | (ancestors[number, i] == block)
    return found


def partial_kernel(sides, ratio, count, number, place, slots, ancestors, tile_ref, *refs):
    piece_refs, out_refs = refs[:sides], refs[sides:-2]
    right_high, right_low = refs[-2:]
    chunk_rows, columns = out_refs[0].shape
    blocks = tile_ref.shape[1] // columns
    step = pl.program_id(0)

    def listed(block):
        return is_listed(ancestors, number, block)

    @pl.when(step == 0)
    def _assemble():
        if len(piece_refs) == 1:
            right_high[...], right_low[...] = halves(piece_refs[0][...])
            return
        for side, ref in enumerate(piece_refs):
            chips, parts, unit_rows, width = ref.shape
            for o in range(chips):
                owner = place[0] ^ (2 * o + side)
                lanes = pl.ds(pl.multiple_of(owner // ratio * width, width), width)
                first = owner % ratio * (parts * unit_rows)
                rows = pl.ds(pl.multiple_of(first, parts * unit_rows), parts * unit_rows)
                high, low = halves(ref[o].reshape(parts * unit_rows, width))
                right_high[rows, lanes] = high
                right_low[rows, lanes] = low

    def multiply(out_ref):
        out_ref[...] = jnp.zeros_like(out_ref)
        chunk = place[0] * count + slots[place[1], step]

        @pl.when(listed(chunk * chunk_rows // columns))
        def _chunk():
            def add(block, carry):
                @pl.when(listed(place[1] * blocks + block))
                def _block():
                    span = pl.ds(pl.multiple_of(block * columns, columns), columns)
                    high, low = halves(tile_ref[:, span])
                    right = right_high[span, :]
                    dot = functools.partial(jnp.dot, preferred_element_type=jnp.float32)
                    out_ref[...] += dot(high, right) + (
                        dot(high, right_low[span, :]) + dot(low, right)
                    )

                return carry

            lax.fori_loop(0, blocks, add, 0)

    for index, out_ref in enumerate(out_refs):
        pl.when(step == index)(functools.partial(multiply, out_ref))


def partial_product(place, slots, ancestors, tiles, pieces, ratio, columns, number, waits):
    rows, cols = tiles.shape
    count = slots.shape[0]
    out = jax.ShapeDtypeStruct((rows // count, columns), jnp.float32)
    tile = pl.BlockSpec((rows // count, cols), lambda i, p, s, a: (s[p[1], i], 0))
    return run(
        functools.partial(partial_kernel, len(pieces), ratio, count, number),
        [place, slots, ancestors],
        [tiles] + pieces,
        [tile] + [whole(piece) for piece in pieces],
        waits,
        [out] * count,
        [whole(out)] * count,
        grid=(count,),
        scratch=[pltpu.VMEM((cols, columns), jnp.bfloat16)] * 2,
        name="partial_product",
    )


def dot(left, right, side=1):
    def one(a, b):
        return lax.dot_general(
            a, b, (((side,), (0,)), ((), ())), preferred_element_type=jnp.float32
        )

    left_high, left_low = halves(left)
    right_high, right_low = halves(right)
    return one(left_high, right_high) + (one(left_high, right_low) + one(left_low, right_high))


def part_by_core(place, matrix_ref, index, keep_ref, send_ref):
    _, chips, rows, _ = keep_ref.shape
    core = place[0] % 2
    for chip in range(chips):
        for ref, side in ((keep_ref, core), (send_ref, 1 - core)):
            first = pl.multiple_of((chip * 2 + side) * rows, rows)
            ref[index, chip] = matrix_ref[pl.ds(first, rows), :]


def finish_kernel(number, last, first, block, place, ancestors, *refs):
    refs = list(refs)
    sums, factor_ref = [refs.pop(0) for _ in range(4)], refs.pop(0)
    if not first:
        old_rest, old_rows, _ = (refs.pop(0) for _ in range(3))
    if not last:
        link_ref, next_ref = refs.pop(0), refs.pop(0)
    offdiag_ref, keep_ref, send_ref = (refs.pop(0) for _ in range(3))
    if not last:
        cross_ref, kept_ref = refs.pop(0), refs.pop(0)
    part_ref = refs.pop(0)
    offdiag_ref[...] = jnp.zeros_like(offdiag_ref)
    part_ref[...] = jnp.zeros_like(part_ref) if first else old_rest[...]

    own = block(place)

    @pl.when(is_listed(ancestors, number, own))
    def _own():
        summed = ((sums[0][...] + sums[1][...]) + sums[2][...]) + sums[3][...]
        part_ref[...] += dot(factor_ref[0], summed, 0)
        offdiag_ref[0] = -(summed if first else summed + old_rows[...])

    part_by_core(place, part_ref, 0, keep_ref, send_ref)
    if last:
        return
    cross_ref[...] = jnp.zeros_like(cross_ref)

    @pl.when(is_listed(ancestors, number + 1, own))
    def _cross():
        cross_ref[...] = dot(offdiag_ref[0], next_ref[0], 0)

    kept_ref[...] = cross_ref[...] + dot(part_ref[...], link_ref[0])
    part_by_core(place, kept_ref, 1, keep_ref, send_ref)


def rest_kernel(link_ref, cross_ref, part_ref, offdiag_ref, rest_ref, rows_ref):
    link = link_ref[0]
    rest_ref[...] = dot(cross_ref[...], link, 0) + dot(link, part_ref[...], 0)
    rows_ref[...] = dot(offdiag_ref[0], link)


def rest_of(link_factor, cross, link_part, offdiag, number):
    _, unit_rows, columns = offdiag.shape
    link = pl.BlockSpec((1, columns, columns), lambda *_: (number, 0, 0))
    rows = pl.BlockSpec((1, unit_rows, columns), lambda *_: (number, 0, 0))
    outs = [cross, jax.ShapeDtypeStruct((unit_rows, columns), jnp.float32)]
    outs = [jax.ShapeDtypeStruct(out.shape, jnp.float32) for out in outs]
    return run(
        rest_kernel, [], [link_factor, cross, link_part, offdiag],
        [link, whole(cross), whole(link_part), rows], [], outs, [whole(out) for out in outs],
        name="rest",
    )


def finish(number, block, place, ancestors, sums, factor, before, link_factor, chips, waits):
    nsuper, unit_rows, columns = factor.shape
    first, last = number == 0, number + 1 == nsuper
    slab = (1, unit_rows, columns)
    arrays, specs = list(sums), [whole(array) for array in sums]
    arrays.append(factor)
    specs.append(pl.BlockSpec(slab, lambda *_: (number, 0, 0)))
    alias = {}
    if not first:
        alias = {2 + len(arrays) + 2: 0}
        arrays += before
        specs += [whole(before[0]), whole(before[1])]
        specs.append(pl.BlockSpec((1, 8, LANES), lambda *_: (0, 0, 0)))
    if not last:
        arrays += [link_factor, factor]
        specs.append(pl.BlockSpec((1, columns, columns), lambda *_: (number, 0, 0)))
        specs.append(pl.BlockSpec(slab, lambda *_: (number + 1, 0, 0)))
    shape = jax.ShapeDtypeStruct
    groups = shape((1 if last else 2, chips, columns // (2 * chips), columns), jnp.float32)
    outs = [shape(factor.shape, jnp.float32), groups, groups]
    out_specs = [pl.BlockSpec(slab, lambda *_: (number, 0, 0)), whole(groups), whole(groups)]
    if not last:
        more = [shape((columns, columns), jnp.float32)] * 2
        outs += more
        out_specs += [whole(array) for array in more]
    return run(
        functools.partial(finish_kernel, number, last, first, block),
        [place, ancestors],
        arrays,
        specs,
        waits,
        outs,
        out_specs,
        scratch=[pltpu.VMEM((columns, columns), jnp.float32)],
        alias=alias,
        name="finish",
    )


def fold_kernel(place, keep_ref, received_ref, *out_refs):
    chip = place[0] // 2
    for o, out_ref in enumerate(out_refs):
        out_ref[...] = keep_ref[:, chip ^ o] + received_ref[:, chip ^ o]


def fold(place, keep, received, waits):
    number, chips, rows, columns = keep.shape
    out = jax.ShapeDtypeStruct((number, rows, columns), jnp.float32)
    specs = [whole(keep)] * 2
    outs = [out] * chips
    return run(
        fold_kernel, [place], [keep, received], specs, waits, outs, [whole(out)] * chips,
        name="fold",
    )


def fold_pair_kernel(place, *refs):
    *piece_refs, kept_ref, other_ref = refs
    mine = place[1] % 2
    for out_ref, index in ((kept_ref, mine), (other_ref, 1 - mine)):
        total = piece_refs[0][index]
        for ref in piece_refs[1:]:
            total = total + ref[index]
        out_ref[...] = total


def fold_pair(place, pieces):
    out = jax.ShapeDtypeStruct(pieces[0].shape[1:], jnp.float32)
    specs = [whole(piece) for piece in pieces]
    return run(
        fold_pair_kernel, [place], pieces, specs, [], [out] * 2, [whole(out)] * 2, name="fold_pair"
    )


def bases_kernel(nsuper, place, diag_ref, link_ref, *refs):
    diag_out, link_out, base_ref, next_ref = refs
    rows = diag_out.shape[1]
    mine = pl.ds(pl.multiple_of(place[0] * rows, rows), rows)
    base_ref[...] = diag_ref[0]
    diag_out[0] = base_ref[mine, :]
    for number in range(1, nsuper):
        link = link_ref[number - 1]
        next_ref[...] = dot(base_ref[...], link)
        link_out[number - 1] = next_ref[mine, :]
        base_ref[...] = diag_ref[number] + dot(link, next_ref[...], 0)
        diag_out[number] = base_ref[mine, :]


def bases_of(place, diag_inverse, link_factor, rows, waits):
    nsuper, columns, _ = diag_inverse.shape
    outs = [
        jax.ShapeDtypeStruct((nsuper, rows, columns), jnp.float32),
        jax.ShapeDtypeStruct((nsuper - 1, rows, columns), jnp.float32),
    ]
    return run(
        functools.partial(bases_kernel, nsuper),
        [place],
        [diag_inverse, link_factor],
        [whole(diag_inverse), whole(link_factor)],
        waits,
        outs,
        [whole(out) for out in outs],
        scratch=[pltpu.VMEM((columns, columns), jnp.float32)] * 2,
        name="bases",
    )


def outputs_kernel(place, *refs):
    diag_base, link_base, *sums, diag_out, link_out = refs
    steps = link_out.shape[0]
    for number in range(steps):
        pair = sums[2 * number : 2 * number + 2]

        def put(diag, link, number=number):
            diag_out[number] = diag[...] + diag_base[number]
            link_out[number] = -(link[...] + link_base[number])

        pl.when(place[1] % 2 == 0)(functools.partial(put, *pair))
        pl.when(place[1] % 2 == 1)(functools.partial(put, *pair[::-1]))
    diag_out[steps] = sums[-2][0] + sums[-1][0] + diag_base[steps]


def outputs(place, bases, sums):
    arrays = list(bases) + sums
    specs = [whole(array) for array in arrays]
    outs = [jax.ShapeDtypeStruct(base.shape, jnp.float32) for base in bases]
    return run(outputs_kernel, [place], arrays, specs, [], outs, specs[:2], name="outputs")


def to_column(pieces, ratio):
    return [pieces[0]] + [flip(pieces[o], "pcol", o * ratio) for o in range(1, len(pieces))]


def to_plane(pieces):
    return [pieces[0]] + [flip(pieces[o], "prow", o) for o in range(1, len(pieces))]


def to_plane_whole(factor, count, ratio):
    pieces = jnp.swapaxes(factor.reshape(factor.shape[0], count, -1), 0, 1)
    groups = [[c * ratio + k for c in range(count)] for k in range(ratio)]
    spread = lax.all_to_all(pieces, "pcol", 0, 0, axis_index_groups=groups)
    return lax.all_to_all(spread, "prow", 0, 0)


def gather_plane(own, pcol_count):
    return [own] + [flip(own, "pcol", offset) for offset in range(2, pcol_count, 2)]


def in_rows(gathered, count, ratio):
    _, _, unit_rows, width = gathered.shape
    split = gathered.reshape(count, ratio, count, unit_rows, width)
    rows = jnp.transpose(split, (1, 2, 3, 0, 4))
    return rows.reshape(ratio * count * unit_rows, count * width)


FOUR_SLOTS = ((3, 2, 1, 0), (2, 0, 3, 1), (1, 3, 0, 2), (0, 1, 2, 3))


def slots_of(count):
    return FOUR_SLOTS if count == len(FOUR_SLOTS) else (tuple(range(count)),) * count


def sum_over_four(slots):
    near = lax.ppermute(slots[0], "prow", [(0, 1), (3, 2)])
    total = lax.ppermute(slots[1], "prow", [(0, 2), (2, 3), (3, 1), (1, 0)])
    middle = lax.ppermute(slots[0], "prow", [(1, 2), (2, 1)])
    both = add_up([slots[2], near], [])
    last = lax.ppermute(both, "prow", [(1, 3), (2, 0), (0, 1), (3, 2)])
    return [slots[3], total, middle, last, near]


def sum_over_line(slots, z):
    count = len(slots)
    if count == len(FOUR_SLOTS):
        return sum_over_four(slots)
    chunks = jnp.stack(slots)

    def chunk(index):
        return lax.dynamic_index_in_dim(chunks, jnp.clip(index, 0, count - 1), 0, keepdims=False)

    up = down = None
    for t in range(1, count):
        up_send, down_send = chunk(z + count - t), chunk(z + t - count)
        if up is not None:
            up_send, down_send = up_send + up, down_send + down
        up = lax.ppermute(up_send, "prow", [(i, i + 1) for i in range(min(t, count - 1))])
        down = lax.ppermute(
            down_send, "prow", [(i, i - 1) for i in range(max(count - t, 1), count)]
        )
    mine = chunk(z)
    none = jnp.zeros_like(mine)
    return [mine, none if up is None else up, none if down is None else down, none, mine]


def sum_plane(place, keep, send, waits):
    pieces = fold(place, keep, flip(send, "pcol", 1), waits)
    return [pieces[0]] + [flip(pieces[o], "pcol", 2 * o) for o in range(1, len(pieces))]


def sum_planes(pieces, count):
    bit = 1
    while True:
        total = add_up(pieces, [])
        if bit >= count:
            return [total, jnp.zeros_like(total)]
        pieces = [total, flip(total, "prow", bit)]
        bit *= 2
        if bit >= count:
            return pieces


def sum_pair_near(place, pieces):
    kept, other = fold_pair(place, pieces)
    return [kept, flip(other, "prow", 1)]


def sum_pair_far(pieces, count, waits):
    bit = 2
    while True:
        total = add_up(pieces, waits)
        if bit >= count:
            return [total, flip(total, "prow", 1)]
        pieces, waits = [total, flip(total, "prow", bit)], []
        bit *= 2


def body(inverse_tiles, factor, link_factor, diag_inverse, ancestors):
    row_count, col_count = inverse_tiles.shape
    nsuper, unit_rows, columns = factor.shape
    count = lax.axis_size("prow")
    pcol_count = lax.axis_size("pcol")
    ratio = col_count // row_count
    z = lax.axis_index("prow")
    pcol_index = lax.axis_index("pcol")
    width = columns // count
    place = jnp.stack([pcol_index, z, pcol_index // ratio]).astype(jnp.int32)
    slots = jnp.asarray(slots_of(count), jnp.int32)

    def own_block(place):
        return (place[0] * count + place[1]) * unit_rows // columns

    received = []
    if width % LANES == 0:
        sent = to_column(cut(place, factor, count), ratio)
        for number in range(nsuper):
            waits = received[-1][1:] if received else []
            received.append(to_plane(turn(place, sent, number, waits)))
    rows, gathered = [], []
    for number in range(nsuper):
        if received:
            own = arrange(place, received[number], gathered)
            found = gather_plane(own, pcol_count)
            gathered = found[1:]
            waits = [piece for later in received[number + 1 : number + 2] for piece in later[1:]]
            packed = pack(found, waits + (rows[-1][1:4] if rows else []))
            pieces = [packed, flip(packed, "pcol", 1)]
        else:
            own = to_plane_whole(factor[number], count, ratio)
            pieces = [in_rows(lax.all_gather(own, "pcol", axis=0), count, ratio)]
        if number == 0:
            bases = bases_of(place, diag_inverse, link_factor, columns // pcol_count, [own])
        partial = partial_product(
            place, slots, ancestors, inverse_tiles, pieces, ratio, columns, number, [bases[0]]
        )
        *early, last_row, near = sum_over_line(partial, z)
        rows.append([*early, near, last_row])

    sums, before, pending = [], [], []
    for number in range(nsuper):
        last = number + 1 == nsuper
        waits = [] if last else rows[number + 1][1:4]
        offdiag, keep, send, *link = finish(
            number, own_block, place, ancestors, rows[number][:3] + rows[number][4:], factor, before,
            link_factor, pcol_count // 2, waits + pending[:1],
        )
        if pending:
            sums += sum_pair_far(pending, count, [keep])
        waits = []
        if not last:
            rest = rest_of(link_factor, *link, offdiag, number)
            before = [*rest, offdiag]
            waits = [rest[0]]
        group = sum_plane(place, keep, send, waits)
        pending = [] if last else sum_pair_near(place, group)
    sums += sum_planes(group, count)
    return (offdiag, *outputs(place, bases, sums))


def solution(mesh):
    in_specs = (P("pcol", "prow"), P(None, ("pcol", "prow"), None), P(), P(), P())
    out_specs = (P(None, ("pcol", "prow"), None), P(None, "pcol", None), P(None, "pcol", None))
    return jax.shard_map(body, mesh=mesh, in_specs=in_specs, out_specs=out_specs, check_vma=False)
```

```python
import functools

import jax
import jax.numpy as jnp
from jax import lax
from jax.experimental import pallas as pl
from jax.experimental.pallas import tpu as pltpu
from jax.sharding import PartitionSpec as P

BOTH = ("prow", "pcol")
VMEM_LIMIT = 28 * 1024 * 1024
LANES = 128


def halves(value):
    high = value.astype(jnp.bfloat16)
    low = (value - high.astype(jnp.float32)).astype(jnp.bfloat16)
    return high, low


def flip(value, axis, bit):
    return lax.ppermute(value, axis, [(i, i ^ bit) for i in range(lax.axis_size(axis))])


def run(
    kernel, scalars, arrays, specs, waits, outs, out_specs, grid=(1,), scratch=(), alias=None, name=None
):
    def corner(array):
        block = (1,) * (array.ndim - 2) + (8, LANES)
        return pl.BlockSpec(block, lambda *_: (0,) * array.ndim)

    def body(*refs):
        first = len(scalars) + len(arrays)
        kernel(*refs[:first], *refs[first + len(waits) :])

    return pl.pallas_call(
        body,
        grid_spec=pltpu.PrefetchScalarGridSpec(
            num_scalar_prefetch=len(scalars),
            grid=grid,
            in_specs=list(specs) + [corner(array) for array in waits],
            out_specs=out_specs,
            scratch_shapes=list(scratch),
        ),
        out_shape=outs,
        input_output_aliases=alias or {},
        compiler_params=pltpu.CompilerParams(vmem_limit_bytes=VMEM_LIMIT),
        cost_estimate=pl.CostEstimate(flops=0, bytes_accessed=0, transcendentals=0),
        name=name,
    )(*scalars, *arrays, *waits)


def whole(array):
    return pl.BlockSpec(array.shape, lambda *_: (0,) * array.ndim)


def cut_kernel(place, factor_ref, *out_refs):
    width = out_refs[0].shape[2]
    for o, out_ref in enumerate(out_refs):
        start = pl.multiple_of((place[2] ^ o) * width, width)
        out_ref[...] = factor_ref[:, :, pl.ds(start, width)]


def cut(place, factor, count):
    nsuper, unit_rows, columns = factor.shape
    piece = jax.ShapeDtypeStruct((nsuper, unit_rows, columns // count), factor.dtype)
    outs = [piece] * count
    specs = [whole(piece)] * count
    return run(cut_kernel, [place], [factor], [whole(factor)], [], outs, specs, name="cut")


def turn_kernel(place, *refs):
    count = len(refs) // 2
    for shift in range(count):

        @pl.when((place[1] ^ place[2]) == shift)
        def _copy(shift=shift):
            for o in range(count):
                refs[count + o][...] = refs[o ^ shift][0]


def turn(place, pieces, number, waits):
    count = len(pieces)
    _, unit_rows, width = pieces[0].shape
    piece = jax.ShapeDtypeStruct((unit_rows, width), pieces[0].dtype)
    spec = pl.BlockSpec((1, unit_rows, width), lambda *_: (number, 0, 0))
    return run(
        turn_kernel, [place], pieces, [spec] * count, waits, [piece] * count,
        [whole(piece)] * count, name="turn",
    )


def arrange_kernel(place, *refs):
    out_ref = refs[-1]
    for o, piece_ref in enumerate(refs[:-1]):
        out_ref[place[1] ^ o] = piece_ref[...]


def arrange(place, pieces, waits):
    out = jax.ShapeDtypeStruct((len(pieces),) + pieces[0].shape, pieces[0].dtype)
    specs = [whole(piece) for piece in pieces]
    return run(arrange_kernel, [place], pieces, specs, waits, out, whole(out), name="arrange")


def pack_kernel(*refs):
    for index, ref in enumerate(refs[:-1]):
        refs[-1][index] = ref[...]


def pack(pieces, waits):
    out = jax.ShapeDtypeStruct((len(pieces),) + pieces[0].shape, pieces[0].dtype)
    specs = [whole(piece) for piece in pieces]
    return run(pack_kernel, [], pieces, specs, waits, out, whole(out), name="pack")


def add_kernel(*refs):
    total = refs[0][...]
    for ref in refs[1:-1]:
        total = total + ref[...]
    refs[-1][...] = total


def add_up(arrays, waits):
    out = jax.ShapeDtypeStruct(arrays[0].shape, arrays[0].dtype)
    specs = [whole(array) for array in arrays]
    return run(add_kernel, [], arrays, specs, waits, out, whole(out), name="add_up")


def is_listed(ancestors, number, block):
    found = ancestors[number, 0] == block
    for i in range(1, ancestors.shape[1]):
        found = found | (ancestors[number, i] == block)
    return found


def partial_kernel(sides, ratio, count, number, block, group, place, slots, ancestors, tile_ref, *refs):
    piece_refs, out_refs = refs[:sides], refs[sides:-2]
    right_high, right_low = refs[-2:]
    chunk_rows, columns = out_refs[0].shape
    blocks = tile_ref.shape[1] // block
    step = pl.program_id(0)

    def listed(block):
        return is_listed(ancestors, number, block)

    @pl.when(step == 0)
    def _assemble():
        if len(piece_refs) == 1:
            right_high[...], right_low[...] = halves(piece_refs[0][...])
            return
        for side, ref in enumerate(piece_refs):
            chips, parts, unit_rows, width = ref.shape
            for o in range(chips):
                owner = place[0] ^ (2 * (group + o) + side)
                lane = owner // ratio % (columns // width) * width
                lanes = pl.ds(pl.multiple_of(lane, width), width)
                first = owner % ratio * (parts * unit_rows)
                rows = pl.ds(pl.multiple_of(first, parts * unit_rows), parts * unit_rows)
                high, low = halves(ref[o].reshape(parts * unit_rows, width))
                right_high[rows, lanes] = high
                right_low[rows, lanes] = low

    def multiply(out_ref):
        out_ref[...] = jnp.zeros_like(out_ref)
        chunk = place[0] * count + slots[place[1], step]

        @pl.when(listed(chunk * chunk_rows // block))
        def _chunk():
            def add(index, carry):
                @pl.when(listed(place[1] * blocks + index))
                def _block():
                    span = pl.ds(pl.multiple_of(index * block, block), block)
                    high, low = halves(tile_ref[:, span])
                    right = right_high[span, :]
                    dot = functools.partial(jnp.dot, preferred_element_type=jnp.float32)
                    out_ref[...] += dot(high, right) + (
                        dot(high, right_low[span, :]) + dot(low, right)
                    )

                return carry

            lax.fori_loop(0, blocks, add, 0)

    for index, out_ref in enumerate(out_refs):
        pl.when(step == index)(functools.partial(multiply, out_ref))


def partial_product(
    place, slots, ancestors, tiles, pieces, ratio, columns, number, group, block, waits
):
    rows, cols = tiles.shape
    count = slots.shape[0]
    out = jax.ShapeDtypeStruct((rows // count, columns), jnp.float32)
    tile = pl.BlockSpec((rows // count, cols), lambda i, p, s, a: (s[p[1], i], 0))
    return run(
        functools.partial(partial_kernel, len(pieces), ratio, count, number, block, group),
        [place, slots, ancestors],
        [tiles] + pieces,
        [tile] + [whole(piece) for piece in pieces],
        waits,
        [out] * count,
        [whole(out)] * count,
        grid=(count,),
        scratch=[pltpu.VMEM((cols, columns), jnp.bfloat16)] * 2,
        name="partial_product",
    )


def dot(left, right, side=1):
    def one(a, b):
        return lax.dot_general(
            a, b, (((side,), (0,)), ((), ())), preferred_element_type=jnp.float32
        )

    left_high, left_low = halves(left)
    right_high, right_low = halves(right)
    return one(left_high, right_high) + (one(left_high, right_low) + one(left_low, right_high))


def part_by_core(place, matrix_ref, index, keep_ref, send_ref):
    _, chips, rows, _ = keep_ref.shape
    core = place[0] % 2
    for chip in range(chips):
        for ref, side in ((keep_ref, core), (send_ref, 1 - core)):
            first = pl.multiple_of((chip * 2 + side) * rows, rows)
            ref[index, chip] = matrix_ref[pl.ds(first, rows), :]


def finish_kernel(number, last, first, block, group_count, count, place, ancestors, *refs):
    refs = list(refs)
    sums = [[refs.pop(0) for _ in range(4)] for _ in range(group_count)]
    factor_ref = refs.pop(0)
    if not first:
        old_rest, old_rows, _ = (refs.pop(0) for _ in range(3))
    if not last:
        link_ref, next_ref = refs.pop(0), refs.pop(0)
    offdiag_ref, keep_ref, send_ref = (refs.pop(0) for _ in range(3))
    if not last:
        cross_ref, kept_ref = refs.pop(0), refs.pop(0)
    part_ref, summed_ref = refs
    offdiag_ref[...] = jnp.zeros_like(offdiag_ref)
    part_ref[...] = jnp.zeros_like(part_ref) if first else old_rest[...]

    own = block(place)

    @pl.when(is_listed(ancestors, number, own))
    def _own():
        for group, (one, two, three, four) in enumerate(sums):
            width = one.shape[1]
            lane = (place[2] // (count // group_count) ^ group) * width
            total = ((one[...] + two[...]) + three[...]) + four[...]
            summed_ref[:, pl.ds(pl.multiple_of(lane, width), width)] = total
        summed = summed_ref[...]
        part_ref[...] += dot(factor_ref[0], summed, 0)
        offdiag_ref[0] = -(summed if first else summed + old_rows[...])

    part_by_core(place, part_ref, 0, keep_ref, send_ref)
    if last:
        return
    cross_ref[...] = jnp.zeros_like(cross_ref)

    @pl.when(is_listed(ancestors, number + 1, own))
    def _cross():
        cross_ref[...] = dot(offdiag_ref[0], next_ref[0], 0)

    kept_ref[...] = cross_ref[...] + dot(part_ref[...], link_ref[0])
    part_by_core(place, kept_ref, 1, keep_ref, send_ref)


def rest_kernel(link_ref, cross_ref, part_ref, offdiag_ref, rest_ref, rows_ref):
    link = link_ref[0]
    rest_ref[...] = dot(cross_ref[...], link, 0) + dot(link, part_ref[...], 0)
    rows_ref[...] = dot(offdiag_ref[0], link)


def rest_of(link_factor, cross, link_part, offdiag, number):
    _, unit_rows, columns = offdiag.shape
    link = pl.BlockSpec((1, columns, columns), lambda *_: (number, 0, 0))
    rows = pl.BlockSpec((1, unit_rows, columns), lambda *_: (number, 0, 0))
    outs = [cross, jax.ShapeDtypeStruct((unit_rows, columns), jnp.float32)]
    outs = [jax.ShapeDtypeStruct(out.shape, jnp.float32) for out in outs]
    return run(
        rest_kernel, [], [link_factor, cross, link_part, offdiag],
        [link, whole(cross), whole(link_part), rows], [], outs, [whole(out) for out in outs],
        name="rest",
    )


def finish(number, block, place, ancestors, groups, factor, before, link_factor, count, chips, waits):
    nsuper, unit_rows, columns = factor.shape
    first, last = number == 0, number + 1 == nsuper
    slab = (1, unit_rows, columns)
    arrays = [array for sums in groups for array in sums]
    specs = [whole(array) for array in arrays]
    arrays.append(factor)
    specs.append(pl.BlockSpec(slab, lambda *_: (number, 0, 0)))
    alias = {}
    if not first:
        alias = {2 + len(arrays) + 2: 0}
        arrays += before
        specs += [whole(before[0]), whole(before[1])]
        specs.append(pl.BlockSpec((1, 8, LANES), lambda *_: (0, 0, 0)))
    if not last:
        arrays += [link_factor, factor]
        specs.append(pl.BlockSpec((1, columns, columns), lambda *_: (number, 0, 0)))
        specs.append(pl.BlockSpec(slab, lambda *_: (number + 1, 0, 0)))
    shape = jax.ShapeDtypeStruct
    parts = shape((1 if last else 2, chips, columns // (2 * chips), columns), jnp.float32)
    outs = [shape(factor.shape, jnp.float32), parts, parts]
    out_specs = [pl.BlockSpec(slab, lambda *_: (number, 0, 0)), whole(parts), whole(parts)]
    if not last:
        more = [shape((columns, columns), jnp.float32)] * 2
        outs += more
        out_specs += [whole(array) for array in more]
    return run(
        functools.partial(finish_kernel, number, last, first, block, len(groups), count),
        [place, ancestors],
        arrays,
        specs,
        waits,
        outs,
        out_specs,
        scratch=[pltpu.VMEM((rows, columns), jnp.float32) for rows in (columns, unit_rows)],
        alias=alias,
        name="finish",
    )


def fold_kernel(place, keep_ref, received_ref, *out_refs):
    chip = place[0] // 2
    for o, out_ref in enumerate(out_refs):
        out_ref[...] = keep_ref[:, chip ^ o] + received_ref[:, chip ^ o]


def fold(place, keep, received, waits):
    number, chips, rows, columns = keep.shape
    out = jax.ShapeDtypeStruct((number, rows, columns), jnp.float32)
    specs = [whole(keep)] * 2
    outs = [out] * chips
    return run(
        fold_kernel, [place], [keep, received], specs, waits, outs, [whole(out)] * chips,
        name="fold",
    )


def fold_pair_kernel(place, *refs):
    *piece_refs, kept_ref, other_ref = refs
    mine = place[1] % 2
    for out_ref, index in ((kept_ref, mine), (other_ref, 1 - mine)):
        total = piece_refs[0][index]
        for ref in piece_refs[1:]:
            total = total + ref[index]
        out_ref[...] = total


def fold_pair(place, pieces):
    out = jax.ShapeDtypeStruct(pieces[0].shape[1:], jnp.float32)
    specs = [whole(piece) for piece in pieces]
    return run(
        fold_pair_kernel, [place], pieces, specs, [], [out] * 2, [whole(out)] * 2, name="fold_pair"
    )


def bases_kernel(nsuper, place, diag_ref, link_ref, *refs):
    diag_out, link_out, base_ref, next_ref = refs
    rows = diag_out.shape[1]
    mine = pl.ds(pl.multiple_of(place[0] * rows, rows), rows)
    base_ref[...] = diag_ref[0]
    diag_out[0] = base_ref[mine, :]
    for number in range(1, nsuper):
        link = link_ref[number - 1]
        next_ref[...] = dot(base_ref[...], link)
        link_out[number - 1] = next_ref[mine, :]
        base_ref[...] = diag_ref[number] + dot(link, next_ref[...], 0)
        diag_out[number] = base_ref[mine, :]


def bases_of(place, diag_inverse, link_factor, rows, waits):
    nsuper, columns, _ = diag_inverse.shape
    outs = [
        jax.ShapeDtypeStruct((nsuper, rows, columns), jnp.float32),
        jax.ShapeDtypeStruct((nsuper - 1, rows, columns), jnp.float32),
    ]
    return run(
        functools.partial(bases_kernel, nsuper),
        [place],
        [diag_inverse, link_factor],
        [whole(diag_inverse), whole(link_factor)],
        waits,
        outs,
        [whole(out) for out in outs],
        scratch=[pltpu.VMEM((columns, columns), jnp.float32)] * 2,
        name="bases",
    )


def outputs_kernel(place, *refs):
    diag_base, link_base, *sums, diag_out, link_out = refs
    steps = link_out.shape[0]
    for number in range(steps):
        pair = sums[2 * number : 2 * number + 2]

        def put(diag, link, number=number):
            diag_out[number] = diag[...] + diag_base[number]
            link_out[number] = -(link[...] + link_base[number])

        pl.when(place[1] % 2 == 0)(functools.partial(put, *pair))
        pl.when(place[1] % 2 == 1)(functools.partial(put, *pair[::-1]))
    diag_out[steps] = sums[-2][0] + sums[-1][0] + diag_base[steps]


def outputs(place, bases, sums):
    arrays = list(bases) + sums
    specs = [whole(array) for array in arrays]
    outs = [jax.ShapeDtypeStruct(base.shape, jnp.float32) for base in bases]
    return run(outputs_kernel, [place], arrays, specs, [], outs, specs[:2], name="outputs")


def to_column(pieces, ratio):
    return [pieces[0]] + [flip(pieces[o], "pcol", o * ratio) for o in range(1, len(pieces))]


def to_plane(pieces):
    return [pieces[0]] + [flip(pieces[o], "prow", o) for o in range(1, len(pieces))]


def to_plane_whole(factor, count, ratio):
    pieces = jnp.swapaxes(factor.reshape(factor.shape[0], count, -1), 0, 1)
    groups = [[c * ratio + k for c in range(count)] for k in range(ratio)]
    spread = lax.all_to_all(pieces, "pcol", 0, 0, axis_index_groups=groups)
    return lax.all_to_all(spread, "prow", 0, 0)


def gather_plane(own, pcol_count):
    return [own] + [flip(own, "pcol", offset) for offset in range(2, pcol_count, 2)]


def in_rows(gathered, count, ratio):
    _, _, unit_rows, width = gathered.shape
    split = gathered.reshape(count, ratio, count, unit_rows, width)
    rows = jnp.transpose(split, (1, 2, 3, 0, 4))
    return rows.reshape(ratio * count * unit_rows, count * width)


FOUR_SLOTS = ((3, 2, 1, 0), (2, 0, 3, 1), (1, 3, 0, 2), (0, 1, 2, 3))


def slots_of(count):
    return FOUR_SLOTS if count == len(FOUR_SLOTS) else (tuple(range(count)),) * count


def sum_over_four(slots):
    near = lax.ppermute(slots[0], "prow", [(0, 1), (3, 2)])
    total = lax.ppermute(slots[1], "prow", [(0, 2), (2, 3), (3, 1), (1, 0)])
    middle = lax.ppermute(slots[0], "prow", [(1, 2), (2, 1)])
    both = add_up([slots[2], near], [])
    last = lax.ppermute(both, "prow", [(1, 3), (2, 0), (0, 1), (3, 2)])
    return [slots[3], total, middle, last, near]


def sum_over_line(slots, z):
    count = len(slots)
    if count == len(FOUR_SLOTS):
        return sum_over_four(slots)
    chunks = jnp.stack(slots)

    def chunk(index):
        return lax.dynamic_index_in_dim(chunks, jnp.clip(index, 0, count - 1), 0, keepdims=False)

    up = down = None
    for t in range(1, count):
        up_send, down_send = chunk(z + count - t), chunk(z + t - count)
        if up is not None:
            up_send, down_send = up_send + up, down_send + down
        up = lax.ppermute(up_send, "prow", [(i, i + 1) for i in range(min(t, count - 1))])
        down = lax.ppermute(
            down_send, "prow", [(i, i - 1) for i in range(max(count - t, 1), count)]
        )
    mine = chunk(z)
    none = jnp.zeros_like(mine)
    return [mine, none if up is None else up, none if down is None else down, none, mine]


def sum_plane(place, keep, send, waits):
    pieces = fold(place, keep, flip(send, "pcol", 1), waits)
    return [pieces[0]] + [flip(pieces[o], "pcol", 2 * o) for o in range(1, len(pieces))]


def sum_planes(pieces, count):
    bit = 1
    while True:
        total = add_up(pieces, [])
        if bit >= count:
            return [total, jnp.zeros_like(total)]
        pieces = [total, flip(total, "prow", bit)]
        bit *= 2
        if bit >= count:
            return pieces


def sum_pair_near(place, pieces):
    kept, other = fold_pair(place, pieces)
    return [kept, flip(other, "prow", 1)]


def sum_pair_far(pieces, count, waits):
    bit = 2
    while True:
        total = add_up(pieces, waits)
        if bit >= count:
            return [total, flip(total, "prow", 1)]
        pieces, waits = [total, flip(total, "prow", bit)], []
        bit *= 2


def body(inverse_tiles, factor, link_factor, diag_inverse, ancestors):
    row_count, col_count = inverse_tiles.shape
    nsuper, unit_rows, columns = factor.shape
    count = lax.axis_size("prow")
    pcol_count = lax.axis_size("pcol")
    ratio = col_count // row_count
    z = lax.axis_index("prow")
    pcol_index = lax.axis_index("pcol")
    width = columns // count
    place = jnp.stack([pcol_index, z, pcol_index // ratio]).astype(jnp.int32)
    slots = jnp.asarray(slots_of(count), jnp.int32)

    def own_block(place):
        return (place[0] * count + place[1]) * unit_rows // columns

    received = []
    if width % LANES == 0:
        sent = to_column(cut(place, factor, count), ratio)
        for number in range(nsuper):
            waits = received[-1][1:] if received else []
            received.append(to_plane(turn(place, sent, number, waits)))
    chips = pcol_count // 2
    waits = received[0][1:2] if received else []
    bases = bases_of(place, diag_inverse, link_factor, columns // pcol_count, waits)
    rows, gathered, early = [], [], []
    for number in range(nsuper):
        rows.append([])
        group_count = 2 if number == 0 and received and count % 2 == 0 and chips % 2 == 0 else 1
        if received:
            own = arrange(place, received[number], gathered)
            found = gather_plane(own, pcol_count)
            gathered = found[1:]
            others = [piece for later in received[number + 1 : number + 2] for piece in later[1:]]
        for group in range(group_count):
            waits = []
            if received:
                size = chips // group_count
                if not group:
                    waits, early = early + others, []
                if group:
                    waits = waits + [rows[-1][-1][3]]
                elif group_count > 1:
                    waits = waits + found[size : size + 1]
                packed = pack(found[group * size : (group + 1) * size], waits)
                pieces = [packed, flip(packed, "pcol", 1)]
            else:
                own = to_plane_whole(factor[number], count, ratio)
                pieces = [in_rows(lax.all_gather(own, "pcol", axis=0), count, ratio)]
            waits = [bases[0]] if group + 1 == group_count else []
            if number and not group:
                waits.append(rows[-2][-1][4])
            for earlier in rows[-1]:
                waits += earlier[1:4]
                early.append(earlier[4])
            partial = partial_product(
                place, slots, ancestors, inverse_tiles, pieces, ratio, columns // group_count,
                number, group * (chips // group_count), columns, waits,
            )
            *three, last_row, near = sum_over_line(partial, z)
            rows[-1].append([*three, near, last_row])
        early = early + rows[-1][-1][1:4]

    sums, before, pending = [], [], []
    for number in range(nsuper):
        last = number + 1 == nsuper
        waits = [] if last else rows[number + 1][0][1:4]
        groups = [sums_of[:3] + sums_of[4:] for sums_of in rows[number]]
        offdiag, keep, send, *link = finish(
            number, own_block, place, ancestors, groups, factor, before, link_factor, count, chips,
            waits + pending[:1],
        )
        if pending:
            sums += sum_pair_far(pending, count, [keep])
        waits = []
        if not last:
            rest = rest_of(link_factor, *link, offdiag, number)
            before = [*rest, offdiag]
            waits = [rest[0]]
        group = sum_plane(place, keep, send, waits)
        pending = [] if last else sum_pair_near(place, group)
    sums += sum_planes(group, count)
    return (offdiag, *outputs(place, bases, sums))


def solution(mesh):
    in_specs = (P("pcol", "prow"), P(None, ("pcol", "prow"), None), P(), P(), P())
    out_specs = (P(None, ("pcol", "prow"), None), P(None, "pcol", None), P(None, "pcol", None))
    return jax.shard_map(body, mesh=mesh, in_specs=in_specs, out_specs=out_specs, check_vma=False)
```

```python
import functools

import jax
import jax.numpy as jnp
from jax import lax
from jax.experimental import pallas as pl
from jax.experimental.pallas import tpu as pltpu
from jax.sharding import PartitionSpec as P

BOTH = ("prow", "pcol")
VMEM_LIMIT = 32 * 1024 * 1024
LANES = 128


def halves(value):
    high = value.astype(jnp.bfloat16)
    low = (value - high.astype(jnp.float32)).astype(jnp.bfloat16)
    return high, low


def flip(value, axis, bit):
    return lax.ppermute(value, axis, [(i, i ^ bit) for i in range(lax.axis_size(axis))])


def run(
    kernel, scalars, arrays, specs, waits, outs, out_specs, grid=(1,), scratch=(), alias=None, name=None
):
    def corner(array):
        block = (1,) * (array.ndim - 2) + (8, LANES)
        return pl.BlockSpec(block, lambda *_: (0,) * array.ndim)

    def body(*refs):
        first = len(scalars) + len(arrays)
        kernel(*refs[:first], *refs[first + len(waits) :])

    return pl.pallas_call(
        body,
        grid_spec=pltpu.PrefetchScalarGridSpec(
            num_scalar_prefetch=len(scalars),
            grid=grid,
            in_specs=list(specs) + [corner(array) for array in waits],
            out_specs=out_specs,
            scratch_shapes=list(scratch),
        ),
        out_shape=outs,
        input_output_aliases=alias or {},
        compiler_params=pltpu.CompilerParams(vmem_limit_bytes=VMEM_LIMIT),
        cost_estimate=pl.CostEstimate(flops=0, bytes_accessed=0, transcendentals=0),
        name=name,
    )(*scalars, *arrays, *waits)


def whole(array):
    return pl.BlockSpec(array.shape, lambda *_: (0,) * array.ndim)


def cut_kernel(place, factor_ref, *out_refs):
    width = out_refs[0].shape[1]
    for o, out_ref in enumerate(out_refs):
        start = pl.multiple_of((place[2] ^ o) * width, width)
        out_ref[...] = factor_ref[0, :, pl.ds(start, width)]


def cut(place, factor, number, count, waits):
    _, unit_rows, columns = factor.shape
    piece = jax.ShapeDtypeStruct((unit_rows, columns // count), factor.dtype)
    spec = pl.BlockSpec((1, unit_rows, columns), lambda *_: (number, 0, 0))
    outs = [piece] * count
    specs = [whole(piece)] * count
    return run(cut_kernel, [place], [factor], [spec], waits, outs, specs, name="cut")


def turn_kernel(place, *refs):
    count = len(refs) // 2
    for shift in range(count):

        @pl.when((place[1] ^ place[2]) == shift)
        def _copy(shift=shift):
            for o in range(count):
                refs[count + o][...] = refs[o ^ shift][...]


def turn(place, pieces, waits):
    count = len(pieces)
    piece = jax.ShapeDtypeStruct(pieces[0].shape, pieces[0].dtype)
    specs = [whole(piece)] * count
    return run(turn_kernel, [place], pieces, specs, waits, [piece] * count, specs, name="turn")


def arrange_kernel(place, *refs):
    out_ref = refs[-1]
    for o, piece_ref in enumerate(refs[:-1]):
        out_ref[place[1] ^ o] = piece_ref[...]


def arrange(place, pieces, waits):
    out = jax.ShapeDtypeStruct((len(pieces),) + pieces[0].shape, pieces[0].dtype)
    specs = [whole(piece) for piece in pieces]
    return run(arrange_kernel, [place], pieces, specs, waits, out, whole(out), name="arrange")


def pack_kernel(*refs):
    for index, ref in enumerate(refs[:-1]):
        refs[-1][index] = ref[...]


def pack(pieces, waits):
    out = jax.ShapeDtypeStruct((len(pieces),) + pieces[0].shape, pieces[0].dtype)
    specs = [whole(piece) for piece in pieces]
    return run(pack_kernel, [], pieces, specs, waits, out, whole(out), name="pack")


def add_kernel(*refs):
    total = refs[0][...]
    for ref in refs[1:-1]:
        total = total + ref[...]
    refs[-1][...] = total


def add_up(arrays, waits):
    out = jax.ShapeDtypeStruct(arrays[0].shape, arrays[0].dtype)
    specs = [whole(array) for array in arrays]
    return run(add_kernel, [], arrays, specs, waits, out, whole(out), name="add_up")


def is_listed(ancestors, number, block):
    found = ancestors[number, 0] == block
    for i in range(1, ancestors.shape[1]):
        found = found | (ancestors[number, i] == block)
    return found


def partial_kernel(sides, ratio, count, number, place, slots, ancestors, tile_ref, *refs):
    piece_refs, out_refs, right_ref = refs[:sides], refs[sides:-1], refs[-1]
    chunk_rows, columns = out_refs[0].shape
    blocks = tile_ref.shape[1] // columns
    step = pl.program_id(0)

    def listed(block):
        return is_listed(ancestors, number, block)

    @pl.when(step == 0)
    def _assemble():
        def put(first, lanes, value):
            high, low = halves(value)
            for index in range(value.shape[0] // columns):
                part = slice(index * columns, (index + 1) * columns)
                for turn, side in enumerate((high, low, high)):
                    right_ref[first + index, pl.ds(turn * columns, columns), lanes] = side[part]

        if len(piece_refs) == 1:
            put(0, slice(None), piece_refs[0][...])
            return
        for side, ref in enumerate(piece_refs):
            chips, parts, unit_rows, width = ref.shape
            span = parts * unit_rows
            for o in range(chips):
                owner = place[0] ^ (2 * o + side)
                lanes = pl.ds(pl.multiple_of(owner // ratio * width, width), width)
                put(owner % ratio * (span // columns), lanes, ref[o].reshape(span, width))

    def multiply(out_ref):
        out_ref[...] = jnp.zeros_like(out_ref)
        chunk = place[0] * count + slots[place[1], step]

        @pl.when(listed(chunk * chunk_rows // columns))
        def _chunk():
            def add(block, carry):
                @pl.when(listed(place[1] * blocks + block))
                def _block():
                    span = pl.ds(pl.multiple_of(block * columns, columns), columns)
                    high, low = halves(tile_ref[:, span])
                    left = jnp.concatenate([high, high, low], axis=1)
                    out_ref[...] += jnp.dot(
                        left, right_ref[block], preferred_element_type=jnp.float32
                    )

                return carry

            lax.fori_loop(0, blocks, add, 0)

    for index, out_ref in enumerate(out_refs):
        pl.when(step == index)(functools.partial(multiply, out_ref))


def partial_product(place, slots, ancestors, tiles, pieces, ratio, columns, number, waits):
    rows, cols = tiles.shape
    count = slots.shape[0]
    out = jax.ShapeDtypeStruct((rows // count, columns), jnp.float32)
    tile = pl.BlockSpec((rows // count, cols), lambda i, p, s, a: (s[p[1], i], 0))
    return run(
        functools.partial(partial_kernel, len(pieces), ratio, count, number),
        [place, slots, ancestors],
        [tiles] + pieces,
        [tile] + [whole(piece) for piece in pieces],
        waits,
        [out] * count,
        [whole(out)] * count,
        grid=(count,),
        scratch=[pltpu.VMEM((cols // columns, 3 * columns, columns), jnp.bfloat16)],
        name="partial_product",
    )


def dot(left, right, side=1):
    def one(a, b):
        return lax.dot_general(
            a, b, (((side,), (0,)), ((), ())), preferred_element_type=jnp.float32
        )

    left_high, left_low = halves(left)
    right_high, right_low = halves(right)
    return one(left_high, right_high) + (one(left_high, right_low) + one(left_low, right_high))


def part_by_core(place, matrix_ref, index, keep_ref, send_ref):
    _, chips, rows, _ = keep_ref.shape
    core = place[0] % 2
    for chip in range(chips):
        for ref, side in ((keep_ref, core), (send_ref, 1 - core)):
            first = pl.multiple_of((chip * 2 + side) * rows, rows)
            ref[index, chip] = matrix_ref[pl.ds(first, rows), :]


def finish_kernel(number, last, first, block, place, ancestors, *refs):
    refs = list(refs)
    sums, factor_ref = [refs.pop(0) for _ in range(4)], refs.pop(0)
    if not first:
        old_rest, old_rows, _ = (refs.pop(0) for _ in range(3))
    if not last:
        link_ref, next_ref = refs.pop(0), refs.pop(0)
    offdiag_ref, keep_ref, send_ref = (refs.pop(0) for _ in range(3))
    if not last:
        cross_ref, kept_ref = refs.pop(0), refs.pop(0)
    part_ref = refs.pop(0)
    offdiag_ref[...] = jnp.zeros_like(offdiag_ref)
    part_ref[...] = jnp.zeros_like(part_ref) if first else old_rest[...]

    own = block(place)

    @pl.when(is_listed(ancestors, number, own))
    def _own():
        summed = ((sums[0][...] + sums[1][...]) + sums[2][...]) + sums[3][...]
        part_ref[...] += dot(factor_ref[0], summed, 0)
        offdiag_ref[0] = -(summed if first else summed + old_rows[...])

    part_by_core(place, part_ref, 0, keep_ref, send_ref)
    if last:
        return
    cross_ref[...] = jnp.zeros_like(cross_ref)

    @pl.when(is_listed(ancestors, number + 1, own))
    def _cross():
        cross_ref[...] = dot(offdiag_ref[0], next_ref[0], 0)

    kept_ref[...] = cross_ref[...] + dot(part_ref[...], link_ref[0])
    part_by_core(place, kept_ref, 1, keep_ref, send_ref)


def rest_kernel(link_ref, cross_ref, part_ref, offdiag_ref, rest_ref, rows_ref):
    link = link_ref[0]
    rest_ref[...] = dot(cross_ref[...], link, 0) + dot(link, part_ref[...], 0)
    rows_ref[...] = dot(offdiag_ref[0], link)


def rest_of(link_factor, cross, link_part, offdiag, number):
    _, unit_rows, columns = offdiag.shape
    link = pl.BlockSpec((1, columns, columns), lambda *_: (number, 0, 0))
    rows = pl.BlockSpec((1, unit_rows, columns), lambda *_: (number, 0, 0))
    outs = [cross, jax.ShapeDtypeStruct((unit_rows, columns), jnp.float32)]
    outs = [jax.ShapeDtypeStruct(out.shape, jnp.float32) for out in outs]
    return run(
        rest_kernel, [], [link_factor, cross, link_part, offdiag],
        [link, whole(cross), whole(link_part), rows], [], outs, [whole(out) for out in outs],
        name="rest",
    )


def finish(number, block, place, ancestors, sums, factor, before, link_factor, chips, waits):
    nsuper, unit_rows, columns = factor.shape
    first, last = number == 0, number + 1 == nsuper
    slab = (1, unit_rows, columns)
    arrays, specs = list(sums), [whole(array) for array in sums]
    arrays.append(factor)
    specs.append(pl.BlockSpec(slab, lambda *_: (number, 0, 0)))
    alias = {}
    if not first:
        alias = {2 + len(arrays) + 2: 0}
        arrays += before
        specs += [whole(before[0]), whole(before[1])]
        specs.append(pl.BlockSpec((1, 8, LANES), lambda *_: (0, 0, 0)))
    if not last:
        arrays += [link_factor, factor]
        specs.append(pl.BlockSpec((1, columns, columns), lambda *_: (number, 0, 0)))
        specs.append(pl.BlockSpec(slab, lambda *_: (number + 1, 0, 0)))
    shape = jax.ShapeDtypeStruct
    groups = shape((1 if last else 2, chips, columns // (2 * chips), columns), jnp.float32)
    outs = [shape(factor.shape, jnp.float32), groups, groups]
    out_specs = [pl.BlockSpec(slab, lambda *_: (number, 0, 0)), whole(groups), whole(groups)]
    if not last:
        more = [shape((columns, columns), jnp.float32)] * 2
        outs += more
        out_specs += [whole(array) for array in more]
    return run(
        functools.partial(finish_kernel, number, last, first, block),
        [place, ancestors],
        arrays,
        specs,
        waits,
        outs,
        out_specs,
        scratch=[pltpu.VMEM((columns, columns), jnp.float32)],
        alias=alias,
        name="finish",
    )


def fold_kernel(place, keep_ref, received_ref, *out_refs):
    chip = place[0] // 2
    for o, out_ref in enumerate(out_refs):
        out_ref[...] = keep_ref[:, chip ^ o] + received_ref[:, chip ^ o]


def fold(place, keep, received, waits):
    number, chips, rows, columns = keep.shape
    out = jax.ShapeDtypeStruct((number, rows, columns), jnp.float32)
    specs = [whole(keep)] * 2
    outs = [out] * chips
    return run(
        fold_kernel, [place], [keep, received], specs, waits, outs, [whole(out)] * chips,
        name="fold",
    )


def fold_pair_kernel(place, *refs):
    *piece_refs, kept_ref, other_ref = refs
    mine = place[1] % 2
    for out_ref, index in ((kept_ref, mine), (other_ref, 1 - mine)):
        total = piece_refs[0][index]
        for ref in piece_refs[1:]:
            total = total + ref[index]
        out_ref[...] = total


def fold_pair(place, pieces):
    out = jax.ShapeDtypeStruct(pieces[0].shape[1:], jnp.float32)
    specs = [whole(piece) for piece in pieces]
    return run(
        fold_pair_kernel, [place], pieces, specs, [], [out] * 2, [whole(out)] * 2, name="fold_pair"
    )


def bases_kernel(nsuper, place, diag_ref, link_ref, *refs):
    diag_out, link_out, base_ref, next_ref = refs
    rows = diag_out.shape[1]
    mine = pl.ds(pl.multiple_of(place[0] * rows, rows), rows)
    base_ref[...] = diag_ref[0]
    diag_out[0] = base_ref[mine, :]
    for number in range(1, nsuper):
        link = link_ref[number - 1]
        next_ref[...] = dot(base_ref[...], link)
        link_out[number - 1] = next_ref[mine, :]
        base_ref[...] = diag_ref[number] + dot(link, next_ref[...], 0)
        diag_out[number] = base_ref[mine, :]


def bases_of(place, diag_inverse, link_factor, rows, waits):
    nsuper, columns, _ = diag_inverse.shape
    outs = [
        jax.ShapeDtypeStruct((nsuper, rows, columns), jnp.float32),
        jax.ShapeDtypeStruct((nsuper - 1, rows, columns), jnp.float32),
    ]
    return run(
        functools.partial(bases_kernel, nsuper),
        [place],
        [diag_inverse, link_factor],
        [whole(diag_inverse), whole(link_factor)],
        waits,
        outs,
        [whole(out) for out in outs],
        scratch=[pltpu.VMEM((columns, columns), jnp.float32)] * 2,
        name="bases",
    )


def outputs_kernel(place, *refs):
    diag_base, link_base, *sums, diag_out, link_out = refs
    steps = link_out.shape[0]
    for number in range(steps):
        pair = sums[2 * number : 2 * number + 2]

        def put(diag, link, number=number):
            diag_out[number] = diag[...] + diag_base[number]
            link_out[number] = -(link[...] + link_base[number])

        pl.when(place[1] % 2 == 0)(functools.partial(put, *pair))
        pl.when(place[1] % 2 == 1)(functools.partial(put, *pair[::-1]))
    diag_out[steps] = sums[-2][0] + sums[-1][0] + diag_base[steps]


def outputs(place, bases, sums):
    arrays = list(bases) + sums
    specs = [whole(array) for array in arrays]
    outs = [jax.ShapeDtypeStruct(base.shape, jnp.float32) for base in bases]
    return run(outputs_kernel, [place], arrays, specs, [], outs, specs[:2], name="outputs")


def to_column(pieces, ratio):
    return [pieces[0]] + [flip(pieces[o], "pcol", o * ratio) for o in range(1, len(pieces))]


def to_plane(pieces):
    return [pieces[0]] + [flip(pieces[o], "prow", o) for o in range(1, len(pieces))]


def to_plane_whole(factor, count, ratio):
    pieces = jnp.swapaxes(factor.reshape(factor.shape[0], count, -1), 0, 1)
    groups = [[c * ratio + k for c in range(count)] for k in range(ratio)]
    spread = lax.all_to_all(pieces, "pcol", 0, 0, axis_index_groups=groups)
    return lax.all_to_all(spread, "prow", 0, 0)


def gather_plane(own, pcol_count):
    return [own] + [flip(own, "pcol", offset) for offset in range(2, pcol_count, 2)]


def in_rows(gathered, count, ratio):
    _, _, unit_rows, width = gathered.shape
    split = gathered.reshape(count, ratio, count, unit_rows, width)
    rows = jnp.transpose(split, (1, 2, 3, 0, 4))
    return rows.reshape(ratio * count * unit_rows, count * width)


FOUR_SLOTS = ((3, 2, 1, 0), (2, 0, 3, 1), (1, 3, 0, 2), (0, 1, 2, 3))


def slots_of(count):
    return FOUR_SLOTS if count == len(FOUR_SLOTS) else (tuple(range(count)),) * count


def sum_over_four(slots):
    near = lax.ppermute(slots[0], "prow", [(0, 1), (3, 2)])
    total = lax.ppermute(slots[1], "prow", [(0, 2), (2, 3), (3, 1), (1, 0)])
    middle = lax.ppermute(slots[0], "prow", [(1, 2), (2, 1)])
    both = add_up([slots[2], near], [])
    last = lax.ppermute(both, "prow", [(1, 3), (2, 0), (0, 1), (3, 2)])
    return [slots[3], total, middle, last, near]


def sum_over_line(slots, z):
    count = len(slots)
    if count == len(FOUR_SLOTS):
        return sum_over_four(slots)
    chunks = jnp.stack(slots)

    def chunk(index):
        return lax.dynamic_index_in_dim(chunks, jnp.clip(index, 0, count - 1), 0, keepdims=False)

    up = down = None
    for t in range(1, count):
        up_send, down_send = chunk(z + count - t), chunk(z + t - count)
        if up is not None:
            up_send, down_send = up_send + up, down_send + down
        up = lax.ppermute(up_send, "prow", [(i, i + 1) for i in range(min(t, count - 1))])
        down = lax.ppermute(
            down_send, "prow", [(i, i - 1) for i in range(max(count - t, 1), count)]
        )
    mine = chunk(z)
    none = jnp.zeros_like(mine)
    return [mine, none if up is None else up, none if down is None else down, none, mine]


def sum_plane(place, keep, send, waits):
    pieces = fold(place, keep, flip(send, "pcol", 1), waits)
    return [pieces[0]] + [flip(pieces[o], "pcol", 2 * o) for o in range(1, len(pieces))]


def sum_planes(pieces, count):
    bit = 1
    while True:
        total = add_up(pieces, [])
        if bit >= count:
            return [total, jnp.zeros_like(total)]
        pieces = [total, flip(total, "prow", bit)]
        bit *= 2
        if bit >= count:
            return pieces


def sum_pair_near(place, pieces):
    kept, other = fold_pair(place, pieces)
    return [kept, flip(other, "prow", 1)]


def sum_pair_far(pieces, count, waits):
    bit = 2
    while True:
        total = add_up(pieces, waits)
        if bit >= count:
            return [total, flip(total, "prow", 1)]
        pieces, waits = [total, flip(total, "prow", bit)], []
        bit *= 2


def body(inverse_tiles, factor, link_factor, diag_inverse, ancestors):
    row_count, col_count = inverse_tiles.shape
    nsuper, unit_rows, columns = factor.shape
    count = lax.axis_size("prow")
    pcol_count = lax.axis_size("pcol")
    ratio = col_count // row_count
    z = lax.axis_index("prow")
    pcol_index = lax.axis_index("pcol")
    width = columns // count
    place = jnp.stack([pcol_index, z, pcol_index // ratio]).astype(jnp.int32)
    slots = jnp.asarray(slots_of(count), jnp.int32)

    def own_block(place):
        return (place[0] * count + place[1]) * unit_rows // columns

    sent, turned, received, waits = [], [], [], []
    if width % LANES == 0:
        for number in range(nsuper):
            sent.append(to_column(cut(place, factor, number, count, waits), ratio))
            waits = received[-1][1:] if received else []
            turned.append(turn(place, sent[number], waits))
            waits = [turned[0][0]]
            received.append(to_plane(turned[number]))
    bases = bases_of(place, diag_inverse, link_factor, columns // pcol_count, [piece[0] for piece in turned[:1]])
    rows, gathered = [], [bases[0]]
    for number in range(nsuper):
        if received:
            gathered += [piece for later in sent[number + 1 : number + 2] for piece in later[1:]]
            own = arrange(place, received[number], gathered)
            found = gather_plane(own, pcol_count)
            gathered = found[1:]
            waits = [piece for later in received[number + 1 : number + 2] for piece in later[1:]]
            packed = pack(found, waits + (rows[-1][1:4] if rows else []))
            pieces = [packed, flip(packed, "pcol", 1)]
        else:
            own = to_plane_whole(factor[number], count, ratio)
            pieces = [in_rows(lax.all_gather(own, "pcol", axis=0), count, ratio)]
        partial = partial_product(
            place, slots, ancestors, inverse_tiles, pieces, ratio, columns, number, [bases[0]]
        )
        *early, last_row, near = sum_over_line(partial, z)
        rows.append([*early, near, last_row])

    sums, before, pending = [], [], []
    for number in range(nsuper):
        last = number + 1 == nsuper
        waits = [] if last else rows[number + 1][1:4]
        offdiag, keep, send, *link = finish(
            number, own_block, place, ancestors, rows[number][:3] + rows[number][4:], factor, before,
            link_factor, pcol_count // 2, waits + pending[:1],
        )
        if pending:
            sums += sum_pair_far(pending, count, [keep])
        waits = []
        if not last:
            rest = rest_of(link_factor, *link, offdiag, number)
            before = [*rest, offdiag]
            waits = [rest[0]]
        group = sum_plane(place, keep, send, waits)
        pending = [] if last else sum_pair_near(place, group)
    sums += sum_planes(group, count)
    return (offdiag, *outputs(place, bases, sums))


def solution(mesh):
    in_specs = (P("pcol", "prow"), P(None, ("pcol", "prow"), None), P(), P(), P())
    out_specs = (P(None, ("pcol", "prow"), None), P(None, "pcol", None), P(None, "pcol", None))
    return jax.shard_map(body, mesh=mesh, in_specs=in_specs, out_specs=out_specs, check_vma=False)
```

```python
import functools

import jax
import jax.numpy as jnp
from jax import lax
from jax.experimental import pallas as pl
from jax.experimental.pallas import tpu as pltpu
from jax.sharding import PartitionSpec as P

BOTH = ("prow", "pcol")
VMEM_LIMIT = 32 * 1024 * 1024
LANES = 128


def halves(value):
    high = value.astype(jnp.bfloat16)
    low = (value - high.astype(jnp.float32)).astype(jnp.bfloat16)
    return high, low


def flip(value, axis, bit):
    return lax.ppermute(value, axis, [(i, i ^ bit) for i in range(lax.axis_size(axis))])


def run(
    kernel, scalars, arrays, specs, waits, outs, out_specs, grid=(1,), scratch=(), alias=None, name=None
):
    def corner(array):
        block = (1,) * (array.ndim - 2) + (8, LANES)
        return pl.BlockSpec(block, lambda *_: (0,) * array.ndim)

    def body(*refs):
        first = len(scalars) + len(arrays)
        kernel(*refs[:first], *refs[first + len(waits) :])

    return pl.pallas_call(
        body,
        grid_spec=pltpu.PrefetchScalarGridSpec(
            num_scalar_prefetch=len(scalars),
            grid=grid,
            in_specs=list(specs) + [corner(array) for array in waits],
            out_specs=out_specs,
            scratch_shapes=list(scratch),
        ),
        out_shape=outs,
        input_output_aliases=alias or {},
        compiler_params=pltpu.CompilerParams(vmem_limit_bytes=VMEM_LIMIT),
        cost_estimate=pl.CostEstimate(flops=0, bytes_accessed=0, transcendentals=0),
        name=name,
    )(*scalars, *arrays, *waits)


def whole(array):
    return pl.BlockSpec(array.shape, lambda *_: (0,) * array.ndim)


def cut_kernel(place, factor_ref, *out_refs):
    width = out_refs[0].shape[1]
    for o, out_ref in enumerate(out_refs):
        start = pl.multiple_of((place[2] ^ o) * width, width)
        out_ref[...] = factor_ref[0, :, pl.ds(start, width)]


def cut(place, factor, number, count, waits):
    _, unit_rows, columns = factor.shape
    piece = jax.ShapeDtypeStruct((unit_rows, columns // count), factor.dtype)
    spec = pl.BlockSpec((1, unit_rows, columns), lambda *_: (number, 0, 0))
    outs = [piece] * count
    specs = [whole(piece)] * count
    return run(cut_kernel, [place], [factor], [spec], waits, outs, specs, name="cut")


def turn_kernel(place, *refs):
    count = len(refs) // 2
    for shift in range(count):

        @pl.when((place[1] ^ place[2]) == shift)
        def _copy(shift=shift):
            for o in range(count):
                refs[count + o][...] = refs[o ^ shift][...]


def turn(place, pieces, waits):
    count = len(pieces)
    piece = jax.ShapeDtypeStruct(pieces[0].shape, pieces[0].dtype)
    specs = [whole(piece)] * count
    return run(turn_kernel, [place], pieces, specs, waits, [piece] * count, specs, name="turn")


def arrange_kernel(place, *refs):
    out_ref = refs[-1]
    for o, piece_ref in enumerate(refs[:-1]):
        out_ref[place[1] ^ o] = piece_ref[...]


def arrange(place, pieces, waits):
    out = jax.ShapeDtypeStruct((len(pieces),) + pieces[0].shape, pieces[0].dtype)
    specs = [whole(piece) for piece in pieces]
    return run(arrange_kernel, [place], pieces, specs, waits, out, whole(out), name="arrange")


def pack_kernel(*refs):
    for index, ref in enumerate(refs[:-1]):
        refs[-1][index] = ref[...]


def pack(pieces, waits):
    out = jax.ShapeDtypeStruct((len(pieces),) + pieces[0].shape, pieces[0].dtype)
    specs = [whole(piece) for piece in pieces]
    return run(pack_kernel, [], pieces, specs, waits, out, whole(out), name="pack")


def add_kernel(*refs):
    total = refs[0][...]
    for ref in refs[1:-1]:
        total = total + ref[...]
    refs[-1][...] = total


def add_up(arrays, waits):
    out = jax.ShapeDtypeStruct(arrays[0].shape, arrays[0].dtype)
    specs = [whole(array) for array in arrays]
    return run(add_kernel, [], arrays, specs, waits, out, whole(out), name="add_up")


def is_listed(ancestors, number, block):
    found = ancestors[number, 0] == block
    for i in range(1, ancestors.shape[1]):
        found = found | (ancestors[number, i] == block)
    return found


def partial_kernel(sides, ratio, count, number, start, place, slots, ancestors, tile_ref, *refs):
    piece_refs, out_refs, right_ref = refs[:sides], refs[sides:-1], refs[-1]
    chunk_rows, columns = out_refs[0].shape
    blocks = tile_ref.shape[1] // columns
    step = pl.program_id(0)

    def listed(block):
        return is_listed(ancestors, number, block)

    @pl.when(step == 0)
    def _assemble():
        def put(first, lanes, value):
            high, low = halves(value)
            for index in range(value.shape[0] // columns):
                part = slice(index * columns, (index + 1) * columns)
                for turn, side in enumerate((high, low, high)):
                    right_ref[first + index, pl.ds(turn * columns, columns), lanes] = side[part]

        if len(piece_refs) == 1:
            put(0, slice(None), piece_refs[0][...])
            return
        for side, ref in enumerate(piece_refs):
            chips, parts, unit_rows, width = ref.shape
            span = parts * unit_rows
            for o in range(chips):
                owner = place[0] ^ (2 * o + side)
                lanes = pl.ds(pl.multiple_of(owner // ratio * width, width), width)
                put(owner % ratio * (span // columns), lanes, ref[o].reshape(span, width))

    def multiply(out_ref):
        out_ref[...] = jnp.zeros_like(out_ref)
        chunk = place[0] * count + slots[place[1], start + step]

        @pl.when(listed(chunk * chunk_rows // columns))
        def _chunk():
            def add(block, carry):
                @pl.when(listed(place[1] * blocks + block))
                def _block():
                    span = pl.ds(pl.multiple_of(block * columns, columns), columns)
                    high, low = halves(tile_ref[:, span])
                    left = jnp.concatenate([high, high, low], axis=1)
                    out_ref[...] += jnp.dot(
                        left, right_ref[block], preferred_element_type=jnp.float32
                    )

                return carry

            lax.fori_loop(0, blocks, add, 0)

    for index, out_ref in enumerate(out_refs):
        pl.when(step == index)(functools.partial(multiply, out_ref))


def partial_product(
    place, slots, ancestors, tiles, pieces, ratio, columns, number, start, stop, waits
):
    rows, cols = tiles.shape
    count = slots.shape[0]
    out = jax.ShapeDtypeStruct((rows // count, columns), jnp.float32)
    tile = pl.BlockSpec((rows // count, cols), lambda i, p, s, a: (s[p[1], start + i], 0))
    return run(
        functools.partial(partial_kernel, len(pieces), ratio, count, number, start),
        [place, slots, ancestors],
        [tiles] + pieces,
        [tile] + [whole(piece) for piece in pieces],
        waits,
        [out] * (stop - start),
        [whole(out)] * (stop - start),
        grid=(stop - start,),
        scratch=[pltpu.VMEM((cols // columns, 3 * columns, columns), jnp.bfloat16)],
        name="partial_product",
    )


def dot(left, right, side=1):
    def one(a, b):
        return lax.dot_general(
            a, b, (((side,), (0,)), ((), ())), preferred_element_type=jnp.float32
        )

    left_high, left_low = halves(left)
    right_high, right_low = halves(right)
    return one(left_high, right_high) + (one(left_high, right_low) + one(left_low, right_high))


def part_by_core(place, matrix_ref, index, keep_ref, send_ref):
    _, chips, rows, _ = keep_ref.shape
    core = place[0] % 2
    for chip in range(chips):
        for ref, side in ((keep_ref, core), (send_ref, 1 - core)):
            first = pl.multiple_of((chip * 2 + side) * rows, rows)
            ref[index, chip] = matrix_ref[pl.ds(first, rows), :]


def finish_kernel(number, last, first, block, place, ancestors, *refs):
    refs = list(refs)
    sums, factor_ref = [refs.pop(0) for _ in range(4)], refs.pop(0)
    if not first:
        old_rest, old_rows, _ = (refs.pop(0) for _ in range(3))
    if not last:
        link_ref, next_ref = refs.pop(0), refs.pop(0)
    offdiag_ref, keep_ref, send_ref = (refs.pop(0) for _ in range(3))
    if not last:
        cross_ref, kept_ref = refs.pop(0), refs.pop(0)
    part_ref = refs.pop(0)
    offdiag_ref[...] = jnp.zeros_like(offdiag_ref)
    part_ref[...] = jnp.zeros_like(part_ref) if first else old_rest[...]

    own = block(place)

    @pl.when(is_listed(ancestors, number, own))
    def _own():
        summed = ((sums[0][...] + sums[1][...]) + sums[2][...]) + sums[3][...]
        part_ref[...] += dot(factor_ref[0], summed, 0)
        offdiag_ref[0] = -(summed if first else summed + old_rows[...])

    part_by_core(place, part_ref, 0, keep_ref, send_ref)
    if last:
        return
    cross_ref[...] = jnp.zeros_like(cross_ref)

    @pl.when(is_listed(ancestors, number + 1, own))
    def _cross():
        cross_ref[...] = dot(offdiag_ref[0], next_ref[0], 0)

    kept_ref[...] = cross_ref[...] + dot(part_ref[...], link_ref[0])
    part_by_core(place, kept_ref, 1, keep_ref, send_ref)


def rest_kernel(link_ref, cross_ref, part_ref, offdiag_ref, rest_ref, rows_ref):
    link = link_ref[0]
    rest_ref[...] = dot(cross_ref[...], link, 0) + dot(link, part_ref[...], 0)
    rows_ref[...] = dot(offdiag_ref[0], link)


def rest_of(link_factor, cross, link_part, offdiag, number):
    _, unit_rows, columns = offdiag.shape
    link = pl.BlockSpec((1, columns, columns), lambda *_: (number, 0, 0))
    rows = pl.BlockSpec((1, unit_rows, columns), lambda *_: (number, 0, 0))
    outs = [cross, jax.ShapeDtypeStruct((unit_rows, columns), jnp.float32)]
    outs = [jax.ShapeDtypeStruct(out.shape, jnp.float32) for out in outs]
    return run(
        rest_kernel, [], [link_factor, cross, link_part, offdiag],
        [link, whole(cross), whole(link_part), rows], [], outs, [whole(out) for out in outs],
        name="rest",
    )


def finish(number, block, place, ancestors, sums, factor, before, link_factor, chips, waits):
    nsuper, unit_rows, columns = factor.shape
    first, last = number == 0, number + 1 == nsuper
    slab = (1, unit_rows, columns)
    arrays, specs = list(sums), [whole(array) for array in sums]
    arrays.append(factor)
    specs.append(pl.BlockSpec(slab, lambda *_: (number, 0, 0)))
    alias = {}
    if not first:
        alias = {2 + len(arrays) + 2: 0}
        arrays += before
        specs += [whole(before[0]), whole(before[1])]
        specs.append(pl.BlockSpec((1, 8, LANES), lambda *_: (0, 0, 0)))
    if not last:
        arrays += [link_factor, factor]
        specs.append(pl.BlockSpec((1, columns, columns), lambda *_: (number, 0, 0)))
        specs.append(pl.BlockSpec(slab, lambda *_: (number + 1, 0, 0)))
    shape = jax.ShapeDtypeStruct
    groups = shape((1 if last else 2, chips, columns // (2 * chips), columns), jnp.float32)
    outs = [shape(factor.shape, jnp.float32), groups, groups]
    out_specs = [pl.BlockSpec(slab, lambda *_: (number, 0, 0)), whole(groups), whole(groups)]
    if not last:
        more = [shape((columns, columns), jnp.float32)] * 2
        outs += more
        out_specs += [whole(array) for array in more]
    return run(
        functools.partial(finish_kernel, number, last, first, block),
        [place, ancestors],
        arrays,
        specs,
        waits,
        outs,
        out_specs,
        scratch=[pltpu.VMEM((columns, columns), jnp.float32)],
        alias=alias,
        name="finish",
    )


def fold_kernel(place, keep_ref, received_ref, *out_refs):
    chip = place[0] // 2
    for o, out_ref in enumerate(out_refs):
        out_ref[...] = keep_ref[:, chip ^ o] + received_ref[:, chip ^ o]


def fold(place, keep, received):
    number, chips, rows, columns = keep.shape
    out = jax.ShapeDtypeStruct((number, rows, columns), jnp.float32)
    specs = [whole(keep)] * 2
    outs = [out] * chips
    return run(
        fold_kernel, [place], [keep, received], specs, [], outs, [whole(out)] * chips, name="fold"
    )


def fold_pair_kernel(place, *refs):
    *piece_refs, kept_ref, other_ref = refs
    mine = place[1] % 2
    for out_ref, index in ((kept_ref, mine), (other_ref, 1 - mine)):
        total = piece_refs[0][index]
        for ref in piece_refs[1:]:
            total = total + ref[index]
        out_ref[...] = total


def fold_pair(place, pieces, waits):
    out = jax.ShapeDtypeStruct(pieces[0].shape[1:], jnp.float32)
    specs = [whole(piece) for piece in pieces]
    return run(
        fold_pair_kernel, [place], pieces, specs, waits, [out] * 2, [whole(out)] * 2,
        name="fold_pair",
    )


def bases_kernel(nsuper, place, diag_ref, link_ref, *refs):
    diag_out, link_out, base_ref, next_ref = refs
    rows = diag_out.shape[1]
    mine = pl.ds(pl.multiple_of(place[0] * rows, rows), rows)
    base_ref[...] = diag_ref[0]
    diag_out[0] = base_ref[mine, :]
    for number in range(1, nsuper):
        link = link_ref[number - 1]
        next_ref[...] = dot(base_ref[...], link)
        link_out[number - 1] = next_ref[mine, :]
        base_ref[...] = diag_ref[number] + dot(link, next_ref[...], 0)
        diag_out[number] = base_ref[mine, :]


def bases_of(place, diag_inverse, link_factor, rows, waits):
    nsuper, columns, _ = diag_inverse.shape
    outs = [
        jax.ShapeDtypeStruct((nsuper, rows, columns), jnp.float32),
        jax.ShapeDtypeStruct((nsuper - 1, rows, columns), jnp.float32),
    ]
    return run(
        functools.partial(bases_kernel, nsuper),
        [place],
        [diag_inverse, link_factor],
        [whole(diag_inverse), whole(link_factor)],
        waits,
        outs,
        [whole(out) for out in outs],
        scratch=[pltpu.VMEM((columns, columns), jnp.float32)] * 2,
        name="bases",
    )


def outputs_kernel(place, *refs):
    diag_base, link_base, *sums, diag_out, link_out = refs
    steps = link_out.shape[0]
    for number in range(steps):
        pair = sums[2 * number : 2 * number + 2]

        def put(diag, link, number=number):
            diag_out[number] = diag[...] + diag_base[number]
            link_out[number] = -(link[...] + link_base[number])

        pl.when(place[1] % 2 == 0)(functools.partial(put, *pair))
        pl.when(place[1] % 2 == 1)(functools.partial(put, *pair[::-1]))
    diag_out[steps] = sums[-2][0] + sums[-1][0] + diag_base[steps]


def outputs(place, bases, sums):
    arrays = list(bases) + sums
    specs = [whole(array) for array in arrays]
    outs = [jax.ShapeDtypeStruct(base.shape, jnp.float32) for base in bases]
    return run(outputs_kernel, [place], arrays, specs, [], outs, specs[:2], name="outputs")


def to_column(pieces, ratio):
    return [pieces[0]] + [flip(pieces[o], "pcol", o * ratio) for o in range(1, len(pieces))]


def to_plane(pieces):
    return [pieces[0]] + [flip(pieces[o], "prow", o) for o in range(1, len(pieces))]


def to_plane_whole(factor, count, ratio):
    pieces = jnp.swapaxes(factor.reshape(factor.shape[0], count, -1), 0, 1)
    groups = [[c * ratio + k for c in range(count)] for k in range(ratio)]
    spread = lax.all_to_all(pieces, "pcol", 0, 0, axis_index_groups=groups)
    return lax.all_to_all(spread, "prow", 0, 0)


def gather_plane(own, pcol_count):
    return [own] + [flip(own, "pcol", offset) for offset in range(2, pcol_count, 2)]


def in_rows(gathered, count, ratio):
    _, _, unit_rows, width = gathered.shape
    split = gathered.reshape(count, ratio, count, unit_rows, width)
    rows = jnp.transpose(split, (1, 2, 3, 0, 4))
    return rows.reshape(ratio * count * unit_rows, count * width)


FOUR_SLOTS = ((3, 2, 1, 0), (2, 0, 3, 1), (1, 3, 0, 2), (0, 1, 2, 3))


def slots_of(count):
    return FOUR_SLOTS if count == len(FOUR_SLOTS) else (tuple(range(count)),) * count


def sum_over_four(slots):
    near = lax.ppermute(slots[0], "prow", [(0, 1), (3, 2)])
    total = lax.ppermute(slots[1], "prow", [(0, 2), (2, 3), (3, 1), (1, 0)])
    middle = lax.ppermute(slots[0], "prow", [(1, 2), (2, 1)])
    both = add_up([slots[2], near], [])
    last = lax.ppermute(both, "prow", [(1, 3), (2, 0), (0, 1), (3, 2)])
    return [slots[3], total, middle, last, near]


def sum_over_line(slots, z):
    count = len(slots)
    if count == len(FOUR_SLOTS):
        return sum_over_four(slots)
    chunks = jnp.stack(slots)

    def chunk(index):
        return lax.dynamic_index_in_dim(chunks, jnp.clip(index, 0, count - 1), 0, keepdims=False)

    up = down = None
    for t in range(1, count):
        up_send, down_send = chunk(z + count - t), chunk(z + t - count)
        if up is not None:
            up_send, down_send = up_send + up, down_send + down
        up = lax.ppermute(up_send, "prow", [(i, i + 1) for i in range(min(t, count - 1))])
        down = lax.ppermute(
            down_send, "prow", [(i, i - 1) for i in range(max(count - t, 1), count)]
        )
    mine = chunk(z)
    none = jnp.zeros_like(mine)
    return [mine, none if up is None else up, none if down is None else down, none, mine]


def sum_plane(place, keep, send):
    pieces = fold(place, keep, flip(send, "pcol", 1))
    return [pieces[0]] + [flip(pieces[o], "pcol", 2 * o) for o in range(1, len(pieces))]


def sum_planes(pieces, count):
    bit = 1
    while True:
        total = add_up(pieces, [])
        if bit >= count:
            return [total, jnp.zeros_like(total)]
        pieces = [total, flip(total, "prow", bit)]
        bit *= 2
        if bit >= count:
            return pieces


def sum_pair_near(place, pieces, waits):
    kept, other = fold_pair(place, pieces, waits)
    return [kept, flip(other, "prow", 1)]


def sum_pair_far(pieces, count, waits):
    bit = 2
    while True:
        total = add_up(pieces, waits)
        if bit >= count:
            return [total, flip(total, "prow", 1)]
        pieces, waits = [total, flip(total, "prow", bit)], []
        bit *= 2


def body(inverse_tiles, factor, link_factor, diag_inverse, ancestors):
    row_count, col_count = inverse_tiles.shape
    nsuper, unit_rows, columns = factor.shape
    count = lax.axis_size("prow")
    pcol_count = lax.axis_size("pcol")
    ratio = col_count // row_count
    z = lax.axis_index("prow")
    pcol_index = lax.axis_index("pcol")
    width = columns // count
    place = jnp.stack([pcol_index, z, pcol_index // ratio]).astype(jnp.int32)
    slots = jnp.asarray(slots_of(count), jnp.int32)

    def own_block(place):
        return (place[0] * count + place[1]) * unit_rows // columns

    sent, turned, received, waits = [], [], [], []
    if width % LANES == 0:
        for number in range(nsuper):
            sent.append(to_column(cut(place, factor, number, count, waits), ratio))
            waits = received[-1][1:] if received else []
            turned.append(turn(place, sent[number], waits))
            waits = [turned[0][0]]
            received.append(to_plane(turned[number]))
    waits = [pieces[0] for pieces in received[:1]]
    bases = bases_of(place, diag_inverse, link_factor, columns // pcol_count, waits)
    rows, gathered = [], []
    for number in range(nsuper):
        if received:
            gathered += [piece for later in sent[number + 1 : number + 2] for piece in later[1:]]
            own = arrange(place, received[number], gathered)
            found = gather_plane(own, pcol_count)
            gathered = found[1:]
            waits = [piece for later in received[number + 1 : number + 2] for piece in later[1:]]
            packed = pack(found, waits + (rows[-1][1:4] + late if rows else [bases[0]]))
            pieces = [packed, flip(packed, "pcol", 1)]
        else:
            own = to_plane_whole(factor[number], count, ratio)
            pieces = [in_rows(lax.all_gather(own, "pcol", axis=0), count, ratio)]
        middle = count // 2 if number == 0 and received else count
        partial, starts = [], [0, middle, count] if middle < count else [0, count]
        for start, stop in zip(starts, starts[1:]):
            partial += partial_product(
                place, slots, ancestors, inverse_tiles, pieces, ratio, columns, number, start, stop,
                [bases[0]],
            )
        rows.append(sum_over_line(partial, z))
        rows[-1] = rows[-1][:3] + rows[-1][:2:-1]
        late = [partial[-1]]

    sums, before, pending = [], [], []
    for number in range(nsuper):
        last = number + 1 == nsuper
        waits = [] if last else rows[number + 1][1:4]
        offdiag, keep, send, *link = finish(
            number, own_block, place, ancestors, rows[number][:3] + rows[number][4:], factor, before,
            link_factor, pcol_count // 2, waits + pending[:1],
        )
        if pending:
            sums += sum_pair_far(pending, count, [keep])
        group = sum_plane(place, keep, send)
        if not last:
            rest = rest_of(link_factor, *link, offdiag, number)
            before = [*rest, offdiag]
            pending = sum_pair_near(place, group, rest[:1])
    sums += sum_planes(group, count)
    return (offdiag, *outputs(place, bases, sums))


def solution(mesh):
    in_specs = (P("pcol", "prow"), P(None, ("pcol", "prow"), None), P(), P(), P())
    out_specs = (P(None, ("pcol", "prow"), None), P(None, "pcol", None), P(None, "pcol", None))
    return jax.shard_map(body, mesh=mesh, in_specs=in_specs, out_specs=out_specs, check_vma=False)
```

```python
import functools

import jax
import jax.numpy as jnp
from jax import lax
from jax.experimental import pallas as pl
from jax.experimental.pallas import tpu as pltpu
from jax.sharding import PartitionSpec as P

BOTH = ("prow", "pcol")
VMEM_LIMIT = 32 * 1024 * 1024
LANES = 128


def halves(value):
    high = value.astype(jnp.bfloat16)
    low = (value - high.astype(jnp.float32)).astype(jnp.bfloat16)
    return high, low


def flip(value, axis, bit):
    return lax.ppermute(value, axis, [(i, i ^ bit) for i in range(lax.axis_size(axis))])


def run(
    kernel, scalars, arrays, specs, waits, outs, out_specs, grid=(1,), scratch=(), alias=None, name=None
):
    def corner(array):
        block = (1,) * (array.ndim - 2) + (8, LANES)
        return pl.BlockSpec(block, lambda *_: (0,) * array.ndim)

    def body(*refs):
        first = len(scalars) + len(arrays)
        kernel(*refs[:first], *refs[first + len(waits) :])

    return pl.pallas_call(
        body,
        grid_spec=pltpu.PrefetchScalarGridSpec(
            num_scalar_prefetch=len(scalars),
            grid=grid,
            in_specs=list(specs) + [corner(array) for array in waits],
            out_specs=out_specs,
            scratch_shapes=list(scratch),
        ),
        out_shape=outs,
        input_output_aliases=alias or {},
        compiler_params=pltpu.CompilerParams(vmem_limit_bytes=VMEM_LIMIT),
        cost_estimate=pl.CostEstimate(flops=0, bytes_accessed=0, transcendentals=0),
        name=name,
    )(*scalars, *arrays, *waits)


def whole(array):
    return pl.BlockSpec(array.shape, lambda *_: (0,) * array.ndim)


def cut_kernel(place, factor_ref, *out_refs):
    width = out_refs[0].shape[1]
    for o, out_ref in enumerate(out_refs):
        start = pl.multiple_of((place[2] ^ o) * width, width)
        out_ref[...] = factor_ref[0, :, pl.ds(start, width)]


def cut(place, factor, number, count, waits):
    _, unit_rows, columns = factor.shape
    piece = jax.ShapeDtypeStruct((unit_rows, columns // count), factor.dtype)
    spec = pl.BlockSpec((1, unit_rows, columns), lambda *_: (number, 0, 0))
    outs = [piece] * count
    specs = [whole(piece)] * count
    return run(cut_kernel, [place], [factor], [spec], waits, outs, specs, name="cut")


def turn_kernel(place, *refs):
    count = len(refs) // 2
    for shift in range(count):

        @pl.when((place[1] ^ place[2]) == shift)
        def _copy(shift=shift):
            for o in range(count):
                refs[count + o][...] = refs[o ^ shift][...]


def turn(place, pieces, waits):
    count = len(pieces)
    piece = jax.ShapeDtypeStruct(pieces[0].shape, pieces[0].dtype)
    specs = [whole(piece)] * count
    return run(turn_kernel, [place], pieces, specs, waits, [piece] * count, specs, name="turn")


def arrange_kernel(place, *refs):
    out_ref = refs[-1]
    for o, piece_ref in enumerate(refs[:-1]):
        out_ref[place[1] ^ o] = piece_ref[...]


def arrange(place, pieces, waits):
    out = jax.ShapeDtypeStruct((len(pieces),) + pieces[0].shape, pieces[0].dtype)
    specs = [whole(piece) for piece in pieces]
    return run(arrange_kernel, [place], pieces, specs, waits, out, whole(out), name="arrange")


def pack_kernel(*refs):
    for index, ref in enumerate(refs[:-1]):
        refs[-1][index] = ref[...]


def pack(pieces, waits):
    out = jax.ShapeDtypeStruct((len(pieces),) + pieces[0].shape, pieces[0].dtype)
    specs = [whole(piece) for piece in pieces]
    return run(pack_kernel, [], pieces, specs, waits, out, whole(out), name="pack")


def add_kernel(*refs):
    total = refs[0][...]
    for ref in refs[1:-1]:
        total = total + ref[...]
    refs[-1][...] = total


def add_up(arrays, waits):
    out = jax.ShapeDtypeStruct(arrays[0].shape, arrays[0].dtype)
    specs = [whole(array) for array in arrays]
    return run(add_kernel, [], arrays, specs, waits, out, whole(out), name="add_up")


def is_listed(ancestors, number, block):
    found = ancestors[number, 0] == block
    for i in range(1, ancestors.shape[1]):
        found = found | (ancestors[number, i] == block)
    return found


def partial_kernel(sides, ratio, count, number, start, place, slots, ancestors, tile_ref, *refs):
    piece_refs, out_refs, right_ref = refs[:sides], refs[sides:-1], refs[-1]
    chunk_rows, columns = out_refs[0].shape
    blocks = tile_ref.shape[1] // columns
    step = pl.program_id(0)

    def listed(block):
        return is_listed(ancestors, number, block)

    @pl.when(step == 0)
    def _assemble():
        def put(first, lanes, value):
            high, low = halves(value)
            for index in range(value.shape[0] // columns):
                part = slice(index * columns, (index + 1) * columns)
                for turn, side in enumerate((high, low, high)):
                    right_ref[first + index, pl.ds(turn * columns, columns), lanes] = side[part]

        if len(piece_refs) == 1:
            put(0, slice(None), piece_refs[0][...])
            return
        for side, ref in enumerate(piece_refs):
            chips, parts, unit_rows, width = ref.shape
            span = parts * unit_rows
            for o in range(chips):
                owner = place[0] ^ (2 * o + side)
                lanes = pl.ds(pl.multiple_of(owner // ratio * width, width), width)
                put(owner % ratio * (span // columns), lanes, ref[o].reshape(span, width))

    def multiply(out_ref):
        out_ref[...] = jnp.zeros_like(out_ref)
        chunk = place[0] * count + slots[place[1], start + step]

        @pl.when(listed(chunk * chunk_rows // columns))
        def _chunk():
            def add(block, carry):
                @pl.when(listed(place[1] * blocks + block))
                def _block():
                    span = pl.ds(pl.multiple_of(block * columns, columns), columns)
                    high, low = halves(tile_ref[:, span])
                    left = jnp.concatenate([high, high, low], axis=1)
                    out_ref[...] += jnp.dot(
                        left, right_ref[block], preferred_element_type=jnp.float32
                    )

                return carry

            lax.fori_loop(0, blocks, add, 0)

    for index, out_ref in enumerate(out_refs):
        pl.when(step == index)(functools.partial(multiply, out_ref))


def partial_product(
    place, slots, ancestors, tiles, pieces, ratio, columns, number, start, stop, waits
):
    rows, cols = tiles.shape
    count = slots.shape[0]
    out = jax.ShapeDtypeStruct((rows // count, columns), jnp.float32)
    tile = pl.BlockSpec((rows // count, cols), lambda i, p, s, a: (s[p[1], start + i], 0))
    return run(
        functools.partial(partial_kernel, len(pieces), ratio, count, number, start),
        [place, slots, ancestors],
        [tiles] + pieces,
        [tile] + [whole(piece) for piece in pieces],
        waits,
        [out] * (stop - start),
        [whole(out)] * (stop - start),
        grid=(stop - start,),
        scratch=[pltpu.VMEM((cols // columns, 3 * columns, columns), jnp.bfloat16)],
        name="partial_product",
    )


def dot(left, right, side=1):
    def one(a, b):
        return lax.dot_general(
            a, b, (((side,), (0,)), ((), ())), preferred_element_type=jnp.float32
        )

    left_high, left_low = halves(left)
    right_high, right_low = halves(right)
    return one(left_high, right_high) + (one(left_high, right_low) + one(left_low, right_high))


def part_by_core(place, matrix_ref, index, keep_ref, send_ref):
    _, chips, rows, _ = keep_ref.shape
    core = place[0] % 2
    for chip in range(chips):
        for ref, side in ((keep_ref, core), (send_ref, 1 - core)):
            first = pl.multiple_of((chip * 2 + side) * rows, rows)
            ref[index, chip] = matrix_ref[pl.ds(first, rows), :]


def finish_kernel(number, last, first, block, place, ancestors, *refs):
    refs = list(refs)
    sums, factor_ref = [refs.pop(0) for _ in range(4)], refs.pop(0)
    if not first:
        old_rest, old_rows, _ = (refs.pop(0) for _ in range(3))
    if not last:
        link_ref, next_ref = refs.pop(0), refs.pop(0)
    offdiag_ref, keep_ref, send_ref = (refs.pop(0) for _ in range(3))
    if not last:
        cross_ref, kept_ref = refs.pop(0), refs.pop(0)
    part_ref = refs.pop(0)
    offdiag_ref[...] = jnp.zeros_like(offdiag_ref)
    part_ref[...] = jnp.zeros_like(part_ref) if first else old_rest[...]

    own = block(place)

    @pl.when(is_listed(ancestors, number, own))
    def _own():
        summed = ((sums[0][...] + sums[1][...]) + sums[2][...]) + sums[3][...]
        part_ref[...] += dot(factor_ref[0], summed, 0)
        offdiag_ref[0] = -(summed if first else summed + old_rows[...])

    part_by_core(place, part_ref, 0, keep_ref, send_ref)
    if last:
        return
    cross_ref[...] = jnp.zeros_like(cross_ref)

    @pl.when(is_listed(ancestors, number + 1, own))
    def _cross():
        cross_ref[...] = dot(offdiag_ref[0], next_ref[0], 0)

    kept_ref[...] = cross_ref[...] + dot(part_ref[...], link_ref[0])
    part_by_core(place, kept_ref, 1, keep_ref, send_ref)


def rest_kernel(link_ref, cross_ref, part_ref, offdiag_ref, rest_ref, rows_ref):
    link = link_ref[0]
    rest_ref[...] = dot(cross_ref[...], link, 0) + dot(link, part_ref[...], 0)
    rows_ref[...] = dot(offdiag_ref[0], link)


def rest_of(link_factor, cross, link_part, offdiag, number):
    _, unit_rows, columns = offdiag.shape
    link = pl.BlockSpec((1, columns, columns), lambda *_: (number, 0, 0))
    rows = pl.BlockSpec((1, unit_rows, columns), lambda *_: (number, 0, 0))
    outs = [cross, jax.ShapeDtypeStruct((unit_rows, columns), jnp.float32)]
    outs = [jax.ShapeDtypeStruct(out.shape, jnp.float32) for out in outs]
    return run(
        rest_kernel, [], [link_factor, cross, link_part, offdiag],
        [link, whole(cross), whole(link_part), rows], [], outs, [whole(out) for out in outs],
        name="rest",
    )


def finish(number, block, place, ancestors, sums, factor, before, link_factor, chips, waits):
    nsuper, unit_rows, columns = factor.shape
    first, last = number == 0, number + 1 == nsuper
    slab = (1, unit_rows, columns)
    arrays, specs = list(sums), [whole(array) for array in sums]
    arrays.append(factor)
    specs.append(pl.BlockSpec(slab, lambda *_: (number, 0, 0)))
    alias = {}
    if not first:
        alias = {2 + len(arrays) + 2: 0}
        arrays += before
        specs += [whole(before[0]), whole(before[1])]
        specs.append(pl.BlockSpec((1, 8, LANES), lambda *_: (0, 0, 0)))
    if not last:
        arrays += [link_factor, factor]
        specs.append(pl.BlockSpec((1, columns, columns), lambda *_: (number, 0, 0)))
        specs.append(pl.BlockSpec(slab, lambda *_: (number + 1, 0, 0)))
    shape = jax.ShapeDtypeStruct
    groups = shape((1 if last else 2, chips, columns // (2 * chips), columns), jnp.float32)
    outs = [shape(factor.shape, jnp.float32), groups, groups]
    out_specs = [pl.BlockSpec(slab, lambda *_: (number, 0, 0)), whole(groups), whole(groups)]
    if not last:
        more = [shape((columns, columns), jnp.float32)] * 2
        outs += more
        out_specs += [whole(array) for array in more]
    return run(
        functools.partial(finish_kernel, number, last, first, block),
        [place, ancestors],
        arrays,
        specs,
        waits,
        outs,
        out_specs,
        scratch=[pltpu.VMEM((columns, columns), jnp.float32)],
        alias=alias,
        name="finish",
    )


def fold_kernel(place, keep_ref, received_ref, *out_refs):
    chip = place[0] // 2
    for o, out_ref in enumerate(out_refs):
        out_ref[...] = keep_ref[:, chip ^ o] + received_ref[:, chip ^ o]


def fold(place, keep, received):
    number, chips, rows, columns = keep.shape
    out = jax.ShapeDtypeStruct((number, rows, columns), jnp.float32)
    specs = [whole(keep)] * 2
    outs = [out] * chips
    return run(
        fold_kernel, [place], [keep, received], specs, [], outs, [whole(out)] * chips, name="fold"
    )


def fold_pair_kernel(place, *refs):
    *piece_refs, kept_ref, other_ref = refs
    mine = place[1] % 2
    for out_ref, index in ((kept_ref, mine), (other_ref, 1 - mine)):
        total = piece_refs[0][index]
        for ref in piece_refs[1:]:
            total = total + ref[index]
        out_ref[...] = total


def fold_pair(place, pieces, waits):
    out = jax.ShapeDtypeStruct(pieces[0].shape[1:], jnp.float32)
    specs = [whole(piece) for piece in pieces]
    return run(
        fold_pair_kernel, [place], pieces, specs, waits, [out] * 2, [whole(out)] * 2,
        name="fold_pair",
    )


def bases_kernel(nsuper, place, diag_ref, link_ref, *refs):
    diag_out, link_out, base_ref, next_ref = refs
    rows = diag_out.shape[1]
    mine = pl.ds(pl.multiple_of(place[0] * rows, rows), rows)
    base_ref[...] = diag_ref[0]
    diag_out[0] = base_ref[mine, :]
    for number in range(1, nsuper):
        link = link_ref[number - 1]
        next_ref[...] = dot(base_ref[...], link)
        link_out[number - 1] = next_ref[mine, :]
        base_ref[...] = diag_ref[number] + dot(link, next_ref[...], 0)
        diag_out[number] = base_ref[mine, :]


def bases_of(place, diag_inverse, link_factor, rows, waits):
    nsuper, columns, _ = diag_inverse.shape
    outs = [
        jax.ShapeDtypeStruct((nsuper, rows, columns), jnp.float32),
        jax.ShapeDtypeStruct((nsuper - 1, rows, columns), jnp.float32),
    ]
    return run(
        functools.partial(bases_kernel, nsuper),
        [place],
        [diag_inverse, link_factor],
        [whole(diag_inverse), whole(link_factor)],
        waits,
        outs,
        [whole(out) for out in outs],
        scratch=[pltpu.VMEM((columns, columns), jnp.float32)] * 2,
        name="bases",
    )


def outputs_kernel(place, *refs):
    diag_base, link_base, *sums, diag_out, link_out = refs
    steps = link_out.shape[0]
    for number in range(steps):
        pair = sums[2 * number : 2 * number + 2]

        def put(diag, link, number=number):
            diag_out[number] = diag[...] + diag_base[number]
            link_out[number] = -(link[...] + link_base[number])

        pl.when(place[1] % 2 == 0)(functools.partial(put, *pair))
        pl.when(place[1] % 2 == 1)(functools.partial(put, *pair[::-1]))
    diag_out[steps] = sums[-2][0] + sums[-1][0] + diag_base[steps]


def outputs(place, bases, sums):
    arrays = list(bases) + sums
    specs = [whole(array) for array in arrays]
    outs = [jax.ShapeDtypeStruct(base.shape, jnp.float32) for base in bases]
    return run(outputs_kernel, [place], arrays, specs, [], outs, specs[:2], name="outputs")


def to_column(pieces, ratio):
    return [pieces[0]] + [flip(pieces[o], "pcol", o * ratio) for o in range(1, len(pieces))]


def to_plane(pieces):
    return [pieces[0]] + [flip(pieces[o], "prow", o) for o in range(1, len(pieces))]


def to_plane_whole(factor, count, ratio):
    pieces = jnp.swapaxes(factor.reshape(factor.shape[0], count, -1), 0, 1)
    groups = [[c * ratio + k for c in range(count)] for k in range(ratio)]
    spread = lax.all_to_all(pieces, "pcol", 0, 0, axis_index_groups=groups)
    return lax.all_to_all(spread, "prow", 0, 0)


def gather_plane(own, pcol_count):
    return [own] + [flip(own, "pcol", offset) for offset in range(2, pcol_count, 2)]


def in_rows(gathered, count, ratio):
    _, _, unit_rows, width = gathered.shape
    split = gathered.reshape(count, ratio, count, unit_rows, width)
    rows = jnp.transpose(split, (1, 2, 3, 0, 4))
    return rows.reshape(ratio * count * unit_rows, count * width)


FOUR_SLOTS = ((3, 2, 1, 0), (2, 0, 3, 1), (1, 3, 0, 2), (0, 1, 2, 3))


def slots_of(count):
    return FOUR_SLOTS if count == len(FOUR_SLOTS) else (tuple(range(count)),) * count


def sum_over_four(slots):
    near = lax.ppermute(slots[0], "prow", [(0, 1), (3, 2)])
    total = lax.ppermute(slots[1], "prow", [(0, 2), (2, 3), (3, 1), (1, 0)])
    middle = lax.ppermute(slots[0], "prow", [(1, 2), (2, 1)])
    both = add_up([slots[2], near], [])
    last = lax.ppermute(both, "prow", [(1, 3), (2, 0), (0, 1), (3, 2)])
    return [slots[3], total, middle, last, near]


def sum_over_line(slots, z):
    count = len(slots)
    if count == len(FOUR_SLOTS):
        return sum_over_four(slots)
    chunks = jnp.stack(slots)

    def chunk(index):
        return lax.dynamic_index_in_dim(chunks, jnp.clip(index, 0, count - 1), 0, keepdims=False)

    up = down = None
    for t in range(1, count):
        up_send, down_send = chunk(z + count - t), chunk(z + t - count)
        if up is not None:
            up_send, down_send = up_send + up, down_send + down
        up = lax.ppermute(up_send, "prow", [(i, i + 1) for i in range(min(t, count - 1))])
        down = lax.ppermute(
            down_send, "prow", [(i, i - 1) for i in range(max(count - t, 1), count)]
        )
    mine = chunk(z)
    none = jnp.zeros_like(mine)
    return [mine, none if up is None else up, none if down is None else down, none, mine]


def sum_plane(place, keep, send):
    pieces = fold(place, keep, flip(send, "pcol", 1))
    return [pieces[0]] + [flip(pieces[o], "pcol", 2 * o) for o in range(1, len(pieces))]


def sum_planes(pieces, count):
    bit = 1
    while True:
        total = add_up(pieces, [])
        if bit >= count:
            return [total, jnp.zeros_like(total)]
        pieces = [total, flip(total, "prow", bit)]
        bit *= 2
        if bit >= count:
            return pieces


def sum_pair_near(place, pieces, waits):
    kept, other = fold_pair(place, pieces, waits)
    return [kept, flip(other, "prow", 1)]


def sum_pair_far(pieces, count, waits):
    bit = 2
    while True:
        total = add_up(pieces, waits)
        if bit >= count:
            return [total, flip(total, "prow", 1)]
        pieces, waits = [total, flip(total, "prow", bit)], []
        bit *= 2


def body(inverse_tiles, factor, link_factor, diag_inverse, ancestors):
    row_count, col_count = inverse_tiles.shape
    nsuper, unit_rows, columns = factor.shape
    count = lax.axis_size("prow")
    pcol_count = lax.axis_size("pcol")
    ratio = col_count // row_count
    z = lax.axis_index("prow")
    pcol_index = lax.axis_index("pcol")
    width = columns // count
    place = jnp.stack([pcol_index, z, pcol_index // ratio]).astype(jnp.int32)
    slots = jnp.asarray(slots_of(count), jnp.int32)

    def own_block(place):
        return (place[0] * count + place[1]) * unit_rows // columns

    sent, turned, received, waits = [], [], [], []
    if width % LANES == 0:
        for number in range(nsuper):
            sent.append(to_column(cut(place, factor, number, count, waits), ratio))
            waits = received[-1][1:] if received else []
            turned.append(turn(place, sent[number], waits))
            waits = [turned[0][0]]
            received.append(to_plane(turned[number]))
    waits = [pieces[0] for pieces in received[:1]]
    bases = bases_of(place, diag_inverse, link_factor, columns // pcol_count, waits)
    rows, gathered = [], []
    for number in range(nsuper):
        if received:
            gathered += [piece for later in sent[number + 1 : number + 2] for piece in later[1:]]
            own = arrange(place, received[number], gathered)
            found = gather_plane(own, pcol_count)
            gathered = found[1:]
            waits = [piece for later in received[number + 1 : number + 2] for piece in later[1:]]
            packed = pack(found, waits + (rows[-1][1:4] + late if rows else [bases[0]]))
            pieces = [packed, flip(packed, "pcol", 1)]
        else:
            own = to_plane_whole(factor[number], count, ratio)
            pieces = [in_rows(lax.all_gather(own, "pcol", axis=0), count, ratio)]
        middle = count // 2 if number == 0 and received else count
        partial, starts = [], [0, middle, count] if middle < count else [0, count]
        for start, stop in zip(starts, starts[1:]):
            partial += partial_product(
                place, slots, ancestors, inverse_tiles, pieces, ratio, columns, number, start, stop,
                [bases[0]],
            )
        rows.append(sum_over_line(partial, z))
        rows[-1] = rows[-1][:3] + rows[-1][:2:-1]
        late = [partial[-1]]

    sums, before, pending = [], [], []
    for number in range(nsuper):
        last = number + 1 == nsuper
        waits = [] if last else rows[number + 1][2:4]
        offdiag, keep, send, *link = finish(
            number, own_block, place, ancestors, rows[number][:3] + rows[number][4:], factor, before,
            link_factor, pcol_count // 2, waits + pending[:1],
        )
        if pending:
            sums += sum_pair_far(pending, count, [keep])
        group = sum_plane(place, keep, send)
        if not last:
            rest = rest_of(link_factor, *link, offdiag, number)
            before = [*rest, offdiag]
            pending = sum_pair_near(place, group, rest[:1])
    sums += sum_planes(group, count)
    return (offdiag, *outputs(place, bases, sums))


def solution(mesh):
    in_specs = (P("pcol", "prow"), P(None, ("pcol", "prow"), None), P(), P(), P())
    out_specs = (P(None, ("pcol", "prow"), None), P(None, "pcol", None), P(None, "pcol", None))
    return jax.shard_map(body, mesh=mesh, in_specs=in_specs, out_specs=out_specs, check_vma=False)
```

```python
import functools

import jax
import jax.numpy as jnp
from jax import lax
from jax.experimental import pallas as pl
from jax.experimental.pallas import tpu as pltpu
from jax.sharding import PartitionSpec as P

BOTH = ("prow", "pcol")
VMEM_LIMIT = 32 * 1024 * 1024
LANES = 128


def halves(value):
    high = value.astype(jnp.bfloat16)
    low = (value - high.astype(jnp.float32)).astype(jnp.bfloat16)
    return high, low


def flip(value, axis, bit):
    return lax.ppermute(value, axis, [(i, i ^ bit) for i in range(lax.axis_size(axis))])


def run(
    kernel, scalars, arrays, specs, waits, outs, out_specs, grid=(1,), scratch=(), alias=None, name=None
):
    def corner(array):
        block = (1,) * (array.ndim - 2) + (8, LANES)
        return pl.BlockSpec(block, lambda *_: (0,) * array.ndim)

    def body(*refs):
        first = len(scalars) + len(arrays)
        kernel(*refs[:first], *refs[first + len(waits) :])

    return pl.pallas_call(
        body,
        grid_spec=pltpu.PrefetchScalarGridSpec(
            num_scalar_prefetch=len(scalars),
            grid=grid,
            in_specs=list(specs) + [corner(array) for array in waits],
            out_specs=out_specs,
            scratch_shapes=list(scratch),
        ),
        out_shape=outs,
        input_output_aliases=alias or {},
        compiler_params=pltpu.CompilerParams(vmem_limit_bytes=VMEM_LIMIT),
        cost_estimate=pl.CostEstimate(flops=0, bytes_accessed=0, transcendentals=0),
        name=name,
    )(*scalars, *arrays, *waits)


def whole(array):
    return pl.BlockSpec(array.shape, lambda *_: (0,) * array.ndim)


def cut_kernel(place, factor_ref, *out_refs):
    width = out_refs[0].shape[1]
    for o, out_ref in enumerate(out_refs):
        start = pl.multiple_of((place[2] ^ o) * width, width)
        out_ref[...] = factor_ref[0, :, pl.ds(start, width)]


def cut(place, factor, number, count, waits):
    _, unit_rows, columns = factor.shape
    piece = jax.ShapeDtypeStruct((unit_rows, columns // count), factor.dtype)
    spec = pl.BlockSpec((1, unit_rows, columns), lambda *_: (number, 0, 0))
    outs = [piece] * count
    specs = [whole(piece)] * count
    return run(cut_kernel, [place], [factor], [spec], waits, outs, specs, name="cut")


def turn_kernel(place, *refs):
    count = len(refs) // 2
    for shift in range(count):

        @pl.when((place[1] ^ place[2]) == shift)
        def _copy(shift=shift):
            for o in range(count):
                refs[count + o][...] = refs[o ^ shift][...]


def turn(place, pieces, waits):
    count = len(pieces)
    piece = jax.ShapeDtypeStruct(pieces[0].shape, pieces[0].dtype)
    specs = [whole(piece)] * count
    return run(turn_kernel, [place], pieces, specs, waits, [piece] * count, specs, name="turn")


def arrange_kernel(place, *refs):
    out_ref = refs[-1]
    for o, piece_ref in enumerate(refs[:-1]):
        out_ref[place[1] ^ o] = piece_ref[...]


def arrange(place, pieces, waits):
    out = jax.ShapeDtypeStruct((len(pieces),) + pieces[0].shape, pieces[0].dtype)
    specs = [whole(piece) for piece in pieces]
    return run(arrange_kernel, [place], pieces, specs, waits, out, whole(out), name="arrange")


def pack_kernel(*refs):
    for index, ref in enumerate(refs[:-1]):
        refs[-1][index] = ref[...]


def pack(pieces, waits):
    out = jax.ShapeDtypeStruct((len(pieces),) + pieces[0].shape, pieces[0].dtype)
    specs = [whole(piece) for piece in pieces]
    return run(pack_kernel, [], pieces, specs, waits, out, whole(out), name="pack")


def add_kernel(*refs):
    total = refs[0][...]
    for ref in refs[1:-1]:
        total = total + ref[...]
    refs[-1][...] = total


def add_up(arrays, waits):
    out = jax.ShapeDtypeStruct(arrays[0].shape, arrays[0].dtype)
    specs = [whole(array) for array in arrays]
    return run(add_kernel, [], arrays, specs, waits, out, whole(out), name="add_up")


def is_listed(ancestors, number, block):
    found = ancestors[number, 0] == block
    for i in range(1, ancestors.shape[1]):
        found = found | (ancestors[number, i] == block)
    return found


def partial_kernel(sides, ratio, count, number, start, place, slots, ancestors, tile_ref, *refs):
    piece_refs, out_refs, right_ref = refs[:sides], refs[sides:-1], refs[-1]
    chunk_rows, columns = out_refs[0].shape
    blocks = tile_ref.shape[1] // columns
    step = pl.program_id(0)

    def listed(block):
        return is_listed(ancestors, number, block)

    @pl.when(step == 0)
    def _assemble():
        def put(first, lanes, value):
            high, low = halves(value)
            for index in range(value.shape[0] // columns):
                part = slice(index * columns, (index + 1) * columns)
                for turn, side in enumerate((high, low, high)):
                    right_ref[first + index, pl.ds(turn * columns, columns), lanes] = side[part]

        if len(piece_refs) == 1:
            put(0, slice(None), piece_refs[0][...])
            return
        for side, ref in enumerate(piece_refs):
            chips, parts, unit_rows, width = ref.shape
            span = parts * unit_rows
            for o in range(chips):
                owner = place[0] ^ (2 * o + side)
                lanes = pl.ds(pl.multiple_of(owner // ratio * width, width), width)
                put(owner % ratio * (span // columns), lanes, ref[o].reshape(span, width))

    def multiply(out_ref):
        out_ref[...] = jnp.zeros_like(out_ref)
        chunk = place[0] * count + slots[place[1], start + step]

        @pl.when(listed(chunk * chunk_rows // columns))
        def _chunk():
            def add(block, carry):
                @pl.when(listed(place[1] * blocks + block))
                def _block():
                    span = pl.ds(pl.multiple_of(block * columns, columns), columns)
                    high, low = halves(tile_ref[:, span])
                    left = jnp.concatenate([high, high, low], axis=1)
                    out_ref[...] += jnp.dot(
                        left, right_ref[block], preferred_element_type=jnp.float32
                    )

                return carry

            lax.fori_loop(0, blocks, add, 0)

    for index, out_ref in enumerate(out_refs):
        pl.when(step == index)(functools.partial(multiply, out_ref))


def partial_product(
    place, slots, ancestors, tiles, pieces, ratio, columns, number, start, stop, waits
):
    rows, cols = tiles.shape
    count = slots.shape[0]
    out = jax.ShapeDtypeStruct((rows // count, columns), jnp.float32)
    tile = pl.BlockSpec((rows // count, cols), lambda i, p, s, a: (s[p[1], start + i], 0))
    return run(
        functools.partial(partial_kernel, len(pieces), ratio, count, number, start),
        [place, slots, ancestors],
        [tiles] + pieces,
        [tile] + [whole(piece) for piece in pieces],
        waits,
        [out] * (stop - start),
        [whole(out)] * (stop - start),
        grid=(stop - start,),
        scratch=[pltpu.VMEM((cols // columns, 3 * columns, columns), jnp.bfloat16)],
        name="partial_product",
    )


def dot(left, right, side=1):
    def one(a, b):
        return lax.dot_general(
            a, b, (((side,), (0,)), ((), ())), preferred_element_type=jnp.float32
        )

    left_high, left_low = halves(left)
    right_high, right_low = halves(right)
    return one(left_high, right_high) + (one(left_high, right_low) + one(left_low, right_high))


def part_by_core(place, matrix_ref, index, keep_ref, send_ref):
    _, chips, rows, _ = keep_ref.shape
    core = place[0] % 2
    for chip in range(chips):
        for ref, side in ((keep_ref, core), (send_ref, 1 - core)):
            first = pl.multiple_of((chip * 2 + side) * rows, rows)
            ref[index, chip] = matrix_ref[pl.ds(first, rows), :]


def finish_kernel(number, last, first, block, place, ancestors, *refs):
    refs = list(refs)
    sums, factor_ref = [refs.pop(0) for _ in range(4)], refs.pop(0)
    if not first:
        old_rest, old_rows, _ = (refs.pop(0) for _ in range(3))
    if not last:
        link_ref, next_ref = refs.pop(0), refs.pop(0)
    offdiag_ref, keep_ref, send_ref = (refs.pop(0) for _ in range(3))
    if not last:
        cross_ref, kept_ref = refs.pop(0), refs.pop(0)
    part_ref = refs.pop(0)
    offdiag_ref[...] = jnp.zeros_like(offdiag_ref)
    part_ref[...] = jnp.zeros_like(part_ref) if first else old_rest[...]

    own = block(place)

    @pl.when(is_listed(ancestors, number, own))
    def _own():
        summed = ((sums[0][...] + sums[1][...]) + sums[2][...]) + sums[3][...]
        part_ref[...] += dot(factor_ref[0], summed, 0)
        offdiag_ref[0] = -(summed if first else summed + old_rows[...])

    part_by_core(place, part_ref, 0, keep_ref, send_ref)
    if last:
        return
    cross_ref[...] = jnp.zeros_like(cross_ref)

    @pl.when(is_listed(ancestors, number + 1, own))
    def _cross():
        cross_ref[...] = dot(offdiag_ref[0], next_ref[0], 0)

    kept_ref[...] = cross_ref[...] + dot(part_ref[...], link_ref[0])
    part_by_core(place, kept_ref, 1, keep_ref, send_ref)


def rest_kernel(link_ref, cross_ref, part_ref, offdiag_ref, rest_ref, rows_ref):
    link = link_ref[0]
    rest_ref[...] = dot(cross_ref[...], link, 0) + dot(link, part_ref[...], 0)
    rows_ref[...] = dot(offdiag_ref[0], link)


def rest_of(link_factor, cross, link_part, offdiag, number):
    _, unit_rows, columns = offdiag.shape
    link = pl.BlockSpec((1, columns, columns), lambda *_: (number, 0, 0))
    rows = pl.BlockSpec((1, unit_rows, columns), lambda *_: (number, 0, 0))
    outs = [cross, jax.ShapeDtypeStruct((unit_rows, columns), jnp.float32)]
    outs = [jax.ShapeDtypeStruct(out.shape, jnp.float32) for out in outs]
    return run(
        rest_kernel, [], [link_factor, cross, link_part, offdiag],
        [link, whole(cross), whole(link_part), rows], [], outs, [whole(out) for out in outs],
        name="rest",
    )


def finish(number, block, place, ancestors, sums, factor, before, link_factor, chips, waits):
    nsuper, unit_rows, columns = factor.shape
    first, last = number == 0, number + 1 == nsuper
    slab = (1, unit_rows, columns)
    arrays, specs = list(sums), [whole(array) for array in sums]
    arrays.append(factor)
    specs.append(pl.BlockSpec(slab, lambda *_: (number, 0, 0)))
    alias = {}
    if not first:
        alias = {2 + len(arrays) + 2: 0}
        arrays += before
        specs += [whole(before[0]), whole(before[1])]
        specs.append(pl.BlockSpec((1, 8, LANES), lambda *_: (0, 0, 0)))
    if not last:
        arrays += [link_factor, factor]
        specs.append(pl.BlockSpec((1, columns, columns), lambda *_: (number, 0, 0)))
        specs.append(pl.BlockSpec(slab, lambda *_: (number + 1, 0, 0)))
    shape = jax.ShapeDtypeStruct
    groups = shape((1 if last else 2, chips, columns // (2 * chips), columns), jnp.float32)
    outs = [shape(factor.shape, jnp.float32), groups, groups]
    out_specs = [pl.BlockSpec(slab, lambda *_: (number, 0, 0)), whole(groups), whole(groups)]
    if not last:
        more = [shape((columns, columns), jnp.float32)] * 2
        outs += more
        out_specs += [whole(array) for array in more]
    return run(
        functools.partial(finish_kernel, number, last, first, block),
        [place, ancestors],
        arrays,
        specs,
        waits,
        outs,
        out_specs,
        scratch=[pltpu.VMEM((columns, columns), jnp.float32)],
        alias=alias,
        name="finish",
    )


def fold_kernel(place, keep_ref, received_ref, *out_refs):
    chip = place[0] // 2
    for o, out_ref in enumerate(out_refs):
        out_ref[...] = keep_ref[:, chip ^ o] + received_ref[:, chip ^ o]


def fold(place, keep, received):
    number, chips, rows, columns = keep.shape
    out = jax.ShapeDtypeStruct((number, rows, columns), jnp.float32)
    specs = [whole(keep)] * 2
    outs = [out] * chips
    return run(
        fold_kernel, [place], [keep, received], specs, [], outs, [whole(out)] * chips, name="fold"
    )


def fold_pair_kernel(place, *refs):
    *piece_refs, kept_ref, other_ref = refs
    mine = place[1] % 2
    for out_ref, index in ((kept_ref, mine), (other_ref, 1 - mine)):
        total = piece_refs[0][index]
        for ref in piece_refs[1:]:
            total = total + ref[index]
        out_ref[...] = total


def fold_pair(place, pieces, waits):
    out = jax.ShapeDtypeStruct(pieces[0].shape[1:], jnp.float32)
    specs = [whole(piece) for piece in pieces]
    return run(
        fold_pair_kernel, [place], pieces, specs, waits, [out] * 2, [whole(out)] * 2,
        name="fold_pair",
    )


def bases_kernel(nsuper, place, diag_ref, link_ref, *refs):
    diag_out, link_out, base_ref, next_ref = refs
    rows = diag_out.shape[1]
    mine = pl.ds(pl.multiple_of(place[0] * rows, rows), rows)
    base_ref[...] = diag_ref[0]
    diag_out[0] = base_ref[mine, :]
    for number in range(1, nsuper):
        link = link_ref[number - 1]
        next_ref[...] = dot(base_ref[...], link)
        link_out[number - 1] = next_ref[mine, :]
        base_ref[...] = diag_ref[number] + dot(link, next_ref[...], 0)
        diag_out[number] = base_ref[mine, :]


def bases_of(place, diag_inverse, link_factor, rows, waits):
    nsuper, columns, _ = diag_inverse.shape
    outs = [
        jax.ShapeDtypeStruct((nsuper, rows, columns), jnp.float32),
        jax.ShapeDtypeStruct((nsuper - 1, rows, columns), jnp.float32),
    ]
    return run(
        functools.partial(bases_kernel, nsuper),
        [place],
        [diag_inverse, link_factor],
        [whole(diag_inverse), whole(link_factor)],
        waits,
        outs,
        [whole(out) for out in outs],
        scratch=[pltpu.VMEM((columns, columns), jnp.float32)] * 2,
        name="bases",
    )


def outputs_kernel(place, *refs):
    diag_base, link_base, *sums, diag_out, link_out = refs
    steps = link_out.shape[0]
    for number in range(steps):
        pair = sums[2 * number : 2 * number + 2]

        def put(diag, link, number=number):
            diag_out[number] = diag[...] + diag_base[number]
            link_out[number] = -(link[...] + link_base[number])

        pl.when(place[1] % 2 == 0)(functools.partial(put, *pair))
        pl.when(place[1] % 2 == 1)(functools.partial(put, *pair[::-1]))
    diag_out[steps] = sums[-2][0] + sums[-1][0] + diag_base[steps]


def outputs(place, bases, sums):
    arrays = list(bases) + sums
    specs = [whole(array) for array in arrays]
    outs = [jax.ShapeDtypeStruct(base.shape, jnp.float32) for base in bases]
    return run(outputs_kernel, [place], arrays, specs, [], outs, specs[:2], name="outputs")


def to_column(pieces, ratio):
    return [pieces[0]] + [flip(pieces[o], "pcol", o * ratio) for o in range(1, len(pieces))]


def to_plane(pieces):
    return [pieces[0]] + [flip(pieces[o], "prow", o) for o in range(1, len(pieces))]


def to_plane_whole(factor, count, ratio):
    pieces = jnp.swapaxes(factor.reshape(factor.shape[0], count, -1), 0, 1)
    groups = [[c * ratio + k for c in range(count)] for k in range(ratio)]
    spread = lax.all_to_all(pieces, "pcol", 0, 0, axis_index_groups=groups)
    return lax.all_to_all(spread, "prow", 0, 0)


def gather_plane(own, pcol_count):
    return [own] + [flip(own, "pcol", offset) for offset in range(2, pcol_count, 2)]


def in_rows(gathered, count, ratio):
    _, _, unit_rows, width = gathered.shape
    split = gathered.reshape(count, ratio, count, unit_rows, width)
    rows = jnp.transpose(split, (1, 2, 3, 0, 4))
    return rows.reshape(ratio * count * unit_rows, count * width)


FOUR_SLOTS = ((3, 2, 1, 0), (2, 0, 3, 1), (1, 3, 0, 2), (0, 1, 2, 3))


def slots_of(count):
    return FOUR_SLOTS if count == len(FOUR_SLOTS) else (tuple(range(count)),) * count


def sum_over_four(slots):
    near = lax.ppermute(slots[0], "prow", [(0, 1), (3, 2)])
    total = lax.ppermute(slots[1], "prow", [(0, 2), (2, 3), (3, 1), (1, 0)])
    middle = lax.ppermute(slots[0], "prow", [(1, 2), (2, 1)])
    both = add_up([slots[2], near], [])
    last = lax.ppermute(both, "prow", [(1, 3), (2, 0), (0, 1), (3, 2)])
    return [slots[3], total, middle, last, near]


def sum_over_line(slots, z):
    count = len(slots)
    if count == len(FOUR_SLOTS):
        return sum_over_four(slots)
    chunks = jnp.stack(slots)

    def chunk(index):
        return lax.dynamic_index_in_dim(chunks, jnp.clip(index, 0, count - 1), 0, keepdims=False)

    up = down = None
    for t in range(1, count):
        up_send, down_send = chunk(z + count - t), chunk(z + t - count)
        if up is not None:
            up_send, down_send = up_send + up, down_send + down
        up = lax.ppermute(up_send, "prow", [(i, i + 1) for i in range(min(t, count - 1))])
        down = lax.ppermute(
            down_send, "prow", [(i, i - 1) for i in range(max(count - t, 1), count)]
        )
    mine = chunk(z)
    none = jnp.zeros_like(mine)
    return [mine, none if up is None else up, none if down is None else down, none, mine]


def sum_plane(place, keep, send):
    pieces = fold(place, keep, flip(send, "pcol", 1))
    return [pieces[0]] + [flip(pieces[o], "pcol", 2 * o) for o in range(1, len(pieces))]


def sum_planes(pieces, count):
    bit = 1
    while True:
        total = add_up(pieces, [])
        if bit >= count:
            return [total, jnp.zeros_like(total)]
        pieces = [total, flip(total, "prow", bit)]
        bit *= 2
        if bit >= count:
            return pieces


def sum_pair_near(place, pieces, waits):
    kept, other = fold_pair(place, pieces, waits)
    return [kept, flip(other, "prow", 1)]


def sum_pair_far(pieces, count, waits):
    bit = 2
    while True:
        total = add_up(pieces, waits)
        if bit >= count:
            return [total, flip(total, "prow", 1)]
        pieces, waits = [total, flip(total, "prow", bit)], []
        bit *= 2


def body(inverse_tiles, factor, link_factor, diag_inverse, ancestors):
    row_count, col_count = inverse_tiles.shape
    nsuper, unit_rows, columns = factor.shape
    count = lax.axis_size("prow")
    pcol_count = lax.axis_size("pcol")
    ratio = col_count // row_count
    z = lax.axis_index("prow")
    pcol_index = lax.axis_index("pcol")
    width = columns // count
    place = jnp.stack([pcol_index, z, pcol_index // ratio]).astype(jnp.int32)
    slots = jnp.asarray(slots_of(count), jnp.int32)

    def own_block(place):
        return (place[0] * count + place[1]) * unit_rows // columns

    sent, turned, received, waits = [], [], [], []
    if width % LANES == 0:
        for number in range(nsuper):
            sent.append(to_column(cut(place, factor, number, count, waits), ratio))
            waits = received[-1][1:] if received else []
            turned.append(turn(place, sent[number], waits))
            waits = [turned[0][0]]
            received.append(to_plane(turned[number]))
    waits = [pieces[0] for pieces in received[:1]]
    bases = bases_of(place, diag_inverse, link_factor, columns // pcol_count, waits)
    rows, lates, gathered = [], [], []
    for number in range(nsuper):
        if received:
            gathered += [piece for later in sent[number + 1 : number + 2] for piece in later[1:]]
            own = arrange(place, received[number], gathered)
            found = gather_plane(own, pcol_count)
            gathered = found[1:]
            waits = [piece for later in received[number + 1 : number + 2] for piece in later[1:]]
            packed = pack(found, waits + (rows[-1][1:4] + late if rows else [bases[0]]))
            pieces = [packed, flip(packed, "pcol", 1)]
        else:
            own = to_plane_whole(factor[number], count, ratio)
            pieces = [in_rows(lax.all_gather(own, "pcol", axis=0), count, ratio)]
        middle = 1 if rows else count // 2
        partial, starts = [], [0, middle, count] if received else [0, count]
        for start, stop in zip(starts, starts[1:]):
            partial += partial_product(
                place, slots, ancestors, inverse_tiles, pieces, ratio, columns, number, start, stop,
                [bases[0]],
            )
        rows.append(sum_over_line(partial, z))
        rows[-1] = rows[-1][:3] + rows[-1][:2:-1]
        late = [partial[-1]]
        lates.append(late)

    sums, before, pending = [], [], []
    for number in range(nsuper):
        last = number + 1 == nsuper
        waits = [] if last else rows[number + 1][2:4] + lates[number + 1]
        offdiag, keep, send, *link = finish(
            number, own_block, place, ancestors, rows[number][:3] + rows[number][4:], factor, before,
            link_factor, pcol_count // 2, waits + pending[:1],
        )
        if pending:
            sums += sum_pair_far(pending, count, [keep])
        group = sum_plane(place, keep, send)
        if not last:
            rest = rest_of(link_factor, *link, offdiag, number)
            before = [*rest, offdiag]
            pending = sum_pair_near(place, group, rest[:1])
    sums += sum_planes(group, count)
    return (offdiag, *outputs(place, bases, sums))


def solution(mesh):
    in_specs = (P("pcol", "prow"), P(None, ("pcol", "prow"), None), P(), P(), P())
    out_specs = (P(None, ("pcol", "prow"), None), P(None, "pcol", None), P(None, "pcol", None))
    return jax.shard_map(body, mesh=mesh, in_specs=in_specs, out_specs=out_specs, check_vma=False)
```

```python
import functools

import jax
import jax.numpy as jnp
from jax import lax
from jax.experimental import pallas as pl
from jax.experimental.pallas import tpu as pltpu
from jax.sharding import PartitionSpec as P

BOTH = ("prow", "pcol")
VMEM_LIMIT = 32 * 1024 * 1024
LANES = 128


def halves(value):
    high = value.astype(jnp.bfloat16)
    low = (value - high.astype(jnp.float32)).astype(jnp.bfloat16)
    return high, low


def flip(value, axis, bit):
    return lax.ppermute(value, axis, [(i, i ^ bit) for i in range(lax.axis_size(axis))])


def run(
    kernel, scalars, arrays, specs, waits, outs, out_specs, grid=(1,), scratch=(), alias=None, name=None
):
    def corner(array):
        block = (1,) * (array.ndim - 2) + (8, LANES)
        return pl.BlockSpec(block, lambda *_: (0,) * array.ndim)

    def body(*refs):
        first = len(scalars) + len(arrays)
        kernel(*refs[:first], *refs[first + len(waits) :])

    return pl.pallas_call(
        body,
        grid_spec=pltpu.PrefetchScalarGridSpec(
            num_scalar_prefetch=len(scalars),
            grid=grid,
            in_specs=list(specs) + [corner(array) for array in waits],
            out_specs=out_specs,
            scratch_shapes=list(scratch),
        ),
        out_shape=outs,
        input_output_aliases=alias or {},
        compiler_params=pltpu.CompilerParams(vmem_limit_bytes=VMEM_LIMIT),
        cost_estimate=pl.CostEstimate(flops=0, bytes_accessed=0, transcendentals=0),
        name=name,
    )(*scalars, *arrays, *waits)


def whole(array):
    return pl.BlockSpec(array.shape, lambda *_: (0,) * array.ndim)


def cut_kernel(place, factor_ref, *out_refs):
    width = out_refs[0].shape[1]
    for o, out_ref in enumerate(out_refs):
        start = pl.multiple_of((place[2] ^ o) * width, width)
        out_ref[...] = factor_ref[0, :, pl.ds(start, width)]


def cut(place, factor, number, count, waits):
    _, unit_rows, columns = factor.shape
    piece = jax.ShapeDtypeStruct((unit_rows, columns // count), factor.dtype)
    spec = pl.BlockSpec((1, unit_rows, columns), lambda *_: (number, 0, 0))
    outs = [piece] * count
    specs = [whole(piece)] * count
    return run(cut_kernel, [place], [factor], [spec], waits, outs, specs, name="cut")


def turn_kernel(place, *refs):
    count = len(refs) // 2
    for shift in range(count):

        @pl.when((place[1] ^ place[2]) == shift)
        def _copy(shift=shift):
            for o in range(count):
                refs[count + o][...] = refs[o ^ shift][...]


def turn(place, pieces, waits):
    count = len(pieces)
    piece = jax.ShapeDtypeStruct(pieces[0].shape, pieces[0].dtype)
    specs = [whole(piece)] * count
    return run(turn_kernel, [place], pieces, specs, waits, [piece] * count, specs, name="turn")


def arrange_kernel(place, *refs):
    out_ref = refs[-1]
    for o, piece_ref in enumerate(refs[:-1]):
        out_ref[place[1] ^ o] = piece_ref[...]


def arrange(place, pieces, waits):
    out = jax.ShapeDtypeStruct((len(pieces),) + pieces[0].shape, pieces[0].dtype)
    specs = [whole(piece) for piece in pieces]
    return run(arrange_kernel, [place], pieces, specs, waits, out, whole(out), name="arrange")


def pack_kernel(*refs):
    for index, ref in enumerate(refs[:-1]):
        refs[-1][index] = ref[...]


def pack(pieces, waits):
    out = jax.ShapeDtypeStruct((len(pieces),) + pieces[0].shape, pieces[0].dtype)
    specs = [whole(piece) for piece in pieces]
    return run(pack_kernel, [], pieces, specs, waits, out, whole(out), name="pack")


def add_kernel(*refs):
    total = refs[0][...]
    for ref in refs[1:-1]:
        total = total + ref[...]
    refs[-1][...] = total


def add_up(arrays, waits):
    out = jax.ShapeDtypeStruct(arrays[0].shape, arrays[0].dtype)
    specs = [whole(array) for array in arrays]
    return run(add_kernel, [], arrays, specs, waits, out, whole(out), name="add_up")


def pass_on_kernel(place, onward_ref, own_ref, near_ref, both_ref, mine_ref):
    near = near_ref[...]
    inside = (place[1] == 1) | (place[1] == 2)
    both_ref[...] = onward_ref[...] + jnp.where(inside, near, 0.0)
    mine_ref[...] = own_ref[...] + jnp.where(inside, 0.0, near)


def pass_on(place, onward, own, near):
    out = jax.ShapeDtypeStruct(own.shape, own.dtype)
    specs = [whole(own)] * 3
    outs = [out] * 2
    return run(
        pass_on_kernel, [place], [onward, own, near], specs, [], outs, specs[:2], name="pass_on"
    )


def is_listed(ancestors, number, block):
    found = ancestors[number, 0] == block
    for i in range(1, ancestors.shape[1]):
        found = found | (ancestors[number, i] == block)
    return found


def partial_kernel(sides, ratio, count, number, start, place, slots, ancestors, tile_ref, *refs):
    piece_refs, out_refs, right_ref = refs[:sides], refs[sides:-1], refs[-1]
    chunk_rows, columns = out_refs[0].shape
    blocks = tile_ref.shape[1] // columns
    step = pl.program_id(0)

    def listed(block):
        return is_listed(ancestors, number, block)

    @pl.when(step == 0)
    def _assemble():
        def put(first, lanes, value):
            high, low = halves(value)
            for index in range(value.shape[0] // columns):
                part = slice(index * columns, (index + 1) * columns)
                for turn, side in enumerate((high, low, high)):
                    right_ref[first + index, pl.ds(turn * columns, columns), lanes] = side[part]

        if len(piece_refs) == 1:
            put(0, slice(None), piece_refs[0][...])
            return
        for side, ref in enumerate(piece_refs):
            chips, parts, unit_rows, width = ref.shape
            span = parts * unit_rows
            for o in range(chips):
                owner = place[0] ^ (2 * o + side)
                lanes = pl.ds(pl.multiple_of(owner // ratio * width, width), width)
                put(owner % ratio * (span // columns), lanes, ref[o].reshape(span, width))

    def multiply(out_ref):
        out_ref[...] = jnp.zeros_like(out_ref)
        chunk = place[0] * count + slots[place[1], start + step]

        @pl.when(listed(chunk * chunk_rows // columns))
        def _chunk():
            def add(block, carry):
                @pl.when(listed(place[1] * blocks + block))
                def _block():
                    span = pl.ds(pl.multiple_of(block * columns, columns), columns)
                    high, low = halves(tile_ref[:, span])
                    left = jnp.concatenate([high, high, low], axis=1)
                    out_ref[...] += jnp.dot(
                        left, right_ref[block], preferred_element_type=jnp.float32
                    )

                return carry

            lax.fori_loop(0, blocks, add, 0)

    for index, out_ref in enumerate(out_refs):
        pl.when(step == index)(functools.partial(multiply, out_ref))


def partial_product(
    place, slots, ancestors, tiles, pieces, ratio, columns, number, start, stop, waits
):
    rows, cols = tiles.shape
    count = slots.shape[0]
    out = jax.ShapeDtypeStruct((rows // count, columns), jnp.float32)
    tile = pl.BlockSpec((rows // count, cols), lambda i, p, s, a: (s[p[1], start + i], 0))
    return run(
        functools.partial(partial_kernel, len(pieces), ratio, count, number, start),
        [place, slots, ancestors],
        [tiles] + pieces,
        [tile] + [whole(piece) for piece in pieces],
        waits,
        [out] * (stop - start),
        [whole(out)] * (stop - start),
        grid=(stop - start,),
        scratch=[pltpu.VMEM((cols // columns, 3 * columns, columns), jnp.bfloat16)],
        name="partial_product",
    )


def dot(left, right, side=1):
    def one(a, b):
        return lax.dot_general(
            a, b, (((side,), (0,)), ((), ())), preferred_element_type=jnp.float32
        )

    left_high, left_low = halves(left)
    right_high, right_low = halves(right)
    return one(left_high, right_high) + (one(left_high, right_low) + one(left_low, right_high))


def part_by_core(place, matrix_ref, index, keep_ref, send_ref):
    _, chips, rows, _ = keep_ref.shape
    core = place[0] % 2
    for chip in range(chips):
        for ref, side in ((keep_ref, core), (send_ref, 1 - core)):
            first = pl.multiple_of((chip * 2 + side) * rows, rows)
            ref[index, chip] = matrix_ref[pl.ds(first, rows), :]


def finish_kernel(number, last, first, block, place, ancestors, *refs):
    refs = list(refs)
    sums, factor_ref = [refs.pop(0) for _ in range(4)], refs.pop(0)
    if not first:
        old_rest, old_rows, _ = (refs.pop(0) for _ in range(3))
    if not last:
        link_ref, next_ref = refs.pop(0), refs.pop(0)
    offdiag_ref, keep_ref, send_ref = (refs.pop(0) for _ in range(3))
    if not last:
        cross_ref, kept_ref = refs.pop(0), refs.pop(0)
    part_ref = refs.pop(0)
    offdiag_ref[...] = jnp.zeros_like(offdiag_ref)
    part_ref[...] = jnp.zeros_like(part_ref) if first else old_rest[...]

    own = block(place)

    @pl.when(is_listed(ancestors, number, own))
    def _own():
        summed = ((sums[0][...] + sums[1][...]) + sums[2][...]) + sums[3][...]
        part_ref[...] += dot(factor_ref[0], summed, 0)
        offdiag_ref[0] = -(summed if first else summed + old_rows[...])

    part_by_core(place, part_ref, 0, keep_ref, send_ref)
    if last:
        return
    cross_ref[...] = jnp.zeros_like(cross_ref)

    @pl.when(is_listed(ancestors, number + 1, own))
    def _cross():
        cross_ref[...] = dot(offdiag_ref[0], next_ref[0], 0)

    kept_ref[...] = cross_ref[...] + dot(part_ref[...], link_ref[0])
    part_by_core(place, kept_ref, 1, keep_ref, send_ref)


def rest_kernel(link_ref, cross_ref, part_ref, offdiag_ref, rest_ref, rows_ref):
    link = link_ref[0]
    rest_ref[...] = dot(cross_ref[...], link, 0) + dot(link, part_ref[...], 0)
    rows_ref[...] = dot(offdiag_ref[0], link)


def rest_of(link_factor, cross, link_part, offdiag, number):
    _, unit_rows, columns = offdiag.shape
    link = pl.BlockSpec((1, columns, columns), lambda *_: (number, 0, 0))
    rows = pl.BlockSpec((1, unit_rows, columns), lambda *_: (number, 0, 0))
    outs = [cross, jax.ShapeDtypeStruct((unit_rows, columns), jnp.float32)]
    outs = [jax.ShapeDtypeStruct(out.shape, jnp.float32) for out in outs]
    return run(
        rest_kernel, [], [link_factor, cross, link_part, offdiag],
        [link, whole(cross), whole(link_part), rows], [], outs, [whole(out) for out in outs],
        name="rest",
    )


def finish(number, block, place, ancestors, sums, factor, before, link_factor, chips, waits):
    nsuper, unit_rows, columns = factor.shape
    first, last = number == 0, number + 1 == nsuper
    slab = (1, unit_rows, columns)
    arrays, specs = list(sums), [whole(array) for array in sums]
    arrays.append(factor)
    specs.append(pl.BlockSpec(slab, lambda *_: (number, 0, 0)))
    alias = {}
    if not first:
        alias = {2 + len(arrays) + 2: 0}
        arrays += before
        specs += [whole(before[0]), whole(before[1])]
        specs.append(pl.BlockSpec((1, 8, LANES), lambda *_: (0, 0, 0)))
    if not last:
        arrays += [link_factor, factor]
        specs.append(pl.BlockSpec((1, columns, columns), lambda *_: (number, 0, 0)))
        specs.append(pl.BlockSpec(slab, lambda *_: (number + 1, 0, 0)))
    shape = jax.ShapeDtypeStruct
    groups = shape((1 if last else 2, chips, columns // (2 * chips), columns), jnp.float32)
    outs = [shape(factor.shape, jnp.float32), groups, groups]
    out_specs = [pl.BlockSpec(slab, lambda *_: (number, 0, 0)), whole(groups), whole(groups)]
    if not last:
        more = [shape((columns, columns), jnp.float32)] * 2
        outs += more
        out_specs += [whole(array) for array in more]
    return run(
        functools.partial(finish_kernel, number, last, first, block),
        [place, ancestors],
        arrays,
        specs,
        waits,
        outs,
        out_specs,
        scratch=[pltpu.VMEM((columns, columns), jnp.float32)],
        alias=alias,
        name="finish",
    )


def fold_kernel(place, keep_ref, received_ref, *out_refs):
    chip = place[0] // 2
    for o, out_ref in enumerate(out_refs):
        out_ref[...] = keep_ref[:, chip ^ o] + received_ref[:, chip ^ o]


def fold(place, keep, received):
    number, chips, rows, columns = keep.shape
    out = jax.ShapeDtypeStruct((number, rows, columns), jnp.float32)
    specs = [whole(keep)] * 2
    outs = [out] * chips
    return run(
        fold_kernel, [place], [keep, received], specs, [], outs, [whole(out)] * chips, name="fold"
    )


def fold_pair_kernel(place, *refs):
    *piece_refs, kept_ref, other_ref = refs
    mine = place[1] % 2
    for out_ref, index in ((kept_ref, mine), (other_ref, 1 - mine)):
        total = piece_refs[0][index]
        for ref in piece_refs[1:]:
            total = total + ref[index]
        out_ref[...] = total


def fold_pair(place, pieces, waits):
    out = jax.ShapeDtypeStruct(pieces[0].shape[1:], jnp.float32)
    specs = [whole(piece) for piece in pieces]
    return run(
        fold_pair_kernel, [place], pieces, specs, waits, [out] * 2, [whole(out)] * 2,
        name="fold_pair",
    )


def bases_kernel(nsuper, place, diag_ref, link_ref, *refs):
    diag_out, link_out, base_ref, next_ref = refs
    rows = diag_out.shape[1]
    mine = pl.ds(pl.multiple_of(place[0] * rows, rows), rows)
    base_ref[...] = diag_ref[0]
    diag_out[0] = base_ref[mine, :]
    for number in range(1, nsuper):
        link = link_ref[number - 1]
        next_ref[...] = dot(base_ref[...], link)
        link_out[number - 1] = next_ref[mine, :]
        base_ref[...] = diag_ref[number] + dot(link, next_ref[...], 0)
        diag_out[number] = base_ref[mine, :]


def bases_of(place, diag_inverse, link_factor, rows, waits):
    nsuper, columns, _ = diag_inverse.shape
    outs = [
        jax.ShapeDtypeStruct((nsuper, rows, columns), jnp.float32),
        jax.ShapeDtypeStruct((nsuper - 1, rows, columns), jnp.float32),
    ]
    return run(
        functools.partial(bases_kernel, nsuper),
        [place],
        [diag_inverse, link_factor],
        [whole(diag_inverse), whole(link_factor)],
        waits,
        outs,
        [whole(out) for out in outs],
        scratch=[pltpu.VMEM((columns, columns), jnp.float32)] * 2,
        name="bases",
    )


def outputs_kernel(place, *refs):
    diag_base, link_base, *sums, diag_out, link_out = refs
    steps = link_out.shape[0]
    for number in range(steps):
        pair = sums[2 * number : 2 * number + 2]

        def put(diag, link, number=number):
            diag_out[number] = diag[...] + diag_base[number]
            link_out[number] = -(link[...] + link_base[number])

        pl.when(place[1] % 2 == 0)(functools.partial(put, *pair))
        pl.when(place[1] % 2 == 1)(functools.partial(put, *pair[::-1]))
    diag_out[steps] = sums[-2][0] + sums[-1][0] + diag_base[steps]


def outputs(place, bases, sums):
    arrays = list(bases) + sums
    specs = [whole(array) for array in arrays]
    outs = [jax.ShapeDtypeStruct(base.shape, jnp.float32) for base in bases]
    return run(outputs_kernel, [place], arrays, specs, [], outs, specs[:2], name="outputs")


def to_column(pieces, ratio):
    return [pieces[0]] + [flip(pieces[o], "pcol", o * ratio) for o in range(1, len(pieces))]


def to_plane(pieces):
    return [pieces[0]] + [flip(pieces[o], "prow", o) for o in range(1, len(pieces))]


def to_plane_whole(factor, count, ratio):
    pieces = jnp.swapaxes(factor.reshape(factor.shape[0], count, -1), 0, 1)
    groups = [[c * ratio + k for c in range(count)] for k in range(ratio)]
    spread = lax.all_to_all(pieces, "pcol", 0, 0, axis_index_groups=groups)
    return lax.all_to_all(spread, "prow", 0, 0)


def gather_plane(own, pcol_count):
    return [own] + [flip(own, "pcol", offset) for offset in range(2, pcol_count, 2)]


def in_rows(gathered, count, ratio):
    _, _, unit_rows, width = gathered.shape
    split = gathered.reshape(count, ratio, count, unit_rows, width)
    rows = jnp.transpose(split, (1, 2, 3, 0, 4))
    return rows.reshape(ratio * count * unit_rows, count * width)


FOUR_SLOTS = ((3, 2, 1, 0), (0, 2, 3, 1), (3, 1, 0, 2), (0, 1, 2, 3))


def slots_of(count):
    return FOUR_SLOTS if count == len(FOUR_SLOTS) else (tuple(range(count)),) * count


def sum_over_four(place, slots):
    near = lax.ppermute(slots[0], "prow", [(0, 1), (3, 2), (1, 0), (2, 3)])
    middle = lax.ppermute(slots[1], "prow", [(1, 2), (2, 1)])
    total = lax.ppermute(slots[1], "prow", [(0, 2), (3, 1)])
    both, mine = pass_on(place, slots[2], slots[3], near)
    last = lax.ppermute(both, "prow", [(1, 3), (2, 0), (0, 1), (3, 2)])
    return [mine, total, middle, last, near]


def sum_over_line(place, slots, z):
    count = len(slots)
    if count == len(FOUR_SLOTS):
        return sum_over_four(place, slots)
    chunks = jnp.stack(slots)

    def chunk(index):
        return lax.dynamic_index_in_dim(chunks, jnp.clip(index, 0, count - 1), 0, keepdims=False)

    up = down = None
    for t in range(1, count):
        up_send, down_send = chunk(z + count - t), chunk(z + t - count)
        if up is not None:
            up_send, down_send = up_send + up, down_send + down
        up = lax.ppermute(up_send, "prow", [(i, i + 1) for i in range(min(t, count - 1))])
        down = lax.ppermute(
            down_send, "prow", [(i, i - 1) for i in range(max(count - t, 1), count)]
        )
    mine = chunk(z)
    none = jnp.zeros_like(mine)
    return [mine, none if up is None else up, none if down is None else down, none, mine]


def sum_plane(place, keep, send):
    pieces = fold(place, keep, flip(send, "pcol", 1))
    return [pieces[0]] + [flip(pieces[o], "pcol", 2 * o) for o in range(1, len(pieces))]


def sum_planes(pieces, count):
    bit = 1
    while True:
        total = add_up(pieces, [])
        if bit >= count:
            return [total, jnp.zeros_like(total)]
        pieces = [total, flip(total, "prow", bit)]
        bit *= 2
        if bit >= count:
            return pieces


def sum_pair_near(place, pieces, waits):
    kept, other = fold_pair(place, pieces, waits)
    return [kept, flip(other, "prow", 1)]


def sum_pair_far(pieces, count, waits):
    bit = 2
    while True:
        total = add_up(pieces, waits)
        if bit >= count:
            return [total, flip(total, "prow", 1)]
        pieces, waits = [total, flip(total, "prow", bit)], []
        bit *= 2


def body(inverse_tiles, factor, link_factor, diag_inverse, ancestors):
    row_count, col_count = inverse_tiles.shape
    nsuper, unit_rows, columns = factor.shape
    count = lax.axis_size("prow")
    pcol_count = lax.axis_size("pcol")
    ratio = col_count // row_count
    z = lax.axis_index("prow")
    pcol_index = lax.axis_index("pcol")
    width = columns // count
    place = jnp.stack([pcol_index, z, pcol_index // ratio]).astype(jnp.int32)
    slots = jnp.asarray(slots_of(count), jnp.int32)

    def own_block(place):
        return (place[0] * count + place[1]) * unit_rows // columns

    sent, turned, received, waits = [], [], [], []
    if width % LANES == 0:
        for number in range(nsuper):
            sent.append(to_column(cut(place, factor, number, count, waits), ratio))
            waits = received[-1][1:] if received else []
            turned.append(turn(place, sent[number], waits))
            waits = [turned[0][0]]
            received.append(to_plane(turned[number]))
    waits = [pieces[0] for pieces in received[:1]]
    bases = bases_of(place, diag_inverse, link_factor, columns // pcol_count, waits)
    rows, lates, gathered = [], [], []
    for number in range(nsuper):
        if received:
            gathered += [piece for later in sent[number + 1 : number + 2] for piece in later[1:]]
            own = arrange(place, received[number], gathered)
            found = gather_plane(own, pcol_count)
            gathered = found[1:]
            waits = [piece for later in received[number + 1 : number + 2] for piece in later[1:]]
            packed = pack(found, waits + (rows[-1][1:4] + late if rows else [bases[0]]))
            pieces = [packed, flip(packed, "pcol", 1)]
        else:
            own = to_plane_whole(factor[number], count, ratio)
            pieces = [in_rows(lax.all_gather(own, "pcol", axis=0), count, ratio)]
        middle = count // 2
        partial, starts = [], [0, middle, count] if received else [0, count]
        for start, stop in zip(starts, starts[1:]):
            partial += partial_product(
                place, slots, ancestors, inverse_tiles, pieces, ratio, columns, number, start, stop,
                [bases[0]],
            )
        rows.append(sum_over_line(place, partial, z))
        rows[-1] = rows[-1][:3] + rows[-1][:2:-1]
        late = [partial[-1]]
        lates.append(late)

    sums, before, pending = [], [], []
    for number in range(nsuper):
        last = number + 1 == nsuper
        waits = [] if last else rows[number + 1][2:4] + lates[number + 1]
        offdiag, keep, send, *link = finish(
            number, own_block, place, ancestors, rows[number][:3] + rows[number][4:], factor, before,
            link_factor, pcol_count // 2, waits + pending[:1],
        )
        if pending:
            sums += sum_pair_far(pending, count, [keep])
        group = sum_plane(place, keep, send)
        if not last:
            rest = rest_of(link_factor, *link, offdiag, number)
            before = [*rest, offdiag]
            pending = sum_pair_near(place, group, rest[:1])
    sums += sum_planes(group, count)
    return (offdiag, *outputs(place, bases, sums))


def solution(mesh):
    in_specs = (P("pcol", "prow"), P(None, ("pcol", "prow"), None), P(), P(), P())
    out_specs = (P(None, ("pcol", "prow"), None), P(None, "pcol", None), P(None, "pcol", None))
    return jax.shard_map(body, mesh=mesh, in_specs=in_specs, out_specs=out_specs, check_vma=False)
```

```python
import functools

import jax
import jax.numpy as jnp
from jax import lax
from jax.experimental import pallas as pl
from jax.experimental.pallas import tpu as pltpu
from jax.sharding import PartitionSpec as P

BOTH = ("prow", "pcol")
VMEM_LIMIT = 32 * 1024 * 1024
LANES = 128


def halves(value):
    high = value.astype(jnp.bfloat16)
    low = (value - high.astype(jnp.float32)).astype(jnp.bfloat16)
    return high, low


def flip(value, axis, bit):
    return lax.ppermute(value, axis, [(i, i ^ bit) for i in range(lax.axis_size(axis))])


def run(
    kernel, scalars, arrays, specs, waits, outs, out_specs, grid=(1,), scratch=(), alias=None, name=None
):
    def corner(array):
        block = (1,) * (array.ndim - 2) + (8, LANES)
        return pl.BlockSpec(block, lambda *_: (0,) * array.ndim)

    def body(*refs):
        first = len(scalars) + len(arrays)
        kernel(*refs[:first], *refs[first + len(waits) :])

    return pl.pallas_call(
        body,
        grid_spec=pltpu.PrefetchScalarGridSpec(
            num_scalar_prefetch=len(scalars),
            grid=grid,
            in_specs=list(specs) + [corner(array) for array in waits],
            out_specs=out_specs,
            scratch_shapes=list(scratch),
        ),
        out_shape=outs,
        input_output_aliases=alias or {},
        compiler_params=pltpu.CompilerParams(vmem_limit_bytes=VMEM_LIMIT),
        cost_estimate=pl.CostEstimate(flops=0, bytes_accessed=0, transcendentals=0),
        name=name,
    )(*scalars, *arrays, *waits)


def whole(array):
    return pl.BlockSpec(array.shape, lambda *_: (0,) * array.ndim)


def cut_kernel(place, factor_ref, *out_refs):
    width = out_refs[0].shape[1]
    for o, out_ref in enumerate(out_refs):
        start = pl.multiple_of((place[2] ^ o) * width, width)
        out_ref[...] = factor_ref[0, :, pl.ds(start, width)]


def cut(place, factor, number, count, waits):
    _, unit_rows, columns = factor.shape
    piece = jax.ShapeDtypeStruct((unit_rows, columns // count), factor.dtype)
    spec = pl.BlockSpec((1, unit_rows, columns), lambda *_: (number, 0, 0))
    outs = [piece] * count
    specs = [whole(piece)] * count
    return run(cut_kernel, [place], [factor], [spec], waits, outs, specs, name="cut")


def turn_kernel(place, *refs):
    count = len(refs) // 2
    for shift in range(count):

        @pl.when((place[1] ^ place[2]) == shift)
        def _copy(shift=shift):
            for o in range(count):
                refs[count + o][...] = refs[o ^ shift][...]


def turn(place, pieces, waits):
    count = len(pieces)
    piece = jax.ShapeDtypeStruct(pieces[0].shape, pieces[0].dtype)
    specs = [whole(piece)] * count
    return run(turn_kernel, [place], pieces, specs, waits, [piece] * count, specs, name="turn")


def arrange_kernel(place, *refs):
    out_ref = refs[-1]
    for o, piece_ref in enumerate(refs[:-1]):
        out_ref[place[1] ^ o] = piece_ref[...]


def arrange(place, pieces, waits):
    out = jax.ShapeDtypeStruct((len(pieces),) + pieces[0].shape, pieces[0].dtype)
    specs = [whole(piece) for piece in pieces]
    return run(arrange_kernel, [place], pieces, specs, waits, out, whole(out), name="arrange")


def pack_kernel(*refs):
    for index, ref in enumerate(refs[:-1]):
        refs[-1][index] = ref[...]


def pack(pieces, waits):
    out = jax.ShapeDtypeStruct((len(pieces),) + pieces[0].shape, pieces[0].dtype)
    specs = [whole(piece) for piece in pieces]
    return run(pack_kernel, [], pieces, specs, waits, out, whole(out), name="pack")


def add_kernel(*refs):
    total = refs[0][...]
    for ref in refs[1:-1]:
        total = total + ref[...]
    refs[-1][...] = total


def add_up(arrays, waits):
    out = jax.ShapeDtypeStruct(arrays[0].shape, arrays[0].dtype)
    specs = [whole(array) for array in arrays]
    return run(add_kernel, [], arrays, specs, waits, out, whole(out), name="add_up")


def is_listed(ancestors, number, block):
    found = ancestors[number, 0] == block
    for i in range(1, ancestors.shape[1]):
        found = found | (ancestors[number, i] == block)
    return found


def partial_kernel(sides, ratio, count, number, start, place, slots, ancestors, tile_ref, *refs):
    piece_refs, out_refs, right_ref = refs[:sides], refs[sides:-1], refs[-1]
    chunk_rows, columns = out_refs[0].shape
    blocks = tile_ref.shape[1] // columns
    step = pl.program_id(0)

    def listed(block):
        return is_listed(ancestors, number, block)

    @pl.when(step == 0)
    def _assemble():
        def put(first, lanes, value):
            high, low = halves(value)
            for index in range(value.shape[0] // columns):
                part = slice(index * columns, (index + 1) * columns)
                for turn, side in enumerate((high, low, high)):
                    right_ref[first + index, pl.ds(turn * columns, columns), lanes] = side[part]

        if len(piece_refs) == 1:
            put(0, slice(None), piece_refs[0][...])
            return
        for side, ref in enumerate(piece_refs):
            chips, parts, unit_rows, width = ref.shape
            span = parts * unit_rows
            for o in range(chips):
                owner = place[0] ^ (2 * o + side)
                lanes = pl.ds(pl.multiple_of(owner // ratio * width, width), width)
                put(owner % ratio * (span // columns), lanes, ref[o].reshape(span, width))

    def multiply(out_ref):
        out_ref[...] = jnp.zeros_like(out_ref)
        chunk = place[0] * count + slots[place[1], start + step]

        @pl.when(listed(chunk * chunk_rows // columns))
        def _chunk():
            def add(block, carry):
                @pl.when(listed(place[1] * blocks + block))
                def _block():
                    span = pl.ds(pl.multiple_of(block * columns, columns), columns)
                    high, low = halves(tile_ref[:, span])
                    left = jnp.concatenate([high, high, low], axis=1)
                    out_ref[...] += jnp.dot(
                        left, right_ref[block], preferred_element_type=jnp.float32
                    )

                return carry

            lax.fori_loop(0, blocks, add, 0)

    for index, out_ref in enumerate(out_refs):
        pl.when(step == index)(functools.partial(multiply, out_ref))


def partial_product(
    place, slots, ancestors, tiles, pieces, ratio, columns, number, start, stop, waits
):
    rows, cols = tiles.shape
    count = slots.shape[0]
    out = jax.ShapeDtypeStruct((rows // count, columns), jnp.float32)
    tile = pl.BlockSpec((rows // count, cols), lambda i, p, s, a: (s[p[1], start + i], 0))
    return run(
        functools.partial(partial_kernel, len(pieces), ratio, count, number, start),
        [place, slots, ancestors],
        [tiles] + pieces,
        [tile] + [whole(piece) for piece in pieces],
        waits,
        [out] * (stop - start),
        [whole(out)] * (stop - start),
        grid=(stop - start,),
        scratch=[pltpu.VMEM((cols // columns, 3 * columns, columns), jnp.bfloat16)],
        name="partial_product",
    )


def dot(left, right, side=1):
    def one(a, b):
        return lax.dot_general(
            a, b, (((side,), (0,)), ((), ())), preferred_element_type=jnp.float32
        )

    left_high, left_low = halves(left)
    right_high, right_low = halves(right)
    return one(left_high, right_high) + (one(left_high, right_low) + one(left_low, right_high))


def part_by_core(place, matrix_ref, index, keep_ref, send_ref):
    _, chips, rows, _ = keep_ref.shape
    core = place[0] % 2
    for chip in range(chips):
        for ref, side in ((keep_ref, core), (send_ref, 1 - core)):
            first = pl.multiple_of((chip * 2 + side) * rows, rows)
            ref[index, chip] = matrix_ref[pl.ds(first, rows), :]


def finish_kernel(number, last, first, block, place, ancestors, *refs):
    refs = list(refs)
    sums, factor_ref = [refs.pop(0) for _ in range(4)], refs.pop(0)
    if not first:
        old_rest, old_rows, _ = (refs.pop(0) for _ in range(3))
    if not last:
        link_ref, next_ref = refs.pop(0), refs.pop(0)
    offdiag_ref, keep_ref, send_ref = (refs.pop(0) for _ in range(3))
    if not last:
        cross_ref, kept_ref = refs.pop(0), refs.pop(0)
    part_ref = refs.pop(0)
    offdiag_ref[...] = jnp.zeros_like(offdiag_ref)
    part_ref[...] = jnp.zeros_like(part_ref) if first else old_rest[...]

    own = block(place)

    @pl.when(is_listed(ancestors, number, own))
    def _own():
        summed = ((sums[0][...] + sums[1][...]) + sums[2][...]) + sums[3][...]
        part_ref[...] += dot(factor_ref[0], summed, 0)
        offdiag_ref[0] = -(summed if first else summed + old_rows[...])

    part_by_core(place, part_ref, 0, keep_ref, send_ref)
    if last:
        return
    cross_ref[...] = jnp.zeros_like(cross_ref)

    @pl.when(is_listed(ancestors, number + 1, own))
    def _cross():
        cross_ref[...] = dot(offdiag_ref[0], next_ref[0], 0)

    kept_ref[...] = cross_ref[...] + dot(part_ref[...], link_ref[0])
    part_by_core(place, kept_ref, 1, keep_ref, send_ref)


def rest_kernel(link_ref, cross_ref, part_ref, offdiag_ref, rest_ref, rows_ref):
    link = link_ref[0]
    rest_ref[...] = dot(cross_ref[...], link, 0) + dot(link, part_ref[...], 0)
    rows_ref[...] = dot(offdiag_ref[0], link)


def rest_of(link_factor, cross, link_part, offdiag, number):
    _, unit_rows, columns = offdiag.shape
    link = pl.BlockSpec((1, columns, columns), lambda *_: (number, 0, 0))
    rows = pl.BlockSpec((1, unit_rows, columns), lambda *_: (number, 0, 0))
    outs = [cross, jax.ShapeDtypeStruct((unit_rows, columns), jnp.float32)]
    outs = [jax.ShapeDtypeStruct(out.shape, jnp.float32) for out in outs]
    return run(
        rest_kernel, [], [link_factor, cross, link_part, offdiag],
        [link, whole(cross), whole(link_part), rows], [], outs, [whole(out) for out in outs],
        name="rest",
    )


def finish(number, block, place, ancestors, sums, factor, before, link_factor, chips, waits):
    nsuper, unit_rows, columns = factor.shape
    first, last = number == 0, number + 1 == nsuper
    slab = (1, unit_rows, columns)
    arrays, specs = list(sums), [whole(array) for array in sums]
    arrays.append(factor)
    specs.append(pl.BlockSpec(slab, lambda *_: (number, 0, 0)))
    alias = {}
    if not first:
        alias = {2 + len(arrays) + 2: 0}
        arrays += before
        specs += [whole(before[0]), whole(before[1])]
        specs.append(pl.BlockSpec((1, 8, LANES), lambda *_: (0, 0, 0)))
    if not last:
        arrays += [link_factor, factor]
        specs.append(pl.BlockSpec((1, columns, columns), lambda *_: (number, 0, 0)))
        specs.append(pl.BlockSpec(slab, lambda *_: (number + 1, 0, 0)))
    shape = jax.ShapeDtypeStruct
    groups = shape((1 if last else 2, chips, columns // (2 * chips), columns), jnp.float32)
    outs = [shape(factor.shape, jnp.float32), groups, groups]
    out_specs = [pl.BlockSpec(slab, lambda *_: (number, 0, 0)), whole(groups), whole(groups)]
    if not last:
        more = [shape((columns, columns), jnp.float32)] * 2
        outs += more
        out_specs += [whole(array) for array in more]
    return run(
        functools.partial(finish_kernel, number, last, first, block),
        [place, ancestors],
        arrays,
        specs,
        waits,
        outs,
        out_specs,
        scratch=[pltpu.VMEM((columns, columns), jnp.float32)],
        alias=alias,
        name="finish",
    )


def fold_kernel(place, keep_ref, received_ref, *out_refs):
    chip = place[0] // 2
    for o, out_ref in enumerate(out_refs):
        out_ref[...] = keep_ref[:, chip ^ o] + received_ref[:, chip ^ o]


def fold(place, keep, received):
    number, chips, rows, columns = keep.shape
    out = jax.ShapeDtypeStruct((number, rows, columns), jnp.float32)
    specs = [whole(keep)] * 2
    outs = [out] * chips
    return run(
        fold_kernel, [place], [keep, received], specs, [], outs, [whole(out)] * chips, name="fold"
    )


def fold_pair_kernel(place, *refs):
    *piece_refs, kept_ref, other_ref = refs
    mine = place[1] % 2
    for out_ref, index in ((kept_ref, mine), (other_ref, 1 - mine)):
        total = piece_refs[0][index]
        for ref in piece_refs[1:]:
            total = total + ref[index]
        out_ref[...] = total


def fold_pair(place, pieces, waits):
    out = jax.ShapeDtypeStruct(pieces[0].shape[1:], jnp.float32)
    specs = [whole(piece) for piece in pieces]
    return run(
        fold_pair_kernel, [place], pieces, specs, waits, [out] * 2, [whole(out)] * 2,
        name="fold_pair",
    )


def bases_kernel(nsuper, place, diag_ref, link_ref, *refs):
    diag_out, link_out, base_ref, next_ref = refs
    rows = diag_out.shape[1]
    mine = pl.ds(pl.multiple_of(place[0] * rows, rows), rows)
    base_ref[...] = diag_ref[0]
    diag_out[0] = base_ref[mine, :]
    for number in range(1, nsuper):
        link = link_ref[number - 1]
        next_ref[...] = dot(base_ref[...], link)
        link_out[number - 1] = next_ref[mine, :]
        base_ref[...] = diag_ref[number] + dot(link, next_ref[...], 0)
        diag_out[number] = base_ref[mine, :]


def bases_of(place, diag_inverse, link_factor, rows, waits):
    nsuper, columns, _ = diag_inverse.shape
    outs = [
        jax.ShapeDtypeStruct((nsuper, rows, columns), jnp.float32),
        jax.ShapeDtypeStruct((nsuper - 1, rows, columns), jnp.float32),
    ]
    return run(
        functools.partial(bases_kernel, nsuper),
        [place],
        [diag_inverse, link_factor],
        [whole(diag_inverse), whole(link_factor)],
        waits,
        outs,
        [whole(out) for out in outs],
        scratch=[pltpu.VMEM((columns, columns), jnp.float32)] * 2,
        name="bases",
    )


def outputs_kernel(place, *refs):
    diag_base, link_base, *sums, diag_out, link_out = refs
    steps = link_out.shape[0]
    for number in range(steps):
        pair = sums[2 * number : 2 * number + 2]

        def put(diag, link, number=number):
            diag_out[number] = diag[...] + diag_base[number]
            link_out[number] = -(link[...] + link_base[number])

        pl.when(place[1] % 2 == 0)(functools.partial(put, *pair))
        pl.when(place[1] % 2 == 1)(functools.partial(put, *pair[::-1]))
    diag_out[steps] = sums[-2][0] + sums[-1][0] + diag_base[steps]


def outputs(place, bases, sums):
    arrays = list(bases) + sums
    specs = [whole(array) for array in arrays]
    outs = [jax.ShapeDtypeStruct(base.shape, jnp.float32) for base in bases]
    return run(outputs_kernel, [place], arrays, specs, [], outs, specs[:2], name="outputs")


def to_column(pieces, ratio):
    return [pieces[0]] + [flip(pieces[o], "pcol", o * ratio) for o in range(1, len(pieces))]


def to_plane(pieces):
    return [pieces[0]] + [flip(pieces[o], "prow", o) for o in range(1, len(pieces))]


def to_plane_whole(factor, count, ratio):
    pieces = jnp.swapaxes(factor.reshape(factor.shape[0], count, -1), 0, 1)
    groups = [[c * ratio + k for c in range(count)] for k in range(ratio)]
    spread = lax.all_to_all(pieces, "pcol", 0, 0, axis_index_groups=groups)
    return lax.all_to_all(spread, "prow", 0, 0)


def gather_plane(own, pcol_count):
    return [own] + [flip(own, "pcol", offset) for offset in range(2, pcol_count, 2)]


def in_rows(gathered, count, ratio):
    _, _, unit_rows, width = gathered.shape
    split = gathered.reshape(count, ratio, count, unit_rows, width)
    rows = jnp.transpose(split, (1, 2, 3, 0, 4))
    return rows.reshape(ratio * count * unit_rows, count * width)


FOUR_SLOTS = ((3, 2, 1, 0), (2, 0, 3, 1), (1, 3, 0, 2), (0, 1, 2, 3))


def slots_of(count):
    return FOUR_SLOTS if count == len(FOUR_SLOTS) else (tuple(range(count)),) * count


def sum_over_four(slots):
    near = lax.ppermute(slots[0], "prow", [(0, 1), (3, 2)])
    total = lax.ppermute(slots[1], "prow", [(0, 2), (2, 3), (3, 1), (1, 0)])
    middle = lax.ppermute(slots[0], "prow", [(1, 2), (2, 1)])
    both = add_up([slots[2], near], [])
    last = lax.ppermute(both, "prow", [(1, 3), (2, 0), (0, 1), (3, 2)])
    return [slots[3], total, middle, last, near]


def sum_over_line(slots, z):
    count = len(slots)
    if count == len(FOUR_SLOTS):
        return sum_over_four(slots)
    chunks = jnp.stack(slots)

    def chunk(index):
        return lax.dynamic_index_in_dim(chunks, jnp.clip(index, 0, count - 1), 0, keepdims=False)

    up = down = None
    for t in range(1, count):
        up_send, down_send = chunk(z + count - t), chunk(z + t - count)
        if up is not None:
            up_send, down_send = up_send + up, down_send + down
        up = lax.ppermute(up_send, "prow", [(i, i + 1) for i in range(min(t, count - 1))])
        down = lax.ppermute(
            down_send, "prow", [(i, i - 1) for i in range(max(count - t, 1), count)]
        )
    mine = chunk(z)
    none = jnp.zeros_like(mine)
    return [mine, none if up is None else up, none if down is None else down, none, mine]


def sum_plane(place, keep, send):
    pieces = fold(place, keep, flip(send, "pcol", 1))
    return [pieces[0]] + [flip(pieces[o], "pcol", 2 * o) for o in range(1, len(pieces))]


def sum_planes(pieces, count):
    bit = 1
    while True:
        total = add_up(pieces, [])
        if bit >= count:
            return [total, jnp.zeros_like(total)]
        pieces = [total, flip(total, "prow", bit)]
        bit *= 2
        if bit >= count:
            return pieces


def sum_pair_near(place, pieces, waits):
    kept, other = fold_pair(place, pieces, waits)
    return [kept, flip(other, "prow", 1)]


def sum_pair_far(pieces, count, waits):
    bit = 2
    while True:
        total = add_up(pieces, waits)
        if bit >= count:
            return [total, flip(total, "prow", 1)]
        pieces, waits = [total, flip(total, "prow", bit)], []
        bit *= 2


def body(inverse_tiles, factor, link_factor, diag_inverse, ancestors):
    row_count, col_count = inverse_tiles.shape
    nsuper, unit_rows, columns = factor.shape
    count = lax.axis_size("prow")
    pcol_count = lax.axis_size("pcol")
    ratio = col_count // row_count
    z = lax.axis_index("prow")
    pcol_index = lax.axis_index("pcol")
    width = columns // count
    place = jnp.stack([pcol_index, z, pcol_index // ratio]).astype(jnp.int32)
    slots = jnp.asarray(slots_of(count), jnp.int32)

    def own_block(place):
        return (place[0] * count + place[1]) * unit_rows // columns

    sent, turned, received, waits = [], [], [], []
    if width % LANES == 0:
        for number in range(nsuper):
            sent.append(to_column(cut(place, factor, number, count, waits), ratio))
            waits = received[-1][1:] if received else []
            turned.append(turn(place, sent[number], waits))
            waits = [turned[0][0]]
            received.append(to_plane(turned[number]))
    waits = [pieces[0] for pieces in received[:1]]
    bases = bases_of(place, diag_inverse, link_factor, columns // pcol_count, waits)
    rows, lates, gathered = [], [], []
    for number in range(nsuper):
        if received:
            gathered += [piece for later in sent[number + 1 : number + 2] for piece in later[1:]]
            own = arrange(place, received[number], gathered)
            found = gather_plane(own, pcol_count)
            gathered = found[1:]
            waits = [piece for later in received[number + 1 : number + 2] for piece in later[1:]]
            packed = pack(found, waits + (rows[-1][1:4] + late if rows else [bases[0]]))
            pieces = [packed, flip(packed, "pcol", 1)]
        else:
            own = to_plane_whole(factor[number], count, ratio)
            pieces = [in_rows(lax.all_gather(own, "pcol", axis=0), count, ratio)]
        middle = 1 if rows else count // 2
        partial, starts = [], [0, middle, count] if received else [0, count]
        for start, stop in zip(starts, starts[1:]):
            partial += partial_product(
                place, slots, ancestors, inverse_tiles, pieces, ratio, columns, number, start, stop,
                [bases[0]],
            )
        rows.append(sum_over_line(partial, z))
        rows[-1] = rows[-1][:3] + rows[-1][:2:-1]
        late = [partial[-1]]
        lates.append(late)

    sums, before, pending = [], [], []
    for number in range(nsuper):
        last = number + 1 == nsuper
        waits = [] if last else rows[number + 1][2:4] + lates[number + 1]
        offdiag, keep, send, *link = finish(
            number, own_block, place, ancestors, rows[number][:3] + rows[number][4:], factor, before,
            link_factor, pcol_count // 2, waits + pending,
        )
        if pending:
            sums += sum_pair_far(pending, count, [keep])
        group = sum_plane(place, keep, send)
        if not last:
            rest = rest_of(link_factor, *link, offdiag, number)
            before = [*rest, offdiag]
            pending = sum_pair_near(place, group, rest[:1])
    sums += sum_planes(group, count)
    return (offdiag, *outputs(place, bases, sums))


def solution(mesh):
    in_specs = (P("pcol", "prow"), P(None, ("pcol", "prow"), None), P(), P(), P())
    out_specs = (P(None, ("pcol", "prow"), None), P(None, "pcol", None), P(None, "pcol", None))
    return jax.shard_map(body, mesh=mesh, in_specs=in_specs, out_specs=out_specs, check_vma=False)
```

```python
import functools

import jax
import jax.numpy as jnp
from jax import lax
from jax.experimental import pallas as pl
from jax.experimental.pallas import tpu as pltpu
from jax.sharding import PartitionSpec as P

BOTH = ("prow", "pcol")
VMEM_LIMIT = 32 * 1024 * 1024
LANES = 128


def halves(value):
    high = value.astype(jnp.bfloat16)
    low = (value - high.astype(jnp.float32)).astype(jnp.bfloat16)
    return high, low


def flip(value, axis, bit):
    return lax.ppermute(value, axis, [(i, i ^ bit) for i in range(lax.axis_size(axis))])


def run(
    kernel, scalars, arrays, specs, waits, outs, out_specs, grid=(1,), scratch=(), alias=None, name=None
):
    def corner(array):
        block = (1,) * (array.ndim - 2) + (8, LANES)
        return pl.BlockSpec(block, lambda *_: (0,) * array.ndim)

    def body(*refs):
        first = len(scalars) + len(arrays)
        kernel(*refs[:first], *refs[first + len(waits) :])

    return pl.pallas_call(
        body,
        grid_spec=pltpu.PrefetchScalarGridSpec(
            num_scalar_prefetch=len(scalars),
            grid=grid,
            in_specs=list(specs) + [corner(array) for array in waits],
            out_specs=out_specs,
            scratch_shapes=list(scratch),
        ),
        out_shape=outs,
        input_output_aliases=alias or {},
        compiler_params=pltpu.CompilerParams(vmem_limit_bytes=VMEM_LIMIT),
        cost_estimate=pl.CostEstimate(flops=0, bytes_accessed=0, transcendentals=0),
        name=name,
    )(*scalars, *arrays, *waits)


def whole(array):
    return pl.BlockSpec(array.shape, lambda *_: (0,) * array.ndim)


def cut_kernel(place, factor_ref, *out_refs):
    width = out_refs[0].shape[1]
    for o, out_ref in enumerate(out_refs):
        start = pl.multiple_of((place[2] ^ o) * width, width)
        out_ref[...] = factor_ref[0, :, pl.ds(start, width)]


def cut(place, factor, number, count, waits):
    _, unit_rows, columns = factor.shape
    piece = jax.ShapeDtypeStruct((unit_rows, columns // count), factor.dtype)
    spec = pl.BlockSpec((1, unit_rows, columns), lambda *_: (number, 0, 0))
    outs = [piece] * count
    specs = [whole(piece)] * count
    return run(cut_kernel, [place], [factor], [spec], waits, outs, specs, name="cut")


def turn_kernel(place, *refs):
    count = len(refs) // 2
    for shift in range(count):

        @pl.when((place[1] ^ place[2]) == shift)
        def _copy(shift=shift):
            for o in range(count):
                refs[count + o][...] = refs[o ^ shift][...]


def turn(place, pieces, waits):
    count = len(pieces)
    piece = jax.ShapeDtypeStruct(pieces[0].shape, pieces[0].dtype)
    specs = [whole(piece)] * count
    return run(turn_kernel, [place], pieces, specs, waits, [piece] * count, specs, name="turn")


def arrange_kernel(place, *refs):
    out_ref = refs[-1]
    for o, piece_ref in enumerate(refs[:-1]):
        out_ref[place[1] ^ o] = piece_ref[...]


def arrange(place, pieces, waits):
    out = jax.ShapeDtypeStruct((len(pieces),) + pieces[0].shape, pieces[0].dtype)
    specs = [whole(piece) for piece in pieces]
    return run(arrange_kernel, [place], pieces, specs, waits, out, whole(out), name="arrange")


def pack_kernel(*refs):
    for index, ref in enumerate(refs[:-1]):
        refs[-1][index] = ref[...]


def pack(pieces, waits):
    out = jax.ShapeDtypeStruct((len(pieces),) + pieces[0].shape, pieces[0].dtype)
    specs = [whole(piece) for piece in pieces]
    return run(pack_kernel, [], pieces, specs, waits, out, whole(out), name="pack")


def add_kernel(*refs):
    total = refs[0][...]
    for ref in refs[1:-1]:
        total = total + ref[...]
    refs[-1][...] = total


def add_up(arrays, waits):
    out = jax.ShapeDtypeStruct(arrays[0].shape, arrays[0].dtype)
    specs = [whole(array) for array in arrays]
    return run(add_kernel, [], arrays, specs, waits, out, whole(out), name="add_up")


def is_listed(ancestors, number, block):
    found = ancestors[number, 0] == block
    for i in range(1, ancestors.shape[1]):
        found = found | (ancestors[number, i] == block)
    return found


def partial_kernel(sides, ratio, count, number, start, place, slots, ancestors, tile_ref, *refs):
    piece_refs, out_refs, right_ref = refs[:sides], refs[sides:-1], refs[-1]
    chunk_rows, columns = out_refs[0].shape
    blocks = tile_ref.shape[1] // columns
    step = pl.program_id(0)

    def listed(block):
        return is_listed(ancestors, number, block)

    @pl.when(step == 0)
    def _assemble():
        def put(first, lanes, value):
            high, low = halves(value)
            for index in range(value.shape[0] // columns):
                part = slice(index * columns, (index + 1) * columns)
                for turn, side in enumerate((high, low, high)):
                    right_ref[first + index, pl.ds(turn * columns, columns), lanes] = side[part]

        if len(piece_refs) == 1:
            put(0, slice(None), piece_refs[0][...])
            return
        for side, ref in enumerate(piece_refs):
            chips, parts, unit_rows, width = ref.shape
            span = parts * unit_rows
            for o in range(chips):
                owner = place[0] ^ (2 * o + side)
                lanes = pl.ds(pl.multiple_of(owner // ratio * width, width), width)
                put(owner % ratio * (span // columns), lanes, ref[o].reshape(span, width))

    def multiply(out_ref):
        out_ref[...] = jnp.zeros_like(out_ref)
        chunk = place[0] * count + slots[place[1], start + step]

        @pl.when(listed(chunk * chunk_rows // columns))
        def _chunk():
            def add(block, carry):
                @pl.when(listed(place[1] * blocks + block))
                def _block():
                    span = pl.ds(pl.multiple_of(block * columns, columns), columns)
                    high, low = halves(tile_ref[:, span])
                    left = jnp.concatenate([high, high, low], axis=1)
                    out_ref[...] += jnp.dot(
                        left, right_ref[block], preferred_element_type=jnp.float32
                    )

                return carry

            lax.fori_loop(0, blocks, add, 0)

    for index, out_ref in enumerate(out_refs):
        pl.when(step == index)(functools.partial(multiply, out_ref))


def partial_product(
    place, slots, ancestors, tiles, pieces, ratio, columns, number, start, stop, waits
):
    rows, cols = tiles.shape
    count = slots.shape[0]
    out = jax.ShapeDtypeStruct((rows // count, columns), jnp.float32)
    tile = pl.BlockSpec((rows // count, cols), lambda i, p, s, a: (s[p[1], start + i], 0))
    return run(
        functools.partial(partial_kernel, len(pieces), ratio, count, number, start),
        [place, slots, ancestors],
        [tiles] + pieces,
        [tile] + [whole(piece) for piece in pieces],
        waits,
        [out] * (stop - start),
        [whole(out)] * (stop - start),
        grid=(stop - start,),
        scratch=[pltpu.VMEM((cols // columns, 3 * columns, columns), jnp.bfloat16)],
        name="partial_product",
    )


def dot(left, right, side=1):
    def one(a, b):
        return lax.dot_general(
            a, b, (((side,), (0,)), ((), ())), preferred_element_type=jnp.float32
        )

    left_high, left_low = halves(left)
    right_high, right_low = halves(right)
    return one(left_high, right_high) + (one(left_high, right_low) + one(left_low, right_high))


def part_by_core(place, matrix_ref, index, keep_ref, send_ref):
    _, chips, rows, _ = keep_ref.shape
    core = place[0] % 2
    for chip in range(chips):
        for ref, side in ((keep_ref, core), (send_ref, 1 - core)):
            first = pl.multiple_of((chip * 2 + side) * rows, rows)
            ref[index, chip] = matrix_ref[pl.ds(first, rows), :]


def finish_kernel(number, last, first, block, place, ancestors, *refs):
    refs = list(refs)
    sums, factor_ref = [refs.pop(0) for _ in range(2)], refs.pop(0)
    if not first:
        old_rest, old_rows, _ = (refs.pop(0) for _ in range(3))
    if not last:
        link_ref, next_ref = refs.pop(0), refs.pop(0)
    offdiag_ref, keep_ref, send_ref = (refs.pop(0) for _ in range(3))
    if not last:
        cross_ref, kept_ref = refs.pop(0), refs.pop(0)
    part_ref = refs.pop(0)
    offdiag_ref[...] = jnp.zeros_like(offdiag_ref)
    part_ref[...] = jnp.zeros_like(part_ref) if first else old_rest[...]

    own = block(place)

    @pl.when(is_listed(ancestors, number, own))
    def _own():
        summed = sums[0][...] + sums[1][...]
        part_ref[...] += dot(factor_ref[0], summed, 0)
        offdiag_ref[0] = -(summed if first else summed + old_rows[...])

    part_by_core(place, part_ref, 0, keep_ref, send_ref)
    if last:
        return
    cross_ref[...] = jnp.zeros_like(cross_ref)

    @pl.when(is_listed(ancestors, number + 1, own))
    def _cross():
        cross_ref[...] = dot(offdiag_ref[0], next_ref[0], 0)

    kept_ref[...] = cross_ref[...] + dot(part_ref[...], link_ref[0])
    part_by_core(place, kept_ref, 1, keep_ref, send_ref)


def rest_kernel(link_ref, cross_ref, part_ref, offdiag_ref, rest_ref, rows_ref):
    link = link_ref[0]
    rest_ref[...] = dot(cross_ref[...], link, 0) + dot(link, part_ref[...], 0)
    rows_ref[...] = dot(offdiag_ref[0], link)


def rest_of(link_factor, cross, link_part, offdiag, number):
    _, unit_rows, columns = offdiag.shape
    link = pl.BlockSpec((1, columns, columns), lambda *_: (number, 0, 0))
    rows = pl.BlockSpec((1, unit_rows, columns), lambda *_: (number, 0, 0))
    outs = [cross, jax.ShapeDtypeStruct((unit_rows, columns), jnp.float32)]
    outs = [jax.ShapeDtypeStruct(out.shape, jnp.float32) for out in outs]
    return run(
        rest_kernel, [], [link_factor, cross, link_part, offdiag],
        [link, whole(cross), whole(link_part), rows], [], outs, [whole(out) for out in outs],
        name="rest",
    )


def finish(number, block, place, ancestors, sums, factor, before, link_factor, chips, waits):
    nsuper, unit_rows, columns = factor.shape
    first, last = number == 0, number + 1 == nsuper
    slab = (1, unit_rows, columns)
    arrays, specs = list(sums), [whole(array) for array in sums]
    arrays.append(factor)
    specs.append(pl.BlockSpec(slab, lambda *_: (number, 0, 0)))
    alias = {}
    if not first:
        alias = {2 + len(arrays) + 2: 0}
        arrays += before
        specs += [whole(before[0]), whole(before[1])]
        specs.append(pl.BlockSpec((1, 8, LANES), lambda *_: (0, 0, 0)))
    if not last:
        arrays += [link_factor, factor]
        specs.append(pl.BlockSpec((1, columns, columns), lambda *_: (number, 0, 0)))
        specs.append(pl.BlockSpec(slab, lambda *_: (number + 1, 0, 0)))
    shape = jax.ShapeDtypeStruct
    groups = shape((1 if last else 2, chips, columns // (2 * chips), columns), jnp.float32)
    outs = [shape(factor.shape, jnp.float32), groups, groups]
    out_specs = [pl.BlockSpec(slab, lambda *_: (number, 0, 0)), whole(groups), whole(groups)]
    if not last:
        more = [shape((columns, columns), jnp.float32)] * 2
        outs += more
        out_specs += [whole(array) for array in more]
    return run(
        functools.partial(finish_kernel, number, last, first, block),
        [place, ancestors],
        arrays,
        specs,
        waits,
        outs,
        out_specs,
        scratch=[pltpu.VMEM((columns, columns), jnp.float32)],
        alias=alias,
        name="finish",
    )


def fold_kernel(place, keep_ref, received_ref, *out_refs):
    chip = place[0] // 2
    for o, out_ref in enumerate(out_refs):
        out_ref[...] = keep_ref[:, chip ^ o] + received_ref[:, chip ^ o]


def fold(place, keep, received):
    number, chips, rows, columns = keep.shape
    out = jax.ShapeDtypeStruct((number, rows, columns), jnp.float32)
    specs = [whole(keep)] * 2
    outs = [out] * chips
    return run(
        fold_kernel, [place], [keep, received], specs, [], outs, [whole(out)] * chips, name="fold"
    )


def fold_pair_kernel(place, *refs):
    *piece_refs, kept_ref, other_ref = refs
    mine = place[1] % 2
    for out_ref, index in ((kept_ref, mine), (other_ref, 1 - mine)):
        total = piece_refs[0][index]
        for ref in piece_refs[1:]:
            total = total + ref[index]
        out_ref[...] = total


def fold_pair(place, pieces, waits):
    out = jax.ShapeDtypeStruct(pieces[0].shape[1:], jnp.float32)
    specs = [whole(piece) for piece in pieces]
    return run(
        fold_pair_kernel, [place], pieces, specs, waits, [out] * 2, [whole(out)] * 2,
        name="fold_pair",
    )


def bases_kernel(nsuper, place, diag_ref, link_ref, *refs):
    diag_out, link_out, base_ref, next_ref = refs
    rows = diag_out.shape[1]
    mine = pl.ds(pl.multiple_of(place[0] * rows, rows), rows)
    base_ref[...] = diag_ref[0]
    diag_out[0] = base_ref[mine, :]
    for number in range(1, nsuper):
        link = link_ref[number - 1]
        next_ref[...] = dot(base_ref[...], link)
        link_out[number - 1] = next_ref[mine, :]
        base_ref[...] = diag_ref[number] + dot(link, next_ref[...], 0)
        diag_out[number] = base_ref[mine, :]


def bases_of(place, diag_inverse, link_factor, rows, waits):
    nsuper, columns, _ = diag_inverse.shape
    outs = [
        jax.ShapeDtypeStruct((nsuper, rows, columns), jnp.float32),
        jax.ShapeDtypeStruct((nsuper - 1, rows, columns), jnp.float32),
    ]
    return run(
        functools.partial(bases_kernel, nsuper),
        [place],
        [diag_inverse, link_factor],
        [whole(diag_inverse), whole(link_factor)],
        waits,
        outs,
        [whole(out) for out in outs],
        scratch=[pltpu.VMEM((columns, columns), jnp.float32)] * 2,
        name="bases",
    )


def outputs_kernel(place, *refs):
    diag_base, link_base, *sums, diag_out, link_out = refs
    steps = link_out.shape[0]
    for number in range(steps):
        pair = sums[2 * number : 2 * number + 2]

        def put(diag, link, number=number):
            diag_out[number] = diag[...] + diag_base[number]
            link_out[number] = -(link[...] + link_base[number])

        pl.when(place[1] % 2 == 0)(functools.partial(put, *pair))
        pl.when(place[1] % 2 == 1)(functools.partial(put, *pair[::-1]))
    diag_out[steps] = sums[-2][0] + sums[-1][0] + diag_base[steps]


def outputs(place, bases, sums):
    arrays = list(bases) + sums
    specs = [whole(array) for array in arrays]
    outs = [jax.ShapeDtypeStruct(base.shape, jnp.float32) for base in bases]
    return run(outputs_kernel, [place], arrays, specs, [], outs, specs[:2], name="outputs")


def to_column(pieces, ratio):
    return [pieces[0]] + [flip(pieces[o], "pcol", o * ratio) for o in range(1, len(pieces))]


def to_plane(pieces):
    return [pieces[0]] + [flip(pieces[o], "prow", o) for o in range(1, len(pieces))]


def to_plane_whole(factor, count, ratio):
    pieces = jnp.swapaxes(factor.reshape(factor.shape[0], count, -1), 0, 1)
    groups = [[c * ratio + k for c in range(count)] for k in range(ratio)]
    spread = lax.all_to_all(pieces, "pcol", 0, 0, axis_index_groups=groups)
    return lax.all_to_all(spread, "prow", 0, 0)


def gather_plane(own, pcol_count):
    return [own] + [flip(own, "pcol", offset) for offset in range(2, pcol_count, 2)]


def in_rows(gathered, count, ratio):
    _, _, unit_rows, width = gathered.shape
    split = gathered.reshape(count, ratio, count, unit_rows, width)
    rows = jnp.transpose(split, (1, 2, 3, 0, 4))
    return rows.reshape(ratio * count * unit_rows, count * width)


FOUR_SLOTS = ((3, 2, 1, 0), (2, 0, 3, 1), (1, 3, 0, 2), (0, 1, 2, 3))


def slots_of(count):
    return FOUR_SLOTS if count == len(FOUR_SLOTS) else (tuple(range(count)),) * count


def sum_over_four(slots):
    near = lax.ppermute(slots[0], "prow", [(0, 1), (3, 2)])
    total = lax.ppermute(slots[1], "prow", [(0, 2), (2, 3), (3, 1), (1, 0)])
    middle = lax.ppermute(slots[0], "prow", [(1, 2), (2, 1)])
    both = add_up([slots[2], near], [])
    last = lax.ppermute(both, "prow", [(1, 3), (2, 0), (0, 1), (3, 2)])
    return [slots[3], total, middle, last, near]


def sum_over_line(slots, z):
    count = len(slots)
    if count == len(FOUR_SLOTS):
        return sum_over_four(slots)
    chunks = jnp.stack(slots)

    def chunk(index):
        return lax.dynamic_index_in_dim(chunks, jnp.clip(index, 0, count - 1), 0, keepdims=False)

    up = down = None
    for t in range(1, count):
        up_send, down_send = chunk(z + count - t), chunk(z + t - count)
        if up is not None:
            up_send, down_send = up_send + up, down_send + down
        up = lax.ppermute(up_send, "prow", [(i, i + 1) for i in range(min(t, count - 1))])
        down = lax.ppermute(
            down_send, "prow", [(i, i - 1) for i in range(max(count - t, 1), count)]
        )
    mine = chunk(z)
    none = jnp.zeros_like(mine)
    return [mine, none if up is None else up, none if down is None else down, none, mine]


def sum_plane(place, keep, send):
    pieces = fold(place, keep, flip(send, "pcol", 1))
    return [pieces[0]] + [flip(pieces[o], "pcol", 2 * o) for o in range(1, len(pieces))]


def sum_planes(pieces, count):
    bit = 1
    while True:
        total = add_up(pieces, [])
        if bit >= count:
            return [total, jnp.zeros_like(total)]
        pieces = [total, flip(total, "prow", bit)]
        bit *= 2
        if bit >= count:
            return pieces


def sum_pair_near(place, pieces, waits):
    kept, other = fold_pair(place, pieces, waits)
    return [kept, flip(other, "prow", 1)]


def sum_pair_far(pieces, count, waits):
    bit = 2
    while True:
        total = add_up(pieces, waits)
        if bit >= count:
            return [total, flip(total, "prow", 1)]
        pieces, waits = [total, flip(total, "prow", bit)], []
        bit *= 2


def body(inverse_tiles, factor, link_factor, diag_inverse, ancestors):
    row_count, col_count = inverse_tiles.shape
    nsuper, unit_rows, columns = factor.shape
    count = lax.axis_size("prow")
    pcol_count = lax.axis_size("pcol")
    ratio = col_count // row_count
    z = lax.axis_index("prow")
    pcol_index = lax.axis_index("pcol")
    width = columns // count
    place = jnp.stack([pcol_index, z, pcol_index // ratio]).astype(jnp.int32)
    slots = jnp.asarray(slots_of(count), jnp.int32)

    def own_block(place):
        return (place[0] * count + place[1]) * unit_rows // columns

    sent, turned, received, waits = [], [], [], []
    if width % LANES == 0:
        for number in range(nsuper):
            sent.append(to_column(cut(place, factor, number, count, waits), ratio))
            waits = received[-1][1:] if received else []
            turned.append(turn(place, sent[number], waits))
            waits = [turned[0][0]]
            received.append(to_plane(turned[number]))
    waits = [pieces[0] for pieces in received[:1]]
    bases = bases_of(place, diag_inverse, link_factor, columns // pcol_count, waits)
    rows, lates, gathered = [], [], []
    for number in range(nsuper):
        if received:
            gathered += [piece for later in sent[number + 1 : number + 2] for piece in later[1:]]
            own = arrange(place, received[number], gathered)
            found = gather_plane(own, pcol_count)
            gathered = found[1:]
            waits = [piece for later in received[number + 1 : number + 2] for piece in later[1:]]
            packed = pack(found, waits + (rows[-1][1:4] + late if rows else [bases[0]]))
            pieces = [packed, flip(packed, "pcol", 1)]
        else:
            own = to_plane_whole(factor[number], count, ratio)
            pieces = [in_rows(lax.all_gather(own, "pcol", axis=0), count, ratio)]
        middle = 1 if rows else count // 2
        partial, starts = [], [0, middle, count] if received else [0, count]
        for start, stop in zip(starts, starts[1:]):
            partial += partial_product(
                place, slots, ancestors, inverse_tiles, pieces, ratio, columns, number, start, stop,
                [bases[0]],
            )
        rows.append(sum_over_line(partial, z))
        rows[-1] = rows[-1][:3] + rows[-1][:2:-1]
        late = [partial[-1]]
        lates.append(late)

    sums, before, pending = [], [], []
    for number in range(nsuper):
        last = number + 1 == nsuper
        waits = [] if last else rows[number + 1][2:4] + lates[number + 1]
        offdiag, keep, send, *link = finish(
            number, own_block, place, ancestors, [add_up(rows[number][:3], []), rows[number][4]], factor, before,
            link_factor, pcol_count // 2, waits + pending[:1],
        )
        if pending:
            sums += sum_pair_far(pending, count, [keep])
        group = sum_plane(place, keep, send)
        if not last:
            rest = rest_of(link_factor, *link, offdiag, number)
            before = [*rest, offdiag]
            pending = sum_pair_near(place, group, rest[:1])
    sums += sum_planes(group, count)
    return (offdiag, *outputs(place, bases, sums))


def solution(mesh):
    in_specs = (P("pcol", "prow"), P(None, ("pcol", "prow"), None), P(), P(), P())
    out_specs = (P(None, ("pcol", "prow"), None), P(None, "pcol", None), P(None, "pcol", None))
    return jax.shard_map(body, mesh=mesh, in_specs=in_specs, out_specs=out_specs, check_vma=False)
```
